32 devices in a mesh: groups: 2 (over y), clus: 16 (over z, x, core).
Axes of the slice: x: 2, y: 2, z: 4, core: 2. Of those that a mesh axis runs over, the one named last changes fastest.
Arguments:
- sources: bfloat16 [256, 8, 256], P(('groups', 'clus')), parts along dimension 0, may hold values from -6 to 6
- near_blocks: bfloat16 [256, 3, 256, 256], P(('groups', 'clus')), parts along dimension 0, may hold values from -0.21875 to 0.21875
- far_u: bfloat16 [8192, 32, 256], P(('groups', 'clus')), parts along dimension 0, may hold values from -0.375 to 0.375
- far_v: bfloat16 [8192, 32, 256], P(('groups', 'clus')), parts along dimension 0, may hold values from -0.1875 to 0.1875
- send_list: int32 [32, 16, 2], P(('groups', 'clus')), parts along dimension 0, may hold values from -1 to 7, as said below
- far_slot: int32 [8192], P(('groups', 'clus')), parts along dimension 0, may hold values from 0 to 31, as said below
- ret_list: int32 [32, 16, 2], P(('groups', 'clus')), parts along dimension 0, may hold values from -1 to 7, as said below
- ret_slot: int32 [8192], P(('groups', 'clus')), parts along dimension 0, may hold values from 0 to 31, as said below
Outputs:
- adjoint_field: float32 [256, 8, 256], P(('groups', 'clus')), parts along dimension 0
The draws below stay inside these ranges and needn't reach their ends.
There are 2 independent parts, one for each index of `groups`. The reference program is written for one: setup_inputs(seed, part) draws one part's arguments, and reference() takes and returns one part's arrays. A program takes and returns all parts, laid end to end along the dimension named above; each array names one. Nothing has to cross between parts.
Inputs may be any that keep to these rules, and one draw needn't show every extreme that they name: Each row send_list[p, d, :] holds its valid local cluster indices, all different, in its first entries and -1 after them; at least one is valid; one receiving device gets 2 clusters from every sender. `far_slot`: every block names a valid entry of send_list for its owner. Each row ret_list[d, q, :] holds its valid local cluster indices, all different, in its first entries and -1 after them; at least one is valid; one device is served 2 clusters by every block owner. `ret_slot`: every block names a valid entry of ret_list for its owner.
All inputs are finite; a program needn't handle non-finite values.
Results may differ from the reference program's by a relative error of at most 0.0021.
Values may be sent and summed in bfloat16 or wider, within the bound.
No kernel may reach another device: no remote copies, remote signals or barrier semaphores. Data moves between devices by JAX's collectives and lax.ppermute only.
A program may use at most 64 MiB of HBM per device.

```python
import jax
import jax.numpy as jnp
from jax import lax

LEAF = 256
RANK = 32
NVEC = 8
CAP = 2
CL_DEV = 8
FAR_DEV = 256
PEERS = 16
CLUSTERS = 128
FAR = 4096


def pair_lists(key, ceiling):
    key_count, key_full, key_order, key_extra = jax.random.split(key, 4)
    counts = jax.random.randint(key_count, (PEERS, PEERS), 1, ceiling + 1)
    fullest = jax.random.randint(key_full, (), 0, PEERS)
    extra_row = jax.random.randint(key_extra, (), 0, PEERS)
    column = jnp.arange(PEERS)[None, :]
    row = jnp.arange(PEERS)[:, None]
    counts = jnp.where(column == fullest, ceiling, counts)
    counts = jnp.where((row == extra_row) & (column == PEERS - 1), ceiling, counts)
    scores = jax.random.randint(key_order, (PEERS, PEERS, CL_DEV), 0, 1 << 20) * CL_DEV + jnp.arange(CL_DEV)
    ordering = jnp.argsort(scores, axis=-1, stable=True)[:, :, :ceiling]
    slot_range = jnp.arange(ceiling)[None, None, :]
    listed = jnp.where(slot_range < counts[:, :, None], ordering, -1)
    return (listed.astype(jnp.int32), counts.astype(jnp.int32))


def block_slots(key, counts, ceiling):
    key_peer, key_rank = jax.random.split(key, 2)
    slot_total = PEERS * ceiling
    slot_lane = (jnp.arange(FAR_DEV) - FAR_DEV) % slot_total
    base_peer = slot_lane // ceiling
    base_rank = slot_lane % ceiling
    owner_dev = jnp.arange(PEERS)[:, None]
    alive = base_rank[None, :] < counts[owner_dev, base_peer[None, :]]
    random_peer = jax.random.randint(key_peer, (PEERS, FAR_DEV), 0, PEERS)
    random_rank = jax.random.randint(key_rank, (PEERS, FAR_DEV), 0, 1 << 20) % counts[owner_dev, random_peer]
    chosen_peer = jnp.where(alive, base_peer[None, :], random_peer)
    chosen_rank = jnp.where(alive, base_rank[None, :], random_rank)
    return (chosen_peer * ceiling + chosen_rank).reshape(-1).astype(jnp.int32)


def send_tables(key):
    return pair_lists(jax.random.fold_in(key, 11), CAP)


def return_tables(key):
    return pair_lists(jax.random.fold_in(key, 12), CAP)


def draw_send_list(key, part):
    listed, counts = send_tables(key)
    return listed


def draw_far_slot(key, part):
    listed, counts = send_tables(key)
    key = jax.random.fold_in(key, 2)
    return block_slots(key, counts.T, CAP)


def draw_ret_list(key, part):
    listed, counts = return_tables(key)
    return listed


def draw_ret_slot(key, part):
    listed, counts = return_tables(key)
    key = jax.random.fold_in(key, 4)
    return block_slots(key, counts, CAP)


def levels(own_key, dims, cuts, low, top_value):
    def one(axis_at, blocks):
        draws = jax.random.uniform(jax.random.fold_in(jax.random.fold_in(own_key, 6), axis_at), (blocks,), jnp.float32, low / len(cuts), top_value / len(cuts))
        return jnp.repeat(jnp.exp(draws), dims[axis_at] // blocks).reshape((-1,) + (1,) * (len(dims) - axis_at - 1))

    factor_of = one(*cuts[0])
    for cut in cuts[1:]:
        factor_of = factor_of * one(*cut)
    return factor_of


def gaussian(own_key, extent, width, most, shards=(), kind=jnp.bfloat16):
    result = width * jax.random.normal(own_key, extent, jnp.float32)
    if shards:
        result = result * levels(own_key, extent, shards, -0.22, 0.18)
    return jnp.clip(result, -most, most).astype(kind)


def setup_inputs(seed: int = 0, part: int = 0) -> dict:
    keys = jax.random.split(jax.random.key(seed), 9)
    own_keys = jax.random.split(jax.random.fold_in(keys[8], part), 9)
    sources = gaussian(own_keys[0], (CLUSTERS, NVEC, LEAF), 1.0, 6.0, ((0, 16),))
    near_blocks = gaussian(own_keys[1], (CLUSTERS, 3, LEAF, LEAF), (3 * LEAF) ** -0.5, 0.21875, ((0, 16),))
    far_u = gaussian(own_keys[2], (FAR, RANK, LEAF), LEAF ** -0.5, 0.375, ((0, 16),))
    far_v = gaussian(own_keys[3], (FAR, RANK, LEAF), (RANK * FAR_DEV // CL_DEV) ** -0.5, 0.1875, ((0, 16),))
    send_list = draw_send_list(jax.random.fold_in(jax.random.fold_in(keys[8], part), 71), part)
    far_slot = draw_far_slot(jax.random.fold_in(jax.random.fold_in(keys[8], part), 71), part)
    ret_list = draw_ret_list(jax.random.fold_in(jax.random.fold_in(keys[8], part), 71), part)
    ret_slot = draw_ret_slot(jax.random.fold_in(jax.random.fold_in(keys[8], part), 71), part)
    return dict(sources=sources, near_blocks=near_blocks, far_u=far_u, far_v=far_v, send_list=send_list, far_slot=far_slot, ret_list=ret_list, ret_slot=ret_slot)


def near_group(pieces):
    rows, blocks = pieces
    return jnp.einsum('covl,colk->cvk', rows.astype(jnp.float32), blocks.astype(jnp.float32))


def reference(sources, near_blocks, far_u, far_v, send_list, far_slot, ret_list, ret_slot):
    padded = jnp.pad(sources, ((1, 1), (0, 0), (0, 0)))
    stacked = jnp.stack([padded[offset:offset + CLUSTERS] for offset in range(3)], axis=1)
    near_part = lax.map(near_group, (stacked.reshape(PEERS, CL_DEV, 3, NVEC, LEAF),
                                     near_blocks.reshape(PEERS, CL_DEV, 3, LEAF, LEAF)))
    near_part = near_part.reshape(CLUSTERS, NVEC, LEAF)
    owner_dev = (jnp.arange(FAR) // FAR_DEV).astype(jnp.int32)
    src_peer = far_slot // CAP
    src_rank = far_slot % CAP
    targets = (src_peer * CL_DEV + send_list[src_peer, owner_dev, src_rank]).astype(jnp.int32)
    dst_peer = ret_slot // CAP
    dst_rank = ret_slot % CAP
    outputs = (dst_peer * CL_DEV + ret_list[owner_dev, dst_peer, dst_rank]).astype(jnp.int32)

    def far_group(total, pieces):
        target_rows, output_rows, u_part, v_part = pieces
        picked = sources[target_rows].astype(jnp.float32)
        coefficients = jnp.einsum('bvl,brl->bvr', picked, u_part.astype(jnp.float32)).astype(jnp.bfloat16)
        contributions = jnp.einsum('bvr,brl->bvl', coefficients.astype(jnp.float32), v_part.astype(jnp.float32))
        return total + jax.ops.segment_sum(contributions, output_rows, num_segments=CLUSTERS), None

    start = jnp.zeros((CLUSTERS, NVEC, LEAF), jnp.float32)
    far_part, _ = lax.scan(far_group, start, (targets.reshape(PEERS, FAR_DEV), outputs.reshape(PEERS, FAR_DEV),
                                              far_u.reshape(PEERS, FAR_DEV, RANK, LEAF),
                                              far_v.reshape(PEERS, FAR_DEV, RANK, LEAF)))
    return near_part + far_part
```

```python
import jax
import jax.numpy as jnp
from jax import lax
from jax.experimental import pallas as pl
from jax.experimental.pallas import tpu as pltpu
from jax.sharding import PartitionSpec as P

VMEM = pl.BlockSpec(memory_space=pltpu.VMEM)
SMEM = pl.BlockSpec(memory_space=pltpu.SMEM)


def pack_kernel(send_ref, ret_ref, src_ref, out_ref):
    clusters, nvec, leaf = src_ref.shape
    cap, peers = send_ref.shape
    me = lax.axis_index("clus")
    half = (nvec, leaf // cap)
    first = src_ref[0].astype(jnp.float32)
    last = src_ref[clusters - 1].astype(jnp.float32)

    def step(p, carry):
        rows = [
            src_ref[jnp.maximum(send_ref[k, p], 0)].astype(jnp.float32) for k in range(cap)
        ]
        rows.append(jnp.where(p > me, last, first))
        rows.append(
            jnp.concatenate(
                [jnp.full(half, ret_ref[k, p].astype(jnp.float32)) for k in range(cap)], axis=1
            )
        )
        out_ref[p] = jnp.concatenate(rows, axis=0).astype(out_ref.dtype)
        return carry

    lax.fori_loop(0, peers, step, 0, unroll=min(peers, 16))


def far_kernel(slot_ref, dest_ref, x_ref, u_ref, v_ref, out_ref, xf, coef, acc):
    peers = x_ref.shape[0]
    slots, nvec, leaf = xf.shape
    cap = slots // peers
    blocks, rank, _ = u_ref.shape
    group = leaf // rank
    ways = acc.shape[0]

    def widen(p, carry):
        rows = x_ref[p, : cap * nvec, :].astype(jnp.float32)
        for k in range(cap):
            xf[p * cap + k] = rows[k * nvec : (k + 1) * nvec]
        return carry

    lax.fori_loop(0, peers, widen, 0, unroll=min(peers, 16))
    acc[...] = jnp.zeros_like(acc)
    owner = lax.broadcasted_iota(jnp.int32, (nvec, leaf), 1) // rank

    def project(g, carry):
        picked = jnp.concatenate(
            [xf[slot_ref[g * group + i]] for i in range(group)], axis=0
        ).astype(jnp.bfloat16)
        u = u_ref[pl.ds(g * group, group)].reshape(group * rank, leaf)
        full = lax.dot_general(
            picked, u, (((1,), (1,)), ((), ())), preferred_element_type=jnp.float32
        )
        kept = full[:nvec]
        for i in range(1, group):
            kept = jnp.where(owner == i, full[i * nvec : (i + 1) * nvec], kept)
        coef[g] = kept
        return carry

    def expand(g, carry):
        kept = coef[g]
        spread = jnp.concatenate(
            [jnp.where(owner == i, kept, 0.0) for i in range(group)], axis=0
        ).astype(jnp.bfloat16)
        v = v_ref[pl.ds(g * group, group)].reshape(group * rank, leaf)
        terms = jnp.dot(spread, v, preferred_element_type=jnp.float32)
        for i in range(group):
            at = dest_ref[g * group + i]
            acc[i % ways, at] += terms[i * nvec : (i + 1) * nvec]
        return carry

    lax.fori_loop(0, blocks // group, project, 0, unroll=4)
    lax.fori_loop(0, blocks // group, expand, 0, unroll=4)

    def narrow(p, carry):
        rows = []
        for k in range(cap):
            total = acc[0, p * cap + k]
            for w in range(1, ways):
                total += acc[w, p * cap + k]
            rows.append(total)
        out_ref[p] = jnp.concatenate(rows, axis=0).astype(out_ref.dtype)
        return carry

    lax.fori_loop(0, peers, narrow, 0, unroll=min(peers, 16))


def near_kernel(src_ref, near_ref, x_ref, near_out, place_out, place):
    clusters, nvec, leaf = src_ref.shape
    peers = x_ref.shape[0]
    cap = place.shape[0] // (peers * nvec)
    me = lax.axis_index("clus")
    edge = slice(cap * nvec, (cap + 1) * nvec)
    before = x_ref[jnp.maximum(me - 1, 0)][edge].astype(jnp.float32)
    after = x_ref[jnp.minimum(me + 1, peers - 1)][edge].astype(jnp.float32)
    before = jnp.where(me > 0, before, 0.0).astype(jnp.bfloat16)
    after = jnp.where(me < peers - 1, after, 0.0).astype(jnp.bfloat16)
    rows = [before] + [src_ref[s] for s in range(clusters)] + [after]
    for s in range(clusters):
        total = jnp.dot(rows[s], near_ref[s, 0], preferred_element_type=jnp.float32)
        for o in range(1, 3):
            total += jnp.dot(rows[s + o], near_ref[s, o], preferred_element_type=jnp.float32)
        near_out[s * nvec : (s + 1) * nvec] = total

    lane = lax.broadcasted_iota(jnp.int32, (nvec, leaf // cap), 1)
    sub = lax.broadcasted_iota(jnp.int32, (nvec, leaf // cap), 0)
    cluster = jnp.where(lane % nvec == sub, lane // nvec, -2).astype(jnp.float32)

    def step(p, carry):
        meta = x_ref[p, (cap + 1) * nvec :, :].astype(jnp.float32)
        for k in range(cap):
            width = leaf // cap
            place[pl.ds((p * cap + k) * nvec, nvec)] = jnp.where(
                meta[:, k * width : (k + 1) * width] == cluster, 1.0, 0.0
            )
        return carry

    lax.fori_loop(0, peers, step, 0, unroll=min(peers, 16))
    place_out[...] = place[...].T[: clusters * nvec].astype(jnp.bfloat16)


def sum_kernel(back_ref, near_ref, place_ref, out_ref):
    peers, rows, leaf = back_ref.shape
    clusters, nvec, _ = out_ref.shape
    terms = back_ref[...].reshape(peers * rows, leaf)
    total = near_ref[...] + jnp.dot(
        place_ref[...], terms, preferred_element_type=jnp.float32
    )
    out_ref[...] = total.reshape(clusters, nvec, leaf)


def cost(flops, moved):
    return pl.CostEstimate(flops=flops, bytes_accessed=moved, transcendentals=0)


def body(sources, near_blocks, far_u, far_v, send_list, far_slot, ret_list, ret_slot):
    clusters, nvec, leaf = sources.shape
    _, peers, cap = send_list.shape
    blocks, rank, _ = far_u.shape
    slots = peers * cap
    group = leaf // rank
    params = pltpu.CompilerParams(vmem_limit_bytes=24 * 2**20)
    message = pl.pallas_call(
        pack_kernel,
        out_shape=jax.ShapeDtypeStruct((peers, (cap + 2) * nvec, leaf), jnp.bfloat16),
        in_specs=[SMEM, SMEM, VMEM],
        out_specs=VMEM,
        compiler_params=params,
        cost_estimate=cost(0, peers * (cap + 2) * nvec * leaf * 2),
        name="pack",
    )(send_list[0].T, ret_list[0].T, sources)
    incoming = lax.all_to_all(message, "clus", split_axis=0, concat_axis=0, tiled=True)
    returns = pl.pallas_call(
        far_kernel,
        out_shape=jax.ShapeDtypeStruct((peers, cap * nvec, leaf), jnp.bfloat16),
        in_specs=[SMEM, SMEM, VMEM, VMEM, VMEM],
        out_specs=VMEM,
        scratch_shapes=[
            pltpu.VMEM((slots, nvec, leaf), jnp.float32),
            pltpu.VMEM((blocks // group, nvec, leaf), jnp.float32),
            pltpu.VMEM((4 if peers <= 16 else 1, slots, nvec, leaf), jnp.float32),
        ],
        compiler_params=params,
        cost_estimate=cost(4 * blocks * 8 * nvec * leaf * rank, 4 * blocks * rank * leaf),
        name="far",
    )(far_slot, ret_slot, incoming, far_u, far_v)
    back = lax.all_to_all(returns, "clus", split_axis=0, concat_axis=0, tiled=True)
    near_part, place = pl.pallas_call(
        near_kernel,
        out_shape=(
            jax.ShapeDtypeStruct((clusters * nvec, leaf), jnp.float32),
            jax.ShapeDtypeStruct((clusters * nvec, slots * nvec), jnp.bfloat16),
        ),
        in_specs=[VMEM, VMEM, VMEM],
        out_specs=(VMEM, VMEM),
        scratch_shapes=[pltpu.VMEM((slots * nvec, leaf // cap), jnp.float32)],
        compiler_params=params,
        cost_estimate=cost(2 * 3 * clusters * nvec * leaf * leaf, 6 * clusters * leaf * leaf),
        name="near",
    )(sources, near_blocks, incoming)
    return pl.pallas_call(
        sum_kernel,
        out_shape=jax.ShapeDtypeStruct((clusters, nvec, leaf), jnp.float32),
        in_specs=[VMEM, VMEM, VMEM],
        out_specs=VMEM,
        compiler_params=params,
        cost_estimate=cost(2 * clusters * nvec * slots * nvec * leaf, slots * nvec * leaf * 2),
        name="sum",
    )(back, near_part, place)


def solution(mesh):
    placed = (
        P(("groups", "clus"), None, None),
        P(("groups", "clus"), None, None, None),
        P(("groups", "clus"), None, None),
        P(("groups", "clus"), None, None),
        P(("groups", "clus"), None, None),
        P(("groups", "clus")),
        P(("groups", "clus"), None, None),
        P(("groups", "clus")),
    )
    return jax.shard_map(
        body,
        mesh=mesh,
        in_specs=placed,
        out_specs=P(("groups", "clus"), None, None),
        check_vma=False,
    )
```

```python
import jax
import jax.numpy as jnp
from jax import lax
from jax.experimental import pallas as pl
from jax.experimental.pallas import tpu as pltpu
from jax.sharding import PartitionSpec as P

VMEM = pl.BlockSpec(memory_space=pltpu.VMEM)
HBM = pl.BlockSpec(memory_space=pltpu.HBM)
CHUNKS = 4


def fetch(pairs, sems):
    copies = [pltpu.make_async_copy(a, b, sems.at[i]) for i, (a, b) in enumerate(pairs)]
    for copy in copies:
        copy.start()
    return copies


def halves(x):
    w = x.shape[1] // 2
    return [x[:, :w], x[:, w:]]


def pack_kernel(send_hbm, ret_hbm, src_hbm, out_ref, send_ref, ret_ref, src_ref, sems):
    for copy in fetch([(send_hbm, send_ref), (ret_hbm, ret_ref), (src_hbm, src_ref)], sems):
        copy.wait()
    clusters, nvec, leaf = src_ref.shape
    cap, peers = send_ref.shape
    me = lax.axis_index("clus")
    first = src_ref[0].astype(jnp.float32)
    last = src_ref[clusters - 1].astype(jnp.float32)

    def step(p, carry):
        rows = []
        for k in range(cap):
            rows += halves(src_ref[jnp.maximum(send_ref[k, p], 0)].astype(jnp.float32))
        rows += halves(jnp.where(p > me, last, first))
        rows.append(
            jnp.concatenate(
                [
                    jnp.full((nvec // cap, leaf // 2), ret_ref[k, p].astype(jnp.float32))
                    for k in range(cap)
                ],
                axis=0,
            )
        )
        out_ref[p] = jnp.concatenate(rows, axis=0).astype(out_ref.dtype)
        return carry

    lax.fori_loop(0, peers, step, 0, unroll=min(peers, 16))


def joined(rows, nvec):
    return jnp.concatenate([rows[:nvec], rows[nvec:]], axis=1)


def far_kernel(
    slot_hbm, dest_hbm, x_ref, u_hbm, v_hbm, out_ref, slot_ref, dest_ref, u_ref, v_ref, xf, *rest
):
    accs, sems = rest[:-1], rest[-1]
    peers = x_ref.shape[0]
    slots, nvec, leaf = xf.shape
    cap = slots // peers
    blocks, rank, _ = u_ref.shape
    group = leaf // rank
    size = blocks // CHUNKS
    pairs = [(slot_hbm, slot_ref), (dest_hbm, dest_ref)]
    for c in range(CHUNKS):
        part = pl.ds(c * size, size)
        pairs += [(u_hbm.at[part], u_ref.at[part]), (v_hbm.at[part], v_ref.at[part])]
    copies = fetch(pairs, sems)

    def widen(p, carry):
        rows = x_ref[p].astype(jnp.float32)
        for k in range(cap):
            xf[p * cap + k] = joined(rows[2 * k * nvec : 2 * (k + 1) * nvec], nvec)
        return carry

    lax.fori_loop(0, peers, widen, 0, unroll=min(peers, 16))
    for acc in accs:
        acc[...] = jnp.zeros_like(acc)
    owner = lax.broadcasted_iota(jnp.int32, (nvec, leaf), 1) // rank
    copies[0].wait()
    copies[1].wait()
    for g in range(blocks // group):
        if g * group % size == 0:
            copies[2 + 2 * (g * group // size)].wait()
            copies[3 + 2 * (g * group // size)].wait()
        picked = jnp.concatenate(
            [xf[slot_ref[g * group + i]] for i in range(group)], axis=0
        ).astype(jnp.bfloat16)
        u = u_ref[g * group : (g + 1) * group].reshape(group * rank, leaf)
        full = lax.dot_general(
            picked, u, (((1,), (1,)), ((), ())), preferred_element_type=jnp.float32
        )
        kept = full[:nvec]
        for i in range(1, group):
            kept = jnp.where(owner == i, full[i * nvec : (i + 1) * nvec], kept)
        spread = jnp.concatenate(
            [jnp.where(owner == i, kept, 0.0) for i in range(group)], axis=0
        ).astype(jnp.bfloat16)
        v = v_ref[g * group : (g + 1) * group].reshape(group * rank, leaf)
        terms = jnp.dot(spread, v, preferred_element_type=jnp.float32)
        for i in range(group):
            accs[i % len(accs)][dest_ref[g * group + i]] += terms[i * nvec : (i + 1) * nvec]

    def narrow(p, carry):
        rows = []
        for k in range(cap):
            total = accs[0][p * cap + k]
            for acc in accs[1:]:
                total += acc[p * cap + k]
            rows.append(total)
        out_ref[p] = jnp.concatenate(rows, axis=0).astype(out_ref.dtype)
        return carry

    lax.fori_loop(0, peers, narrow, 0, unroll=min(peers, 16))


def near_kernel(src_ref, near_hbm, x_ref, near_out, place_out, near_ref, place, sems):
    clusters, nvec, leaf = src_ref.shape
    peers = x_ref.shape[0]
    cap = place.shape[0] // (peers * nvec)
    copies = fetch([(near_hbm.at[s], near_ref.at[s]) for s in range(clusters)], sems)

    width = leaf // 2
    lane = lax.broadcasted_iota(jnp.int32, (nvec, width), 1)
    sub = lax.broadcasted_iota(jnp.int32, (nvec, width), 0)
    cluster = jnp.where(lane % nvec == sub, lane // nvec, -2).astype(jnp.float32)

    def step(p, carry):
        meta = x_ref[p, 2 * (cap + 1) * nvec :, :].astype(jnp.float32)
        for k in range(cap):
            at = jnp.broadcast_to(meta[k * nvec // cap : k * nvec // cap + 1], (nvec, width))
            place[pl.ds((p * cap + k) * nvec, nvec)] = jnp.where(at == cluster, 1.0, 0.0)
        return carry

    lax.fori_loop(0, peers, step, 0, unroll=min(peers, 16))
    place_out[...] = place[...].T[: clusters * nvec].astype(jnp.bfloat16)

    me = lax.axis_index("clus")
    edge = slice(2 * cap * nvec, 2 * (cap + 1) * nvec)
    before = joined(x_ref[jnp.maximum(me - 1, 0)][edge].astype(jnp.float32), nvec)
    after = joined(x_ref[jnp.minimum(me + 1, peers - 1)][edge].astype(jnp.float32), nvec)
    before = jnp.where(me > 0, before, 0.0).astype(jnp.bfloat16)
    after = jnp.where(me < peers - 1, after, 0.0).astype(jnp.bfloat16)
    rows = [before] + [src_ref[s] for s in range(clusters)] + [after]
    for s in range(clusters):
        copies[s].wait()
        total = jnp.dot(rows[s], near_ref[s, 0], preferred_element_type=jnp.float32)
        for o in range(1, 3):
            total += jnp.dot(rows[s + o], near_ref[s, o], preferred_element_type=jnp.float32)
        near_out[s * nvec : (s + 1) * nvec] = total


def sum_kernel(back_ref, near_ref, place_ref, out_ref):
    peers, rows, leaf = back_ref.shape
    clusters, nvec, _ = out_ref.shape
    terms = back_ref[...].reshape(peers * rows, leaf)
    total = near_ref[...] + jnp.dot(
        place_ref[...], terms, preferred_element_type=jnp.float32
    )
    out_ref[...] = total.reshape(clusters, nvec, leaf)


def cost(flops, moved):
    return pl.CostEstimate(flops=flops, bytes_accessed=moved, transcendentals=0)


def body(sources, near_blocks, far_u, far_v, send_list, far_slot, ret_list, ret_slot):
    clusters, nvec, leaf = sources.shape
    _, peers, cap = send_list.shape
    blocks, rank, _ = far_u.shape
    slots = peers * cap
    rows = 2 * (cap + 1) * nvec + nvec
    params = pltpu.CompilerParams(vmem_limit_bytes=24 * 2**20)
    message = pl.pallas_call(
        pack_kernel,
        out_shape=jax.ShapeDtypeStruct((peers, rows, leaf // 2), jnp.bfloat16),
        in_specs=[HBM, HBM, HBM],
        out_specs=VMEM,
        scratch_shapes=[
            pltpu.SMEM((cap, peers), jnp.int32),
            pltpu.SMEM((cap, peers), jnp.int32),
            pltpu.VMEM((clusters, nvec, leaf), jnp.bfloat16),
            pltpu.SemaphoreType.DMA((3,)),
        ],
        compiler_params=params,
        cost_estimate=cost(0, peers * rows * leaf),
        name="pack",
    )(send_list[0].T, ret_list[0].T, sources)
    incoming = lax.all_to_all(message, "clus", split_axis=0, concat_axis=0, tiled=True)
    returns = pl.pallas_call(
        far_kernel,
        out_shape=jax.ShapeDtypeStruct((peers, cap * nvec, leaf), jnp.bfloat16),
        in_specs=[HBM, HBM, VMEM, HBM, HBM],
        out_specs=VMEM,
        scratch_shapes=[
            pltpu.SMEM((blocks,), jnp.int32),
            pltpu.SMEM((blocks,), jnp.int32),
            pltpu.VMEM((blocks, rank, leaf), jnp.bfloat16),
            pltpu.VMEM((blocks, rank, leaf), jnp.bfloat16),
            pltpu.VMEM((slots, nvec, leaf), jnp.float32),
        ]
        + [pltpu.VMEM((slots, nvec, leaf), jnp.float32)] * (4 if peers <= 16 else 1)
        + [pltpu.SemaphoreType.DMA((2 + 2 * CHUNKS,))],
        compiler_params=params,
        cost_estimate=cost(4 * blocks * 8 * nvec * leaf * rank, 4 * blocks * rank * leaf),
        name="far",
    )(far_slot, ret_slot, incoming, far_u, far_v)
    back = lax.all_to_all(returns, "clus", split_axis=0, concat_axis=0, tiled=True)
    near_part, place = pl.pallas_call(
        near_kernel,
        out_shape=(
            jax.ShapeDtypeStruct((clusters * nvec, leaf), jnp.float32),
            jax.ShapeDtypeStruct((clusters * nvec, slots * nvec), jnp.bfloat16),
        ),
        in_specs=[VMEM, HBM, VMEM],
        out_specs=(VMEM, VMEM),
        scratch_shapes=[
            pltpu.VMEM(near_blocks.shape, jnp.bfloat16),
            pltpu.VMEM((slots * nvec, leaf // 2), jnp.float32),
            pltpu.SemaphoreType.DMA((clusters,)),
        ],
        compiler_params=params,
        cost_estimate=cost(2 * 3 * clusters * nvec * leaf * leaf, 6 * clusters * leaf * leaf),
        name="near",
    )(sources, near_blocks, incoming)
    return pl.pallas_call(
        sum_kernel,
        out_shape=jax.ShapeDtypeStruct((clusters, nvec, leaf), jnp.float32),
        in_specs=[VMEM, VMEM, VMEM],
        out_specs=VMEM,
        compiler_params=params,
        cost_estimate=cost(2 * clusters * nvec * slots * nvec * leaf, slots * nvec * leaf * 2),
        name="sum",
    )(back, near_part, place)


def solution(mesh):
    placed = (
        P(("groups", "clus"), None, None),
        P(("groups", "clus"), None, None, None),
        P(("groups", "clus"), None, None),
        P(("groups", "clus"), None, None),
        P(("groups", "clus"), None, None),
        P(("groups", "clus")),
        P(("groups", "clus"), None, None),
        P(("groups", "clus")),
    )
    return jax.shard_map(
        body,
        mesh=mesh,
        in_specs=placed,
        out_specs=P(("groups", "clus"), None, None),
        check_vma=False,
    )
```

```python
import jax
import jax.numpy as jnp
from jax import lax
from jax.experimental import pallas as pl
from jax.experimental.pallas import tpu as pltpu
from jax.sharding import PartitionSpec as P

VMEM = pl.BlockSpec(memory_space=pltpu.VMEM)
HBM = pl.BlockSpec(memory_space=pltpu.HBM)
CHUNKS = 4


def fetch(pairs, sems):
    copies = [pltpu.make_async_copy(a, b, sems.at[i]) for i, (a, b) in enumerate(pairs)]
    for copy in copies:
        copy.start()
    return copies


def halves(x):
    w = x.shape[1] // 2
    return [x[:, :w], x[:, w:]]


def pack_kernel(send_hbm, ret_hbm, src_hbm, out_ref, send_ref, ret_ref, src_ref, sems):
    for copy in fetch([(send_hbm, send_ref), (ret_hbm, ret_ref), (src_hbm, src_ref)], sems):
        copy.wait()
    clusters, nvec, leaf = src_ref.shape
    cap, peers = send_ref.shape
    me = lax.axis_index("clus")
    first = src_ref[0].astype(jnp.float32)
    last = src_ref[clusters - 1].astype(jnp.float32)

    def step(p, carry):
        rows = []
        for k in range(cap):
            rows += halves(src_ref[jnp.maximum(send_ref[k, p], 0)].astype(jnp.float32))
        rows += halves(jnp.where(p > me, last, first))
        rows.append(
            jnp.concatenate(
                [
                    jnp.full((nvec // cap, leaf // 2), ret_ref[k, p].astype(jnp.float32))
                    for k in range(cap)
                ],
                axis=0,
            )
        )
        out_ref[p] = jnp.concatenate(rows, axis=0).astype(out_ref.dtype)
        return carry

    lax.fori_loop(0, peers, step, 0, unroll=min(peers, 16))


def joined(rows, nvec):
    return jnp.concatenate([rows[:nvec], rows[nvec:]], axis=1)


def far_kernel(
    slot_hbm,
    dest_hbm,
    x_hbm,
    u_hbm,
    v_hbm,
    out_ref,
    slot_ref,
    dest_ref,
    x_ref,
    u_ref,
    v_ref,
    xf,
    *rest,
):
    accs, sems = rest[:-1], rest[-1]
    peers = x_ref.shape[0]
    slots, nvec, leaf = xf.shape
    cap = slots // peers
    blocks, rank, _ = u_ref.shape
    group = leaf // rank
    size = blocks // CHUNKS
    pairs = [(x_hbm, x_ref), (slot_hbm, slot_ref), (dest_hbm, dest_ref)]
    for c in range(CHUNKS):
        part = pl.ds(c * size, size)
        pairs += [(u_hbm.at[part], u_ref.at[part]), (v_hbm.at[part], v_ref.at[part])]
    copies = fetch(pairs, sems)
    for acc in accs:
        acc[...] = jnp.zeros_like(acc)
    copies[0].wait()

    def widen(p, carry):
        rows = x_ref[p].astype(jnp.float32)
        for k in range(cap):
            xf[p * cap + k] = joined(rows[2 * k * nvec : 2 * (k + 1) * nvec], nvec)
        return carry

    lax.fori_loop(0, peers, widen, 0, unroll=min(peers, 16))
    owner = lax.broadcasted_iota(jnp.int32, (nvec, leaf), 1) // rank
    copies[1].wait()
    copies[2].wait()
    for g in range(blocks // group):
        if g * group % size == 0:
            copies[3 + 2 * (g * group // size)].wait()
            copies[4 + 2 * (g * group // size)].wait()
        picked = jnp.concatenate(
            [xf[slot_ref[g * group + i]] for i in range(group)], axis=0
        ).astype(jnp.bfloat16)
        u = u_ref[g * group : (g + 1) * group].reshape(group * rank, leaf)
        full = lax.dot_general(
            picked, u, (((1,), (1,)), ((), ())), preferred_element_type=jnp.float32
        )
        kept = full[:nvec]
        for i in range(1, group):
            kept = jnp.where(owner == i, full[i * nvec : (i + 1) * nvec], kept)
        spread = jnp.concatenate(
            [jnp.where(owner == i, kept, 0.0) for i in range(group)], axis=0
        ).astype(jnp.bfloat16)
        v = v_ref[g * group : (g + 1) * group].reshape(group * rank, leaf)
        terms = jnp.dot(spread, v, preferred_element_type=jnp.float32)
        for i in range(group):
            accs[i % len(accs)][dest_ref[g * group + i]] += terms[i * nvec : (i + 1) * nvec]

    def narrow(p, carry):
        rows = []
        for k in range(cap):
            total = accs[0][p * cap + k]
            for acc in accs[1:]:
                total += acc[p * cap + k]
            rows.append(total)
        out_ref[p] = jnp.concatenate(rows, axis=0).astype(out_ref.dtype)
        return carry

    lax.fori_loop(0, peers, narrow, 0, unroll=min(peers, 16))


def near_kernel(src_ref, near_ref, x_ref, near_out, place_out, place):
    clusters, nvec, leaf = src_ref.shape
    peers = x_ref.shape[0]
    cap = place.shape[0] // (peers * nvec)
    width = leaf // 2
    lane = lax.broadcasted_iota(jnp.int32, (nvec, width), 1)
    sub = lax.broadcasted_iota(jnp.int32, (nvec, width), 0)
    cluster = jnp.where(lane % nvec == sub, lane // nvec, -2).astype(jnp.float32)

    def step(p, carry):
        meta = x_ref[p, 2 * (cap + 1) * nvec :, :].astype(jnp.float32)
        for k in range(cap):
            at = jnp.broadcast_to(meta[k * nvec // cap : k * nvec // cap + 1], (nvec, width))
            place[pl.ds((p * cap + k) * nvec, nvec)] = jnp.where(at == cluster, 1.0, 0.0)
        return carry

    lax.fori_loop(0, peers, step, 0, unroll=min(peers, 16))
    place_out[...] = place[...].T[: clusters * nvec].astype(jnp.bfloat16)

    me = lax.axis_index("clus")
    edge = slice(2 * cap * nvec, 2 * (cap + 1) * nvec)
    before = joined(x_ref[jnp.maximum(me - 1, 0)][edge].astype(jnp.float32), nvec)
    after = joined(x_ref[jnp.minimum(me + 1, peers - 1)][edge].astype(jnp.float32), nvec)
    before = jnp.where(me > 0, before, 0.0).astype(jnp.bfloat16)
    after = jnp.where(me < peers - 1, after, 0.0).astype(jnp.bfloat16)
    rows = [before] + [src_ref[s] for s in range(clusters)] + [after]
    for s in range(clusters):
        total = jnp.dot(rows[s], near_ref[s, 0], preferred_element_type=jnp.float32)
        for o in range(1, 3):
            total += jnp.dot(rows[s + o], near_ref[s, o], preferred_element_type=jnp.float32)
        near_out[s * nvec : (s + 1) * nvec] = total


def sum_kernel(back_hbm, near_hbm, place_hbm, out_ref, back_ref, near_ref, place_ref, sems):
    pairs = [(back_hbm, back_ref), (near_hbm, near_ref), (place_hbm, place_ref)]
    for copy in fetch(pairs, sems):
        copy.wait()
    peers, rows, leaf = back_ref.shape
    clusters, nvec, _ = out_ref.shape
    terms = back_ref[...].reshape(peers * rows, leaf)
    total = near_ref[...] + jnp.dot(
        place_ref[...], terms, preferred_element_type=jnp.float32
    )
    out_ref[...] = total.reshape(clusters, nvec, leaf)


def cost(flops, moved):
    return pl.CostEstimate(flops=flops, bytes_accessed=moved, transcendentals=0)


def body(sources, near_blocks, far_u, far_v, send_list, far_slot, ret_list, ret_slot):
    clusters, nvec, leaf = sources.shape
    _, peers, cap = send_list.shape
    blocks, rank, _ = far_u.shape
    slots = peers * cap
    rows = 2 * (cap + 1) * nvec + nvec
    part = pltpu.CompilerParams(vmem_limit_bytes=24 * 2**20)
    whole = pltpu.CompilerParams(vmem_limit_bytes=64 * 2**20)
    message = pl.pallas_call(
        pack_kernel,
        out_shape=jax.ShapeDtypeStruct((peers, rows, leaf // 2), jnp.bfloat16),
        in_specs=[HBM, HBM, HBM],
        out_specs=VMEM,
        scratch_shapes=[
            pltpu.SMEM((cap, peers), jnp.int32),
            pltpu.SMEM((cap, peers), jnp.int32),
            pltpu.VMEM((clusters, nvec, leaf), jnp.bfloat16),
            pltpu.SemaphoreType.DMA((3,)),
        ],
        compiler_params=whole,
        cost_estimate=cost(0, peers * rows * leaf),
        name="pack",
    )(send_list[0].T, ret_list[0].T, sources)
    incoming = lax.all_to_all(message, "clus", split_axis=0, concat_axis=0, tiled=True)
    returns = pl.pallas_call(
        far_kernel,
        out_shape=jax.ShapeDtypeStruct((peers, cap * nvec, leaf), jnp.bfloat16),
        in_specs=[HBM] * 5,
        out_specs=VMEM,
        scratch_shapes=[
            pltpu.SMEM((blocks,), jnp.int32),
            pltpu.SMEM((blocks,), jnp.int32),
            pltpu.VMEM(incoming.shape, jnp.bfloat16),
            pltpu.VMEM((blocks, rank, leaf), jnp.bfloat16),
            pltpu.VMEM((blocks, rank, leaf), jnp.bfloat16),
            pltpu.VMEM((slots, nvec, leaf), jnp.float32),
        ]
        + [pltpu.VMEM((slots, nvec, leaf), jnp.float32)] * (4 if peers <= 16 else 1)
        + [pltpu.SemaphoreType.DMA((3 + 2 * CHUNKS,))],
        compiler_params=whole,
        cost_estimate=cost(4 * blocks * 8 * nvec * leaf * rank, 4 * blocks * rank * leaf),
        name="far",
    )(far_slot, ret_slot, incoming, far_u, far_v)
    back = lax.all_to_all(returns, "clus", split_axis=0, concat_axis=0, tiled=True)
    near_part, place = pl.pallas_call(
        near_kernel,
        out_shape=(
            jax.ShapeDtypeStruct((clusters * nvec, leaf), jnp.float32),
            jax.ShapeDtypeStruct((clusters * nvec, slots * nvec), jnp.bfloat16),
        ),
        in_specs=[VMEM, VMEM, VMEM],
        out_specs=(VMEM, VMEM),
        scratch_shapes=[pltpu.VMEM((slots * nvec, leaf // 2), jnp.float32)],
        compiler_params=part,
        cost_estimate=cost(2 * 3 * clusters * nvec * leaf * leaf, 6 * clusters * leaf * leaf),
        name="near",
    )(sources, near_blocks, incoming)
    return pl.pallas_call(
        sum_kernel,
        out_shape=jax.ShapeDtypeStruct((clusters, nvec, leaf), jnp.float32),
        in_specs=[HBM, HBM, HBM],
        out_specs=VMEM,
        scratch_shapes=[
            pltpu.VMEM(back.shape, jnp.bfloat16),
            pltpu.VMEM(near_part.shape, jnp.float32),
            pltpu.VMEM(place.shape, jnp.bfloat16),
            pltpu.SemaphoreType.DMA((3,)),
        ],
        compiler_params=whole,
        cost_estimate=cost(2 * clusters * nvec * slots * nvec * leaf, slots * nvec * leaf * 2),
        name="sum",
    )(back, near_part, place)


def solution(mesh):
    placed = (
        P(("groups", "clus"), None, None),
        P(("groups", "clus"), None, None, None),
        P(("groups", "clus"), None, None),
        P(("groups", "clus"), None, None),
        P(("groups", "clus"), None, None),
        P(("groups", "clus")),
        P(("groups", "clus"), None, None),
        P(("groups", "clus")),
    )
    return jax.shard_map(
        body,
        mesh=mesh,
        in_specs=placed,
        out_specs=P(("groups", "clus"), None, None),
        check_vma=False,
    )
```

```python
import jax
import jax.numpy as jnp
from jax import lax
from jax.experimental import pallas as pl
from jax.experimental.pallas import tpu as pltpu
from jax.sharding import PartitionSpec as P

VMEM = pl.BlockSpec(memory_space=pltpu.VMEM)
SMEM = pl.BlockSpec(memory_space=pltpu.SMEM)


def halves(x):
    w = x.shape[1] // 2
    return [x[:, :w], x[:, w:]]


def pack_kernel(send_ref, ret_ref, src_ref, out_ref):
    clusters, nvec, leaf = src_ref.shape
    cap, peers = send_ref.shape
    me = lax.axis_index("clus")
    first = src_ref[0].astype(jnp.float32)
    last = src_ref[clusters - 1].astype(jnp.float32)

    def step(p, carry):
        rows = []
        for k in range(cap):
            rows += halves(src_ref[jnp.maximum(send_ref[k, p], 0)].astype(jnp.float32))
        rows += halves(jnp.where(p > me, last, first))
        rows.append(
            jnp.concatenate(
                [
                    jnp.full((nvec // cap, leaf // 2), ret_ref[k, p].astype(jnp.float32))
                    for k in range(cap)
                ],
                axis=0,
            )
        )
        out_ref[p] = jnp.concatenate(rows, axis=0).astype(out_ref.dtype)
        return carry

    lax.fori_loop(0, peers, step, 0, unroll=min(peers, 16))


def joined(rows, nvec):
    return jnp.concatenate([rows[:nvec], rows[nvec:]], axis=1)


def far_kernel(slot_ref, dest_ref, x_ref, u_ref, v_ref, out_ref, xf, *accs):
    peers = x_ref.shape[0]
    slots, nvec, leaf = xf.shape
    cap = slots // peers
    blocks, rank, _ = u_ref.shape
    group = leaf // rank
    for acc in accs:
        acc[...] = jnp.zeros_like(acc)

    def widen(p, carry):
        rows = x_ref[p].astype(jnp.float32)
        for k in range(cap):
            xf[p * cap + k] = joined(rows[2 * k * nvec : 2 * (k + 1) * nvec], nvec)
        return carry

    lax.fori_loop(0, peers, widen, 0, unroll=min(peers, 16))
    owner = lax.broadcasted_iota(jnp.int32, (nvec, leaf), 1) // rank
    for g in range(blocks // group):
        picked = jnp.concatenate(
            [xf[slot_ref[g * group + i]] for i in range(group)], axis=0
        ).astype(jnp.bfloat16)
        u = u_ref[g * group : (g + 1) * group].reshape(group * rank, leaf)
        full = lax.dot_general(
            picked, u, (((1,), (1,)), ((), ())), preferred_element_type=jnp.float32
        )
        kept = full[:nvec]
        for i in range(1, group):
            kept = jnp.where(owner == i, full[i * nvec : (i + 1) * nvec], kept)
        spread = jnp.concatenate(
            [jnp.where(owner == i, kept, 0.0) for i in range(group)], axis=0
        ).astype(jnp.bfloat16)
        v = v_ref[g * group : (g + 1) * group].reshape(group * rank, leaf)
        terms = jnp.dot(spread, v, preferred_element_type=jnp.float32)
        for i in range(group):
            accs[i % len(accs)][dest_ref[g * group + i]] += terms[i * nvec : (i + 1) * nvec]

    def narrow(p, carry):
        rows = []
        for k in range(cap):
            total = accs[0][p * cap + k]
            for acc in accs[1:]:
                total += acc[p * cap + k]
            rows.append(total)
        out_ref[p] = jnp.concatenate(rows, axis=0).astype(out_ref.dtype)
        return carry

    lax.fori_loop(0, peers, narrow, 0, unroll=min(peers, 16))


def sum_kernel(back_ref, src_ref, near_ref, x_ref, out_ref, place):
    clusters, nvec, leaf = src_ref.shape
    peers, back_rows, _ = back_ref.shape
    cap = back_rows // nvec
    width = leaf // 2
    lane = lax.broadcasted_iota(jnp.int32, (nvec, width), 1)
    sub = lax.broadcasted_iota(jnp.int32, (nvec, width), 0)
    cluster = jnp.where(lane % nvec == sub, lane // nvec, -2).astype(jnp.float32)

    def step(p, carry):
        meta = x_ref[p, 2 * (cap + 1) * nvec :, :].astype(jnp.float32)
        for k in range(cap):
            at = jnp.broadcast_to(meta[k * nvec // cap : k * nvec // cap + 1], (nvec, width))
            place[pl.ds((p * cap + k) * nvec, nvec)] = jnp.where(at == cluster, 1.0, 0.0)
        return carry

    lax.fori_loop(0, peers, step, 0, unroll=min(peers, 16))
    spread = place[...].T[: clusters * nvec].astype(jnp.bfloat16)
    terms = back_ref[...].reshape(peers * back_rows, leaf)
    far_part = jnp.dot(spread, terms, preferred_element_type=jnp.float32)

    me = lax.axis_index("clus")
    edge = slice(2 * cap * nvec, 2 * (cap + 1) * nvec)
    before = joined(x_ref[jnp.maximum(me - 1, 0)][edge].astype(jnp.float32), nvec)
    after = joined(x_ref[jnp.minimum(me + 1, peers - 1)][edge].astype(jnp.float32), nvec)
    before = jnp.where(me > 0, before, 0.0).astype(jnp.bfloat16)
    after = jnp.where(me < peers - 1, after, 0.0).astype(jnp.bfloat16)
    rows = [before] + [src_ref[s] for s in range(clusters)] + [after]
    for s in range(clusters):
        total = far_part[s * nvec : (s + 1) * nvec]
        for o in range(3):
            total += jnp.dot(rows[s + o], near_ref[s, o], preferred_element_type=jnp.float32)
        out_ref[s] = total


def cost(flops, moved):
    return pl.CostEstimate(flops=flops, bytes_accessed=moved, transcendentals=0)


def body(sources, near_blocks, far_u, far_v, send_list, far_slot, ret_list, ret_slot):
    clusters, nvec, leaf = sources.shape
    _, peers, cap = send_list.shape
    blocks, rank, _ = far_u.shape
    slots = peers * cap
    rows = 2 * (cap + 1) * nvec + nvec
    params = pltpu.CompilerParams(vmem_limit_bytes=8 * 2**20)
    message = pl.pallas_call(
        pack_kernel,
        out_shape=jax.ShapeDtypeStruct((peers, rows, leaf // 2), jnp.bfloat16),
        in_specs=[SMEM, SMEM, VMEM],
        out_specs=VMEM,
        compiler_params=params,
        cost_estimate=cost(10**10, peers * rows * leaf),
        name="pack",
    )(send_list[0].T, ret_list[0].T, sources)
    incoming = lax.all_to_all(message, "clus", split_axis=0, concat_axis=0, tiled=True)
    returns = pl.pallas_call(
        far_kernel,
        out_shape=jax.ShapeDtypeStruct((peers, cap * nvec, leaf), jnp.bfloat16),
        in_specs=[SMEM, SMEM, VMEM, VMEM, VMEM],
        out_specs=VMEM,
        scratch_shapes=[pltpu.VMEM((slots, nvec, leaf), jnp.float32)]
        * (5 if peers <= 16 else 2),
        compiler_params=params,
        cost_estimate=cost(4 * blocks * 8 * nvec * leaf * rank, 4 * blocks * rank * leaf),
        name="far",
    )(far_slot, ret_slot, incoming, far_u, far_v)
    back = lax.all_to_all(returns, "clus", split_axis=0, concat_axis=0, tiled=True)
    return pl.pallas_call(
        sum_kernel,
        out_shape=jax.ShapeDtypeStruct((clusters, nvec, leaf), jnp.float32),
        in_specs=[VMEM] * 4,
        out_specs=VMEM,
        scratch_shapes=[pltpu.VMEM((slots * nvec, leaf // 2), jnp.float32)],
        compiler_params=params,
        cost_estimate=cost(2 * 3 * clusters * nvec * leaf * leaf, 6 * clusters * leaf * leaf),
        name="sum",
    )(back, sources, near_blocks, incoming)


def solution(mesh):
    placed = (
        P(("groups", "clus"), None, None),
        P(("groups", "clus"), None, None, None),
        P(("groups", "clus"), None, None),
        P(("groups", "clus"), None, None),
        P(("groups", "clus"), None, None),
        P(("groups", "clus")),
        P(("groups", "clus"), None, None),
        P(("groups", "clus")),
    )
    return jax.shard_map(
        body,
        mesh=mesh,
        in_specs=placed,
        out_specs=P(("groups", "clus"), None, None),
        check_vma=False,
    )
```

```python
import jax
import jax.numpy as jnp
from jax import lax
from jax.experimental import pallas as pl
from jax.experimental.pallas import tpu as pltpu
from jax.sharding import PartitionSpec as P

VMEM = pl.BlockSpec(memory_space=pltpu.VMEM)
CHUNKS = 4
SMEM = pl.BlockSpec(memory_space=pltpu.SMEM)


def halves(x):
    w = x.shape[1] // 2
    return [x[:, :w], x[:, w:]]


def pack_kernel(send_ref, ret_ref, src_ref, out_ref):
    clusters, nvec, leaf = src_ref.shape
    cap, peers = send_ref.shape
    me = lax.axis_index("clus")
    first = src_ref[0].astype(jnp.float32)
    last = src_ref[clusters - 1].astype(jnp.float32)

    def step(p, carry):
        rows = []
        for k in range(cap):
            rows += halves(src_ref[jnp.maximum(send_ref[k, p], 0)].astype(jnp.float32))
        rows += halves(jnp.where(p > me, last, first))
        rows.append(
            jnp.concatenate(
                [
                    jnp.full((nvec // cap, leaf // 2), ret_ref[k, p].astype(jnp.float32))
                    for k in range(cap)
                ],
                axis=0,
            )
        )
        out_ref[p] = jnp.concatenate(rows, axis=0).astype(out_ref.dtype)
        return carry

    lax.fori_loop(0, peers, step, 0, unroll=min(peers, 16))


def joined(rows, nvec):
    return jnp.concatenate([rows[:nvec], rows[nvec:]], axis=1)


def widen_sources(x_ref, xf):
    peers = x_ref.shape[0]
    slots, nvec, _ = xf.shape
    cap = slots // peers

    def widen(p, carry):
        rows = x_ref[p].astype(jnp.float32)
        for k in range(cap):
            xf[p * cap + k] = joined(rows[2 * k * nvec : 2 * (k + 1) * nvec], nvec)
        return carry

    lax.fori_loop(0, peers, widen, 0, unroll=min(peers, 16))


def project(picked, u, owner, nvec, group):
    full = lax.dot_general(picked, u, (((1,), (1,)), ((), ())), preferred_element_type=jnp.float32)
    kept = full[:nvec]
    for i in range(1, group):
        kept = jnp.where(owner == i, full[i * nvec : (i + 1) * nvec], kept)
    return kept


def far_kernel(slot_ref, dest_ref, x_ref, u_ref, v_ref, out_ref, xf, picked, wide):
    peers = x_ref.shape[0]
    slots, nvec, leaf = xf.shape
    blocks, rank, _ = u_ref.shape
    group = leaf // rank
    groups = blocks // group
    per = groups // CHUNKS
    widen_sources(x_ref, xf)
    for g in range(groups):
        rows = [xf[slot_ref[g * group + i]] for i in range(group)]
        picked[g] = jnp.concatenate(rows, axis=0).astype(jnp.bfloat16)
    owner = lax.broadcasted_iota(jnp.int32, (nvec, leaf), 1) // rank
    total = None
    for c in range(CHUNKS):
        for g in range(c * per, (c + 1) * per):
            u = u_ref[g * group : (g + 1) * group].reshape(leaf, leaf)
            kept = project(picked[g], u, owner, nvec, group)
            dest = jnp.full((nvec, leaf), dest_ref[g * group], jnp.int32)
            for i in range(1, group):
                dest = jnp.where(owner == i, dest_ref[g * group + i], dest)
            dest = dest.astype(jnp.float32)
            kept = jnp.concatenate([kept, kept], axis=0).astype(jnp.bfloat16)
            dest = jnp.concatenate([dest, dest - 1.0], axis=0).astype(jnp.bfloat16)
            for o in range(0, slots, 2):
                wide[o * nvec : (o + 2) * nvec, g * leaf : (g + 1) * leaf] = jnp.where(
                    dest == jnp.bfloat16(o), kept, jnp.bfloat16(0)
                )
        v = v_ref[c * per * group : (c + 1) * per * group].reshape(per * leaf, leaf)
        part = jnp.dot(
            wide[:, c * per * leaf : (c + 1) * per * leaf], v, preferred_element_type=jnp.float32
        )
        total = part if total is None else total + part
    out_ref[...] = total.reshape(out_ref.shape).astype(out_ref.dtype)


def far_many_kernel(slot_ref, dest_ref, x_ref, u_ref, v_ref, out_ref, xf, coef, acc):
    slots, nvec, leaf = xf.shape
    blocks, rank, _ = u_ref.shape
    group = leaf // rank
    widen_sources(x_ref, xf)
    acc[...] = jnp.zeros_like(acc)
    owner = lax.broadcasted_iota(jnp.int32, (nvec, leaf), 1) // rank

    def forward(g, carry):
        rows = [xf[slot_ref[g * group + i]] for i in range(group)]
        picked = jnp.concatenate(rows, axis=0).astype(jnp.bfloat16)
        u = u_ref[pl.ds(g * group, group)].reshape(leaf, leaf)
        coef[g] = project(picked, u, owner, nvec, group)
        return carry

    def backward(g, carry):
        kept = coef[g]
        spread = jnp.concatenate(
            [jnp.where(owner == i, kept, 0.0) for i in range(group)], axis=0
        ).astype(jnp.bfloat16)
        v = v_ref[pl.ds(g * group, group)].reshape(leaf, leaf)
        terms = jnp.dot(spread, v, preferred_element_type=jnp.float32)
        for i in range(group):
            acc[dest_ref[g * group + i]] += terms[i * nvec : (i + 1) * nvec]
        return carry

    lax.fori_loop(0, blocks // group, forward, 0, unroll=4)
    lax.fori_loop(0, blocks // group, backward, 0, unroll=4)
    out_ref[...] = acc[...].reshape(out_ref.shape).astype(out_ref.dtype)


def sum_kernel(back_ref, src_ref, near_ref, x_ref, out_ref, place):
    clusters, nvec, leaf = src_ref.shape
    peers, back_rows, _ = back_ref.shape
    cap = back_rows // nvec
    width = leaf // 2
    lane = lax.broadcasted_iota(jnp.int32, (nvec, width), 1)
    sub = lax.broadcasted_iota(jnp.int32, (nvec, width), 0)
    cluster = jnp.where(lane % nvec == sub, lane // nvec, -2).astype(jnp.float32)

    def step(p, carry):
        meta = x_ref[p, 2 * (cap + 1) * nvec :, :].astype(jnp.float32)
        for k in range(cap):
            at = jnp.broadcast_to(meta[k * nvec // cap : k * nvec // cap + 1], (nvec, width))
            place[pl.ds((p * cap + k) * nvec, nvec)] = jnp.where(at == cluster, 1.0, 0.0)
        return carry

    lax.fori_loop(0, peers, step, 0, unroll=min(peers, 16))
    spread = place[...].T[: clusters * nvec].astype(jnp.bfloat16)
    terms = back_ref[...].reshape(peers * back_rows, leaf)
    far_part = jnp.dot(spread, terms, preferred_element_type=jnp.float32)

    me = lax.axis_index("clus")
    edge = slice(2 * cap * nvec, 2 * (cap + 1) * nvec)
    before = joined(x_ref[jnp.maximum(me - 1, 0)][edge].astype(jnp.float32), nvec)
    after = joined(x_ref[jnp.minimum(me + 1, peers - 1)][edge].astype(jnp.float32), nvec)
    before = jnp.where(me > 0, before, 0.0).astype(jnp.bfloat16)
    after = jnp.where(me < peers - 1, after, 0.0).astype(jnp.bfloat16)
    rows = [before] + [src_ref[s] for s in range(clusters)] + [after]
    for s in range(clusters):
        total = far_part[s * nvec : (s + 1) * nvec]
        for o in range(3):
            total += jnp.dot(rows[s + o], near_ref[s, o], preferred_element_type=jnp.float32)
        out_ref[s] = total


def cost(flops, moved):
    return pl.CostEstimate(flops=flops, bytes_accessed=moved, transcendentals=0)


def body(sources, near_blocks, far_u, far_v, send_list, far_slot, ret_list, ret_slot):
    clusters, nvec, leaf = sources.shape
    _, peers, cap = send_list.shape
    blocks, rank, _ = far_u.shape
    slots = peers * cap
    rows = 2 * (cap + 1) * nvec + nvec
    params = pltpu.CompilerParams(vmem_limit_bytes=8 * 2**20)
    message = pl.pallas_call(
        pack_kernel,
        out_shape=jax.ShapeDtypeStruct((peers, rows, leaf // 2), jnp.bfloat16),
        in_specs=[SMEM, SMEM, VMEM],
        out_specs=VMEM,
        compiler_params=params,
        cost_estimate=cost(10**10, peers * rows * leaf),
        name="pack",
    )(send_list[0].T, ret_list[0].T, sources)
    incoming = lax.all_to_all(message, "clus", split_axis=0, concat_axis=0, tiled=True)
    few = slots <= 32
    if few:
        scratch = [
            pltpu.VMEM((blocks * rank // leaf, leaf // rank * nvec, leaf), jnp.bfloat16),
            pltpu.VMEM((slots * nvec, blocks * rank), jnp.bfloat16),
        ]
    else:
        scratch = [
            pltpu.VMEM((blocks * rank // leaf, nvec, leaf), jnp.float32),
            pltpu.VMEM((slots, nvec, leaf), jnp.float32),
        ]
    returns = pl.pallas_call(
        far_kernel if few else far_many_kernel,
        out_shape=jax.ShapeDtypeStruct((peers, cap * nvec, leaf), jnp.bfloat16),
        in_specs=[SMEM, SMEM, VMEM, VMEM, VMEM],
        out_specs=VMEM,
        scratch_shapes=[pltpu.VMEM((slots, nvec, leaf), jnp.float32)] + scratch,
        compiler_params=pltpu.CompilerParams(vmem_limit_bytes=16 * 2**20),
        cost_estimate=cost(4 * blocks * 8 * nvec * leaf * rank, 4 * blocks * rank * leaf),
        name="far",
    )(far_slot, ret_slot, incoming, far_u, far_v)
    back = lax.all_to_all(returns, "clus", split_axis=0, concat_axis=0, tiled=True)
    return pl.pallas_call(
        sum_kernel,
        out_shape=jax.ShapeDtypeStruct((clusters, nvec, leaf), jnp.float32),
        in_specs=[VMEM] * 4,
        out_specs=VMEM,
        scratch_shapes=[pltpu.VMEM((slots * nvec, leaf // 2), jnp.float32)],
        compiler_params=params,
        cost_estimate=cost(2 * 3 * clusters * nvec * leaf * leaf, 6 * clusters * leaf * leaf),
        name="sum",
    )(back, sources, near_blocks, incoming)


def solution(mesh):
    placed = (
        P(("groups", "clus"), None, None),
        P(("groups", "clus"), None, None, None),
        P(("groups", "clus"), None, None),
        P(("groups", "clus"), None, None),
        P(("groups", "clus"), None, None),
        P(("groups", "clus")),
        P(("groups", "clus"), None, None),
        P(("groups", "clus")),
    )
    return jax.shard_map(
        body,
        mesh=mesh,
        in_specs=placed,
        out_specs=P(("groups", "clus"), None, None),
        check_vma=False,
    )
```

```python
import jax
import jax.numpy as jnp
from jax import lax
from jax.experimental import pallas as pl
from jax.experimental.pallas import tpu as pltpu
from jax.sharding import PartitionSpec as P

VMEM = pl.BlockSpec(memory_space=pltpu.VMEM)
CHUNKS = 4
SMEM = pl.BlockSpec(memory_space=pltpu.SMEM)


def halves(x):
    w = x.shape[1] // 2
    return [x[:, :w], x[:, w:]]


def pattern_kernel(out_ref):
    nvec, width = out_ref.shape
    lane = lax.broadcasted_iota(jnp.int32, (nvec, width), 1)
    sub = lax.broadcasted_iota(jnp.int32, (nvec, width), 0)
    out_ref[...] = jnp.where(lane % nvec == sub, lane // nvec, -2).astype(jnp.float32)


def pack_kernel(send_ref, ret_ref, src_ref, pattern_ref, out_ref):
    clusters, nvec, leaf = src_ref.shape
    cap, peers = send_ref.shape
    me = lax.axis_index("clus")
    first = src_ref[0].astype(jnp.float32)
    last = src_ref[clusters - 1].astype(jnp.float32)

    def step(p, carry):
        rows = []
        for k in range(cap):
            rows += halves(src_ref[jnp.maximum(send_ref[k, p], 0)].astype(jnp.float32))
        rows += halves(jnp.where(p > me, last, first))
        rows.append(
            jnp.concatenate(
                [
                    jnp.full((nvec // cap, leaf // 2), ret_ref[k, p].astype(jnp.float32))
                    for k in range(cap)
                ],
                axis=0,
            )
        )
        out_ref[p] = jnp.concatenate(rows, axis=0).astype(out_ref.dtype)
        return carry

    lax.fori_loop(0, peers, step, 0, unroll=min(peers, 16))


def joined(rows, nvec):
    return jnp.concatenate([rows[:nvec], rows[nvec:]], axis=1)


def widen_sources(x_ref, xf):
    peers = x_ref.shape[0]
    slots, nvec, _ = xf.shape
    cap = slots // peers

    def widen(p, carry):
        rows = x_ref[p].astype(jnp.float32)
        for k in range(cap):
            xf[p * cap + k] = joined(rows[2 * k * nvec : 2 * (k + 1) * nvec], nvec)
        return carry

    lax.fori_loop(0, peers, widen, 0, unroll=min(peers, 16))


def project(picked, u, owner, nvec, group):
    full = lax.dot_general(picked, u, (((1,), (1,)), ((), ())), preferred_element_type=jnp.float32)
    kept = full[:nvec]
    for i in range(1, group):
        kept = jnp.where(owner == i, full[i * nvec : (i + 1) * nvec], kept)
    return kept


def far_kernel(slot_ref, dest_ref, x_ref, u_ref, v_ref, out_ref, xf, picked, wide):
    peers = x_ref.shape[0]
    slots, nvec, leaf = xf.shape
    blocks, rank, _ = u_ref.shape
    group = leaf // rank
    groups = blocks // group
    per = groups // CHUNKS
    widen_sources(x_ref, xf)
    for g in range(groups):
        rows = [xf[slot_ref[g * group + i]] for i in range(group)]
        picked[g] = jnp.concatenate(rows, axis=0).astype(jnp.bfloat16)
    owner = lax.broadcasted_iota(jnp.int32, (nvec, leaf), 1) // rank
    total = None
    for c in range(CHUNKS):
        for g in range(c * per, (c + 1) * per):
            u = u_ref[g * group : (g + 1) * group].reshape(leaf, leaf)
            kept = project(picked[g], u, owner, nvec, group)
            dest = jnp.full((nvec, leaf), dest_ref[g * group], jnp.int32)
            for i in range(1, group):
                dest = jnp.where(owner == i, dest_ref[g * group + i], dest)
            dest = dest.astype(jnp.float32)
            kept = jnp.concatenate([kept, kept], axis=0).astype(jnp.bfloat16)
            dest = jnp.concatenate([dest, dest - 1.0], axis=0).astype(jnp.bfloat16)
            for o in range(0, slots, 2):
                wide[o * nvec : (o + 2) * nvec, g * leaf : (g + 1) * leaf] = jnp.where(
                    dest == jnp.bfloat16(o), kept, jnp.bfloat16(0)
                )
        v = v_ref[c * per * group : (c + 1) * per * group].reshape(per * leaf, leaf)
        part = jnp.dot(
            wide[:, c * per * leaf : (c + 1) * per * leaf], v, preferred_element_type=jnp.float32
        )
        total = part if total is None else total + part
    out_ref[...] = total.reshape(out_ref.shape).astype(out_ref.dtype)


def far_many_kernel(slot_ref, dest_ref, x_ref, u_ref, v_ref, out_ref, xf, coef, acc):
    slots, nvec, leaf = xf.shape
    blocks, rank, _ = u_ref.shape
    group = leaf // rank
    widen_sources(x_ref, xf)
    acc[...] = jnp.zeros_like(acc)
    owner = lax.broadcasted_iota(jnp.int32, (nvec, leaf), 1) // rank

    def forward(g, carry):
        rows = [xf[slot_ref[g * group + i]] for i in range(group)]
        picked = jnp.concatenate(rows, axis=0).astype(jnp.bfloat16)
        u = u_ref[pl.ds(g * group, group)].reshape(leaf, leaf)
        coef[g] = project(picked, u, owner, nvec, group)
        return carry

    def backward(g, carry):
        kept = coef[g]
        spread = jnp.concatenate(
            [jnp.where(owner == i, kept, 0.0) for i in range(group)], axis=0
        ).astype(jnp.bfloat16)
        v = v_ref[pl.ds(g * group, group)].reshape(leaf, leaf)
        terms = jnp.dot(spread, v, preferred_element_type=jnp.float32)
        for i in range(group):
            acc[dest_ref[g * group + i]] += terms[i * nvec : (i + 1) * nvec]
        return carry

    lax.fori_loop(0, blocks // group, forward, 0, unroll=4)
    lax.fori_loop(0, blocks // group, backward, 0, unroll=4)
    out_ref[...] = acc[...].reshape(out_ref.shape).astype(out_ref.dtype)


def sum_kernel(back_ref, src_ref, near_ref, x_ref, pattern_ref, out_ref, place):
    clusters, nvec, leaf = src_ref.shape
    peers, back_rows, _ = back_ref.shape
    cap = back_rows // nvec
    width = leaf // 2
    cluster = pattern_ref[...]

    def step(p, carry):
        meta = x_ref[p, 2 * (cap + 1) * nvec :, :].astype(jnp.float32)
        for k in range(cap):
            at = jnp.broadcast_to(meta[k * nvec // cap : k * nvec // cap + 1], (nvec, width))
            place[pl.ds((p * cap + k) * nvec, nvec)] = jnp.where(at == cluster, 1.0, 0.0)
        return carry

    lax.fori_loop(0, peers, step, 0, unroll=min(peers, 16))
    spread = place[...].T[: clusters * nvec].astype(jnp.bfloat16)
    terms = back_ref[...].reshape(peers * back_rows, leaf)
    far_part = jnp.dot(spread, terms, preferred_element_type=jnp.float32)

    me = lax.axis_index("clus")
    edge = slice(2 * cap * nvec, 2 * (cap + 1) * nvec)
    before = joined(x_ref[jnp.maximum(me - 1, 0)][edge].astype(jnp.float32), nvec)
    after = joined(x_ref[jnp.minimum(me + 1, peers - 1)][edge].astype(jnp.float32), nvec)
    before = jnp.where(me > 0, before, 0.0).astype(jnp.bfloat16)
    after = jnp.where(me < peers - 1, after, 0.0).astype(jnp.bfloat16)
    rows = [before] + [src_ref[s] for s in range(clusters)] + [after]
    for s in range(clusters):
        total = jnp.dot(
            jnp.concatenate(rows[s : s + 3], axis=1),
            near_ref[s].reshape(3 * leaf, leaf),
            preferred_element_type=jnp.float32,
        )
        out_ref[s] = far_part[s * nvec : (s + 1) * nvec] + total


def cost(flops, moved):
    return pl.CostEstimate(flops=flops, bytes_accessed=moved, transcendentals=0)


def body(sources, near_blocks, far_u, far_v, send_list, far_slot, ret_list, ret_slot):
    clusters, nvec, leaf = sources.shape
    _, peers, cap = send_list.shape
    blocks, rank, _ = far_u.shape
    slots = peers * cap
    rows = 2 * (cap + 1) * nvec + nvec
    params = pltpu.CompilerParams(vmem_limit_bytes=8 * 2**20)
    pattern = pl.pallas_call(
        pattern_kernel,
        out_shape=jax.ShapeDtypeStruct((nvec, leaf // 2), jnp.float32),
        out_specs=VMEM,
        compiler_params=params,
        cost_estimate=cost(10**10, nvec * leaf * 2),
        name="pattern",
    )()
    message = pl.pallas_call(
        pack_kernel,
        out_shape=jax.ShapeDtypeStruct((peers, rows, leaf // 2), jnp.bfloat16),
        in_specs=[SMEM, SMEM, VMEM, VMEM],
        out_specs=VMEM,
        compiler_params=params,
        cost_estimate=cost(10**10, peers * rows * leaf),
        name="pack",
    )(send_list[0].T, ret_list[0].T, sources, pattern)
    incoming = lax.all_to_all(message, "clus", split_axis=0, concat_axis=0, tiled=True)
    few = slots <= 32
    if few:
        scratch = [
            pltpu.VMEM((blocks * rank // leaf, leaf // rank * nvec, leaf), jnp.bfloat16),
            pltpu.VMEM((slots * nvec, blocks * rank), jnp.bfloat16),
        ]
    else:
        scratch = [
            pltpu.VMEM((blocks * rank // leaf, nvec, leaf), jnp.float32),
            pltpu.VMEM((slots, nvec, leaf), jnp.float32),
        ]
    returns = pl.pallas_call(
        far_kernel if few else far_many_kernel,
        out_shape=jax.ShapeDtypeStruct((peers, cap * nvec, leaf), jnp.bfloat16),
        in_specs=[SMEM, SMEM, VMEM, VMEM, VMEM],
        out_specs=VMEM,
        scratch_shapes=[pltpu.VMEM((slots, nvec, leaf), jnp.float32)] + scratch,
        compiler_params=pltpu.CompilerParams(vmem_limit_bytes=16 * 2**20),
        cost_estimate=cost(4 * blocks * 8 * nvec * leaf * rank, 4 * blocks * rank * leaf),
        name="far",
    )(far_slot, ret_slot, incoming, far_u, far_v)
    back = lax.all_to_all(returns, "clus", split_axis=0, concat_axis=0, tiled=True)
    return pl.pallas_call(
        sum_kernel,
        out_shape=jax.ShapeDtypeStruct((clusters, nvec, leaf), jnp.float32),
        in_specs=[VMEM] * 5,
        out_specs=VMEM,
        scratch_shapes=[pltpu.VMEM((slots * nvec, leaf // 2), jnp.float32)],
        compiler_params=params,
        cost_estimate=cost(2 * 3 * clusters * nvec * leaf * leaf, 6 * clusters * leaf * leaf),
        name="sum",
    )(back, sources, near_blocks, incoming, pattern)


def solution(mesh):
    placed = (
        P(("groups", "clus"), None, None),
        P(("groups", "clus"), None, None, None),
        P(("groups", "clus"), None, None),
        P(("groups", "clus"), None, None),
        P(("groups", "clus"), None, None),
        P(("groups", "clus")),
        P(("groups", "clus"), None, None),
        P(("groups", "clus")),
    )
    return jax.shard_map(
        body,
        mesh=mesh,
        in_specs=placed,
        out_specs=P(("groups", "clus"), None, None),
        check_vma=False,
    )
```

```python
import jax
import jax.numpy as jnp
from jax import lax
from jax.experimental import pallas as pl
from jax.experimental.pallas import tpu as pltpu
from jax.sharding import PartitionSpec as P

VMEM = pl.BlockSpec(memory_space=pltpu.VMEM)
CHUNKS = 4
SMEM = pl.BlockSpec(memory_space=pltpu.SMEM)


def halves(x):
    w = x.shape[1] // 2
    return [x[:, :w], x[:, w:]]


def pattern_kernel(out_ref):
    nvec, width = out_ref.shape
    lane = lax.broadcasted_iota(jnp.int32, (nvec, width), 1)
    sub = lax.broadcasted_iota(jnp.int32, (nvec, width), 0)
    out_ref[...] = jnp.where(lane % nvec == sub, lane // nvec, -2).astype(jnp.float32)


def pack_kernel(send_ref, ret_ref, src_ref, pattern_ref, out_ref):
    clusters, nvec, leaf = src_ref.shape
    cap, peers = send_ref.shape
    me = lax.axis_index("clus")
    first = src_ref[0].astype(jnp.float32)
    last = src_ref[clusters - 1].astype(jnp.float32)

    def step(p, carry):
        rows = []
        for k in range(cap):
            rows += halves(src_ref[jnp.maximum(send_ref[k, p], 0)].astype(jnp.float32))
        rows += halves(jnp.where(p > me, last, first))
        rows.append(
            jnp.concatenate(
                [
                    jnp.full((nvec // cap, leaf // 2), ret_ref[k, p].astype(jnp.float32))
                    for k in range(cap)
                ],
                axis=0,
            )
        )
        out_ref[p] = jnp.concatenate(rows, axis=0).astype(out_ref.dtype)
        return carry

    lax.fori_loop(0, peers, step, 0, unroll=min(peers, 16))


def joined(rows, nvec):
    return jnp.concatenate([rows[:nvec], rows[nvec:]], axis=1)


def widen_sources(x_ref, xf):
    peers = x_ref.shape[0]
    slots, nvec, _ = xf.shape
    cap = slots // peers

    def widen(p, carry):
        rows = x_ref[p].astype(jnp.float32)
        for k in range(cap):
            xf[p * cap + k] = joined(rows[2 * k * nvec : 2 * (k + 1) * nvec], nvec)
        return carry

    lax.fori_loop(0, peers, widen, 0, unroll=min(peers, 16))


def placement(x_ref, pattern_ref, place, place_out):
    nvec, width = pattern_ref.shape
    peers, rows, _ = x_ref.shape
    cap = place.shape[0] // (peers * nvec)

    def step(p, carry):
        meta = x_ref[p, rows - nvec :, :].astype(jnp.float32)
        for k in range(cap):
            at = jnp.broadcast_to(meta[k * nvec // cap : k * nvec // cap + 1], (nvec, width))
            place[pl.ds((p * cap + k) * nvec, nvec)] = jnp.where(at == pattern_ref[...], 1.0, 0.0)
        return carry

    lax.fori_loop(0, peers, step, 0, unroll=min(peers, 16))
    place_out[...] = place[...].T[: place_out.shape[0]].astype(jnp.bfloat16)


def project(picked, u, owner, nvec, group):
    full = lax.dot_general(picked, u, (((1,), (1,)), ((), ())), preferred_element_type=jnp.float32)
    kept = full[:nvec]
    for i in range(1, group):
        kept = jnp.where(owner == i, full[i * nvec : (i + 1) * nvec], kept)
    return kept


def far_kernel(slot_ref, dest_ref, x_ref, u_ref, v_ref, pattern_ref, out_ref, place_out, xf, place, picked, wide, acc):
    peers = x_ref.shape[0]
    slots, nvec, leaf = xf.shape
    blocks, rank, _ = u_ref.shape
    group = leaf // rank
    groups = blocks // group
    per = groups // CHUNKS
    widen_sources(x_ref, xf)
    placement(x_ref, pattern_ref, place, place_out)
    owner = lax.broadcasted_iota(jnp.int32, (nvec, leaf), 1) // rank
    acc[...] = jnp.zeros_like(acc)

    def chunk(c, carry):
        first = c * per
        for g in range(per):
            rows = [xf[slot_ref[(first + g) * group + i]] for i in range(group)]
            picked[g] = jnp.concatenate(rows, axis=0).astype(jnp.bfloat16)
        for g in range(per):
            u = u_ref[pl.ds((first + g) * group, group)].reshape(leaf, leaf)
            kept = project(picked[g], u, owner, nvec, group)
            dest = jnp.full((nvec, leaf), dest_ref[(first + g) * group], jnp.int32)
            for i in range(1, group):
                dest = jnp.where(owner == i, dest_ref[(first + g) * group + i], dest)
            dest = dest.astype(jnp.float32)
            kept = jnp.concatenate([kept, kept], axis=0).astype(jnp.bfloat16)
            dest = jnp.concatenate([dest, dest - 1.0], axis=0).astype(jnp.bfloat16)
            for o in range(0, slots, 2):
                wide[o * nvec : (o + 2) * nvec, g * leaf : (g + 1) * leaf] = jnp.where(
                    dest == jnp.bfloat16(o), kept, jnp.bfloat16(0)
                )
        v = v_ref[pl.ds(first * group, per * group)].reshape(per * leaf, leaf)
        acc[...] += jnp.dot(wide[...], v, preferred_element_type=jnp.float32)
        return carry

    lax.fori_loop(0, CHUNKS, chunk, 0)
    out_ref[...] = acc[...].reshape(out_ref.shape).astype(out_ref.dtype)


def far_many_kernel(slot_ref, dest_ref, x_ref, u_ref, v_ref, pattern_ref, out_ref, place_out, xf, place, coef, acc):
    slots, nvec, leaf = xf.shape
    blocks, rank, _ = u_ref.shape
    group = leaf // rank
    widen_sources(x_ref, xf)
    placement(x_ref, pattern_ref, place, place_out)
    acc[...] = jnp.zeros_like(acc)
    owner = lax.broadcasted_iota(jnp.int32, (nvec, leaf), 1) // rank

    def forward(g, carry):
        rows = [xf[slot_ref[g * group + i]] for i in range(group)]
        picked = jnp.concatenate(rows, axis=0).astype(jnp.bfloat16)
        u = u_ref[pl.ds(g * group, group)].reshape(leaf, leaf)
        coef[g] = project(picked, u, owner, nvec, group)
        return carry

    def backward(g, carry):
        kept = coef[g]
        spread = jnp.concatenate(
            [jnp.where(owner == i, kept, 0.0) for i in range(group)], axis=0
        ).astype(jnp.bfloat16)
        v = v_ref[pl.ds(g * group, group)].reshape(leaf, leaf)
        terms = jnp.dot(spread, v, preferred_element_type=jnp.float32)
        for i in range(group):
            acc[dest_ref[g * group + i]] += terms[i * nvec : (i + 1) * nvec]
        return carry

    lax.fori_loop(0, blocks // group, forward, 0, unroll=4)
    lax.fori_loop(0, blocks // group, backward, 0, unroll=4)
    out_ref[...] = acc[...].reshape(out_ref.shape).astype(out_ref.dtype)


def sum_kernel(back_ref, src_ref, near_ref, x_ref, place_ref, out_ref):
    clusters, nvec, leaf = src_ref.shape
    peers, back_rows, _ = back_ref.shape
    cap = back_rows // nvec
    terms = back_ref[...].reshape(peers * back_rows, leaf)
    far_part = jnp.dot(place_ref[...], terms, preferred_element_type=jnp.float32)

    me = lax.axis_index("clus")
    edge = slice(2 * cap * nvec, 2 * (cap + 1) * nvec)
    before = joined(x_ref[jnp.maximum(me - 1, 0)][edge].astype(jnp.float32), nvec)
    after = joined(x_ref[jnp.minimum(me + 1, peers - 1)][edge].astype(jnp.float32), nvec)
    before = jnp.where(me > 0, before, 0.0).astype(jnp.bfloat16)
    after = jnp.where(me < peers - 1, after, 0.0).astype(jnp.bfloat16)
    rows = [before] + [src_ref[s] for s in range(clusters)] + [after]
    for s in range(clusters):
        total = jnp.dot(
            jnp.concatenate(rows[s : s + 3], axis=1),
            near_ref[s].reshape(3 * leaf, leaf),
            preferred_element_type=jnp.float32,
        )
        out_ref[s] = far_part[s * nvec : (s + 1) * nvec] + total


def cost(flops, moved):
    return pl.CostEstimate(flops=flops, bytes_accessed=moved, transcendentals=0)


def body(sources, near_blocks, far_u, far_v, send_list, far_slot, ret_list, ret_slot):
    clusters, nvec, leaf = sources.shape
    _, peers, cap = send_list.shape
    blocks, rank, _ = far_u.shape
    slots = peers * cap
    rows = 2 * (cap + 1) * nvec + nvec
    params = pltpu.CompilerParams(vmem_limit_bytes=8 * 2**20)
    pattern = pl.pallas_call(
        pattern_kernel,
        out_shape=jax.ShapeDtypeStruct((nvec, leaf // 2), jnp.float32),
        out_specs=VMEM,
        compiler_params=params,
        cost_estimate=cost(10**10, nvec * leaf * 2),
        name="pattern",
    )()
    message = pl.pallas_call(
        pack_kernel,
        out_shape=jax.ShapeDtypeStruct((peers, rows, leaf // 2), jnp.bfloat16),
        in_specs=[SMEM, SMEM, VMEM, VMEM],
        out_specs=VMEM,
        compiler_params=params,
        cost_estimate=cost(10**10, peers * rows * leaf),
        name="pack",
    )(send_list[0].T, ret_list[0].T, sources, pattern)
    incoming = lax.all_to_all(message, "clus", split_axis=0, concat_axis=0, tiled=True)
    few = slots <= 32
    if few:
        scratch = [
            pltpu.VMEM((blocks * rank // leaf // CHUNKS, leaf // rank * nvec, leaf), jnp.bfloat16),
            pltpu.VMEM((slots * nvec, blocks * rank // CHUNKS), jnp.bfloat16),
            pltpu.VMEM((slots * nvec, leaf), jnp.float32),
        ]
    else:
        scratch = [
            pltpu.VMEM((blocks * rank // leaf, nvec, leaf), jnp.float32),
            pltpu.VMEM((slots, nvec, leaf), jnp.float32),
        ]
    returns, place = pl.pallas_call(
        far_kernel if few else far_many_kernel,
        out_shape=(
            jax.ShapeDtypeStruct((peers, cap * nvec, leaf), jnp.bfloat16),
            jax.ShapeDtypeStruct((clusters * nvec, slots * nvec), jnp.bfloat16),
        ),
        in_specs=[SMEM, SMEM, VMEM, VMEM, VMEM, VMEM],
        out_specs=(VMEM, VMEM),
        scratch_shapes=[
            pltpu.VMEM((slots, nvec, leaf), jnp.float32),
            pltpu.VMEM((slots * nvec, leaf // 2), jnp.float32),
        ]
        + scratch,
        compiler_params=pltpu.CompilerParams(vmem_limit_bytes=16 * 2**20),
        cost_estimate=cost(4 * blocks * 8 * nvec * leaf * rank, 4 * blocks * rank * leaf),
        name="far",
    )(far_slot, ret_slot, incoming, far_u, far_v, pattern)
    back = lax.all_to_all(returns, "clus", split_axis=0, concat_axis=0, tiled=True)
    return pl.pallas_call(
        sum_kernel,
        out_shape=jax.ShapeDtypeStruct((clusters, nvec, leaf), jnp.float32),
        in_specs=[VMEM] * 5,
        out_specs=VMEM,
        compiler_params=params,
        cost_estimate=cost(2 * 3 * clusters * nvec * leaf * leaf, 6 * clusters * leaf * leaf),
        name="sum",
    )(back, sources, near_blocks, incoming, place)


def solution(mesh):
    placed = (
        P(("groups", "clus"), None, None),
        P(("groups", "clus"), None, None, None),
        P(("groups", "clus"), None, None),
        P(("groups", "clus"), None, None),
        P(("groups", "clus"), None, None),
        P(("groups", "clus")),
        P(("groups", "clus"), None, None),
        P(("groups", "clus")),
    )
    return jax.shard_map(
        body,
        mesh=mesh,
        in_specs=placed,
        out_specs=P(("groups", "clus"), None, None),
        check_vma=False,
    )
```

```python
import jax
import jax.numpy as jnp
from jax import lax
from jax.experimental import pallas as pl
from jax.experimental.pallas import tpu as pltpu
from jax.sharding import PartitionSpec as P

VMEM = pl.BlockSpec(memory_space=pltpu.VMEM)
CHUNKS = 4
SMEM = pl.BlockSpec(memory_space=pltpu.SMEM)


def halves(x):
    w = x.shape[1] // 2
    return [x[:, :w], x[:, w:]]


def pattern_kernel(out_ref):
    nvec, width = out_ref.shape
    lane = lax.broadcasted_iota(jnp.int32, (nvec, width), 1)
    sub = lax.broadcasted_iota(jnp.int32, (nvec, width), 0)
    out_ref[...] = jnp.where(lane % nvec == sub, lane // nvec, -2).astype(jnp.float32)


def pack_kernel(send_ref, ret_ref, src_ref, pattern_ref, out_ref):
    clusters, nvec, leaf = src_ref.shape
    cap, peers = send_ref.shape
    inner = out_ref.shape[0]
    me = lax.axis_index("clus")
    first = src_ref[0].astype(jnp.float32)
    last = src_ref[clusters - 1].astype(jnp.float32)

    def step(p, carry):
        rows = []
        for k in range(cap):
            rows += halves(src_ref[jnp.maximum(send_ref[k, p], 0)].astype(jnp.float32))
        rows += halves(jnp.where(p > me, last, first))
        rows.append(
            jnp.concatenate(
                [
                    jnp.full((nvec // cap, leaf // 2), ret_ref[k, p].astype(jnp.float32))
                    for k in range(cap)
                ],
                axis=0,
            )
        )
        out_ref[p % inner, p // inner] = jnp.concatenate(rows, axis=0).astype(out_ref.dtype)
        return carry

    lax.fori_loop(0, peers, step, 0, unroll=min(peers, 16))


def regroup_kernel(x_ref, out_ref):
    for i in range(x_ref.shape[0]):
        for j in range(x_ref.shape[1]):
            out_ref[j, i] = x_ref[i, j]


def exchange(x, inner, params):
    outer = x.shape[1]
    rows = [[o * inner + i for i in range(inner)] for o in range(outer)]
    columns = [[o * inner + i for o in range(outer)] for i in range(inner)]
    x = lax.all_to_all(x, "clus", 0, 0, axis_index_groups=rows, tiled=True)
    x = pl.pallas_call(
        regroup_kernel,
        out_shape=jax.ShapeDtypeStruct((outer, inner) + x.shape[2:], x.dtype),
        in_specs=[VMEM],
        out_specs=VMEM,
        compiler_params=params,
        cost_estimate=cost(0, 2 * x.size * 2),
        name="regroup",
    )(x)
    x = lax.all_to_all(x, "clus", 0, 0, axis_index_groups=columns, tiled=True)
    return x.reshape((inner * outer,) + x.shape[2:])


def joined(rows, nvec):
    return jnp.concatenate([rows[:nvec], rows[nvec:]], axis=1)


def widen_sources(x_ref, xf):
    peers = x_ref.shape[0]
    slots, nvec, _ = xf.shape
    cap = slots // peers

    def widen(p, carry):
        rows = x_ref[p].astype(jnp.float32)
        for k in range(cap):
            xf[p * cap + k] = joined(rows[2 * k * nvec : 2 * (k + 1) * nvec], nvec)
        return carry

    lax.fori_loop(0, peers, widen, 0, unroll=min(peers, 16))


def project(picked, u, owner, nvec, group):
    full = lax.dot_general(picked, u, (((1,), (1,)), ((), ())), preferred_element_type=jnp.float32)
    kept = full[:nvec]
    for i in range(1, group):
        kept = jnp.where(owner == i, full[i * nvec : (i + 1) * nvec], kept)
    return kept


def put(total, out_ref):
    inner, outer, rows, _ = out_ref.shape
    for p in range(inner * outer):
        out_ref[p % inner, p // inner] = total[p * rows : (p + 1) * rows].astype(out_ref.dtype)


def far_kernel(slot_ref, dest_ref, x_ref, u_ref, v_ref, out_ref, xf, picked, wide):
    peers = x_ref.shape[0]
    slots, nvec, leaf = xf.shape
    blocks, rank, _ = u_ref.shape
    group = leaf // rank
    groups = blocks // group
    per = groups // CHUNKS
    widen_sources(x_ref, xf)
    for g in range(groups):
        rows = [xf[slot_ref[g * group + i]] for i in range(group)]
        picked[g] = jnp.concatenate(rows, axis=0).astype(jnp.bfloat16)
    owner = lax.broadcasted_iota(jnp.int32, (nvec, leaf), 1) // rank
    total = None
    for c in range(CHUNKS):
        for g in range(c * per, (c + 1) * per):
            u = u_ref[g * group : (g + 1) * group].reshape(leaf, leaf)
            kept = project(picked[g], u, owner, nvec, group)
            dest = jnp.full((nvec, leaf), dest_ref[g * group], jnp.int32)
            for i in range(1, group):
                dest = jnp.where(owner == i, dest_ref[g * group + i], dest)
            dest = dest.astype(jnp.float32)
            kept = jnp.concatenate([kept, kept], axis=0).astype(jnp.bfloat16)
            dest = jnp.concatenate([dest, dest - 1.0], axis=0).astype(jnp.bfloat16)
            for o in range(0, slots, 2):
                wide[o * nvec : (o + 2) * nvec, g * leaf : (g + 1) * leaf] = jnp.where(
                    dest == jnp.bfloat16(o), kept, jnp.bfloat16(0)
                )
        v = v_ref[c * per * group : (c + 1) * per * group].reshape(per * leaf, leaf)
        part = jnp.dot(
            wide[:, c * per * leaf : (c + 1) * per * leaf], v, preferred_element_type=jnp.float32
        )
        total = part if total is None else total + part
    put(total, out_ref)


def far_many_kernel(slot_ref, dest_ref, x_ref, u_ref, v_ref, out_ref, xf, coef, acc):
    slots, nvec, leaf = xf.shape
    blocks, rank, _ = u_ref.shape
    group = leaf // rank
    widen_sources(x_ref, xf)
    acc[...] = jnp.zeros_like(acc)
    owner = lax.broadcasted_iota(jnp.int32, (nvec, leaf), 1) // rank

    def forward(g, carry):
        rows = [xf[slot_ref[g * group + i]] for i in range(group)]
        picked = jnp.concatenate(rows, axis=0).astype(jnp.bfloat16)
        u = u_ref[pl.ds(g * group, group)].reshape(leaf, leaf)
        coef[g] = project(picked, u, owner, nvec, group)
        return carry

    def backward(g, carry):
        kept = coef[g]
        spread = jnp.concatenate(
            [jnp.where(owner == i, kept, 0.0) for i in range(group)], axis=0
        ).astype(jnp.bfloat16)
        v = v_ref[pl.ds(g * group, group)].reshape(leaf, leaf)
        terms = jnp.dot(spread, v, preferred_element_type=jnp.float32)
        for i in range(group):
            acc[dest_ref[g * group + i]] += terms[i * nvec : (i + 1) * nvec]
        return carry

    lax.fori_loop(0, blocks // group, forward, 0, unroll=4)
    lax.fori_loop(0, blocks // group, backward, 0, unroll=4)
    put(acc[...].reshape(slots * nvec, leaf), out_ref)


def sum_kernel(back_ref, src_ref, near_ref, x_ref, pattern_ref, out_ref, place):
    clusters, nvec, leaf = src_ref.shape
    peers, back_rows, _ = back_ref.shape
    cap = back_rows // nvec
    width = leaf // 2
    cluster = pattern_ref[...]

    def step(p, carry):
        meta = x_ref[p, 2 * (cap + 1) * nvec :, :].astype(jnp.float32)
        for k in range(cap):
            at = jnp.broadcast_to(meta[k * nvec // cap : k * nvec // cap + 1], (nvec, width))
            place[pl.ds((p * cap + k) * nvec, nvec)] = jnp.where(at == cluster, 1.0, 0.0)
        return carry

    lax.fori_loop(0, peers, step, 0, unroll=min(peers, 16))
    spread = place[...].T[: clusters * nvec].astype(jnp.bfloat16)
    terms = back_ref[...].reshape(peers * back_rows, leaf)
    far_part = jnp.dot(spread, terms, preferred_element_type=jnp.float32)

    me = lax.axis_index("clus")
    edge = slice(2 * cap * nvec, 2 * (cap + 1) * nvec)
    before = joined(x_ref[jnp.maximum(me - 1, 0)][edge].astype(jnp.float32), nvec)
    after = joined(x_ref[jnp.minimum(me + 1, peers - 1)][edge].astype(jnp.float32), nvec)
    before = jnp.where(me > 0, before, 0.0).astype(jnp.bfloat16)
    after = jnp.where(me < peers - 1, after, 0.0).astype(jnp.bfloat16)
    rows = [before] + [src_ref[s] for s in range(clusters)] + [after]
    for s in range(clusters):
        total = jnp.dot(
            jnp.concatenate(rows[s : s + 3], axis=1),
            near_ref[s].reshape(3 * leaf, leaf),
            preferred_element_type=jnp.float32,
        )
        out_ref[s] = far_part[s * nvec : (s + 1) * nvec] + total


def cost(flops, moved):
    return pl.CostEstimate(flops=flops, bytes_accessed=moved, transcendentals=0)


def body(sources, near_blocks, far_u, far_v, send_list, far_slot, ret_list, ret_slot):
    clusters, nvec, leaf = sources.shape
    _, peers, cap = send_list.shape
    blocks, rank, _ = far_u.shape
    slots = peers * cap
    inner = 4 if peers % 4 == 0 else 1
    rows = 2 * (cap + 1) * nvec + nvec
    params = pltpu.CompilerParams(vmem_limit_bytes=8 * 2**20)
    pattern = pl.pallas_call(
        pattern_kernel,
        out_shape=jax.ShapeDtypeStruct((nvec, leaf // 2), jnp.float32),
        out_specs=VMEM,
        compiler_params=params,
        cost_estimate=cost(10**10, nvec * leaf * 2),
        name="pattern",
    )()
    message = pl.pallas_call(
        pack_kernel,
        out_shape=jax.ShapeDtypeStruct((inner, peers // inner, rows, leaf // 2), jnp.bfloat16),
        in_specs=[SMEM, SMEM, VMEM, VMEM],
        out_specs=VMEM,
        compiler_params=params,
        cost_estimate=cost(10**10, peers * rows * leaf),
        name="pack",
    )(send_list[0].T, ret_list[0].T, sources, pattern)
    incoming = exchange(message, inner, params)
    few = slots <= 32
    if few:
        scratch = [
            pltpu.VMEM((blocks * rank // leaf, leaf // rank * nvec, leaf), jnp.bfloat16),
            pltpu.VMEM((slots * nvec, blocks * rank), jnp.bfloat16),
        ]
    else:
        scratch = [
            pltpu.VMEM((blocks * rank // leaf, nvec, leaf), jnp.float32),
            pltpu.VMEM((slots, nvec, leaf), jnp.float32),
        ]
    returns = pl.pallas_call(
        far_kernel if few else far_many_kernel,
        out_shape=jax.ShapeDtypeStruct((inner, peers // inner, cap * nvec, leaf), jnp.bfloat16),
        in_specs=[SMEM, SMEM, VMEM, VMEM, VMEM],
        out_specs=VMEM,
        scratch_shapes=[pltpu.VMEM((slots, nvec, leaf), jnp.float32)] + scratch,
        compiler_params=pltpu.CompilerParams(vmem_limit_bytes=16 * 2**20),
        cost_estimate=cost(4 * blocks * 8 * nvec * leaf * rank, 4 * blocks * rank * leaf),
        name="far",
    )(far_slot, ret_slot, incoming, far_u, far_v)
    back = exchange(returns, inner, params)
    return pl.pallas_call(
        sum_kernel,
        out_shape=jax.ShapeDtypeStruct((clusters, nvec, leaf), jnp.float32),
        in_specs=[VMEM] * 5,
        out_specs=VMEM,
        scratch_shapes=[pltpu.VMEM((slots * nvec, leaf // 2), jnp.float32)],
        compiler_params=params,
        cost_estimate=cost(2 * 3 * clusters * nvec * leaf * leaf, 6 * clusters * leaf * leaf),
        name="sum",
    )(back, sources, near_blocks, incoming, pattern)


def solution(mesh):
    placed = (
        P(("groups", "clus"), None, None),
        P(("groups", "clus"), None, None, None),
        P(("groups", "clus"), None, None),
        P(("groups", "clus"), None, None),
        P(("groups", "clus"), None, None),
        P(("groups", "clus")),
        P(("groups", "clus"), None, None),
        P(("groups", "clus")),
    )
    return jax.shard_map(
        body,
        mesh=mesh,
        in_specs=placed,
        out_specs=P(("groups", "clus"), None, None),
        check_vma=False,
    )
```

```python
import jax
import jax.numpy as jnp
from jax import lax
from jax.experimental import pallas as pl
from jax.experimental.pallas import tpu as pltpu
from jax.sharding import PartitionSpec as P

VMEM = pl.BlockSpec(memory_space=pltpu.VMEM)
ANY = pl.BlockSpec(memory_space=pl.ANY)
CHUNKS = 8


def halves(x):
    w = x.shape[1] // 2
    return [x[:, :w], x[:, w:]]


def pattern_kernel(out_ref):
    nvec, width = out_ref.shape
    lane = lax.broadcasted_iota(jnp.int32, (nvec, width), 1)
    sub = lax.broadcasted_iota(jnp.int32, (nvec, width), 0)
    out_ref[...] = jnp.where(lane % nvec == sub, lane // nvec, -2).astype(jnp.float32)


def pack_kernel(send_ref, ret_ref, src_ref, pattern_ref, out_ref):
    clusters, nvec, leaf = src_ref.shape
    cap, peers = send_ref.shape
    me = lax.axis_index("clus")
    rows = peers * nvec
    repeat = lax.broadcasted_iota(jnp.int32, (rows, peers), 0) // nvec
    repeat = (repeat == lax.broadcasted_iota(jnp.int32, (rows, peers), 1)).astype(jnp.bfloat16)

    def columns(list_ref):
        entries = list_ref[...].astype(jnp.float32).astype(jnp.bfloat16)
        return lax.dot_general(
            repeat, entries, (((1,), (1,)), ((), ())), preferred_element_type=jnp.float32
        )

    send = jnp.maximum(columns(send_ref), 0.0)
    ret = columns(ret_ref)
    row = lax.broadcasted_iota(jnp.int32, (rows, clusters * nvec), 0)
    lane = lax.broadcasted_iota(jnp.int32, (rows, clusters * nvec), 1)
    cluster = jnp.where(row % nvec == lane % nvec, lane // nvec, -2).astype(jnp.float32)
    source = src_ref[...].reshape(clusters * nvec, leaf)
    picked = []
    for k in range(cap):
        pick = jnp.where(send[:, k : k + 1] == cluster, 1.0, 0.0).astype(jnp.bfloat16)
        picked.append(jnp.dot(pick, source, preferred_element_type=jnp.float32))
    vector = lax.broadcasted_iota(jnp.int32, (rows, leaf // 2), 0) % nvec
    places = jnp.broadcast_to(ret[:, :1], (rows, leaf // 2))
    for k in range(1, cap):
        places = jnp.where(vector >= k * nvec // cap, ret[:, k : k + 1], places)
    first = src_ref[0].astype(jnp.float32)
    last = src_ref[clusters - 1].astype(jnp.float32)
    for p in range(peers):
        at = slice(p * nvec, (p + 1) * nvec)
        parts = []
        for k in range(cap):
            parts += halves(picked[k][at])
        parts += halves(jnp.where(p > me, last, first))
        parts.append(places[at])
        out_ref[p] = jnp.concatenate(parts, axis=0).astype(out_ref.dtype)


def joined(rows, nvec):
    return jnp.concatenate([rows[:nvec], rows[nvec:]], axis=1)


def load_slots(slots_any, dests_any, slot_ref, dest_ref, sems):
    copies = [
        pltpu.make_async_copy(slots_any, slot_ref, sems.at[0]),
        pltpu.make_async_copy(dests_any, dest_ref, sems.at[1]),
    ]
    for copy in copies:
        copy.start()
    return copies


def widen_sources(x_ref, xf):
    peers = x_ref.shape[0]
    slots, nvec, _ = xf.shape
    cap = slots // peers

    def widen(p, carry):
        rows = x_ref[p].astype(jnp.float32)
        for k in range(cap):
            xf[p * cap + k] = joined(rows[2 * k * nvec : 2 * (k + 1) * nvec], nvec)
        return carry

    lax.fori_loop(0, peers, widen, 0, unroll=min(peers, 16))


def project(picked, u, owner, nvec, group):
    full = lax.dot_general(picked, u, (((1,), (1,)), ((), ())), preferred_element_type=jnp.float32)
    kept = full[:nvec]
    for i in range(1, group):
        kept = jnp.where(owner == i, full[i * nvec : (i + 1) * nvec], kept)
    return kept


def far_kernel(
    slots_any, dests_any, x_ref, u_ref, v_ref, out_ref, slot_ref, dest_ref, sems, xf, picked, wide
):
    peers = x_ref.shape[0]
    slots, nvec, leaf = xf.shape
    blocks, rank, _ = u_ref.shape
    group = leaf // rank
    groups = blocks // group
    per = groups // CHUNKS
    copies = load_slots(slots_any, dests_any, slot_ref, dest_ref, sems)
    widen_sources(x_ref, xf)
    for copy in copies:
        copy.wait()
    for g in range(groups):
        rows = [xf[slot_ref[g * group + i]] for i in range(group)]
        picked[g] = jnp.concatenate(rows, axis=0).astype(jnp.bfloat16)
    owner = lax.broadcasted_iota(jnp.int32, (nvec, leaf), 1) // rank
    total = None
    for c in range(CHUNKS):
        for g in range(c * per, (c + 1) * per):
            u = u_ref[g * group : (g + 1) * group].reshape(leaf, leaf)
            kept = project(picked[g], u, owner, nvec, group)
            dest = jnp.full((nvec, leaf), dest_ref[g * group], jnp.int32)
            for i in range(1, group):
                dest = jnp.where(owner == i, dest_ref[g * group + i], dest)
            dest = dest.astype(jnp.float32)
            kept = jnp.concatenate([kept, kept], axis=0).astype(jnp.bfloat16)
            dest = jnp.concatenate([dest, dest - 1.0], axis=0).astype(jnp.bfloat16)
            for o in range(0, slots, 2):
                wide[o * nvec : (o + 2) * nvec, g * leaf : (g + 1) * leaf] = jnp.where(
                    dest == jnp.bfloat16(o), kept, jnp.bfloat16(0)
                )
        v = v_ref[c * per * group : (c + 1) * per * group].reshape(per * leaf, leaf)
        part = jnp.dot(
            wide[:, c * per * leaf : (c + 1) * per * leaf], v, preferred_element_type=jnp.float32
        )
        total = part if total is None else total + part
    out_ref[...] = total.reshape(out_ref.shape).astype(out_ref.dtype)


def far_many_kernel(
    slots_any, dests_any, x_ref, u_ref, v_ref, out_ref, slot_ref, dest_ref, sems, xf, coef, acc
):
    slots, nvec, leaf = xf.shape
    blocks, rank, _ = u_ref.shape
    group = leaf // rank
    copies = load_slots(slots_any, dests_any, slot_ref, dest_ref, sems)
    widen_sources(x_ref, xf)
    for copy in copies:
        copy.wait()
    acc[...] = jnp.zeros_like(acc)
    owner = lax.broadcasted_iota(jnp.int32, (nvec, leaf), 1) // rank

    def forward(g, carry):
        rows = [xf[slot_ref[g * group + i]] for i in range(group)]
        picked = jnp.concatenate(rows, axis=0).astype(jnp.bfloat16)
        u = u_ref[pl.ds(g * group, group)].reshape(leaf, leaf)
        coef[g] = project(picked, u, owner, nvec, group)
        return carry

    def backward(g, carry):
        kept = coef[g]
        spread = jnp.concatenate(
            [jnp.where(owner == i, kept, 0.0) for i in range(group)], axis=0
        ).astype(jnp.bfloat16)
        v = v_ref[pl.ds(g * group, group)].reshape(leaf, leaf)
        terms = jnp.dot(spread, v, preferred_element_type=jnp.float32)
        for i in range(group):
            acc[dest_ref[g * group + i]] += terms[i * nvec : (i + 1) * nvec]
        return carry

    lax.fori_loop(0, blocks // group, forward, 0, unroll=4)
    lax.fori_loop(0, blocks // group, backward, 0, unroll=4)
    out_ref[...] = acc[...].reshape(out_ref.shape).astype(out_ref.dtype)


def sum_kernel(back_ref, src_ref, near_ref, x_ref, pattern_ref, out_ref, place):
    clusters, nvec, leaf = src_ref.shape
    peers, back_rows, _ = back_ref.shape
    cap = back_rows // nvec
    width = leaf // 2
    cluster = pattern_ref[...]

    def step(p, carry):
        meta = x_ref[p, 2 * (cap + 1) * nvec :, :].astype(jnp.float32)
        for k in range(cap):
            at = jnp.broadcast_to(meta[k * nvec // cap : k * nvec // cap + 1], (nvec, width))
            place[pl.ds((p * cap + k) * nvec, nvec)] = jnp.where(at == cluster, 1.0, 0.0)
        return carry

    lax.fori_loop(0, peers, step, 0, unroll=min(peers, 16))
    spread = place[...].T[: clusters * nvec].astype(jnp.bfloat16)
    terms = back_ref[...].reshape(peers * back_rows, leaf)
    far_part = jnp.dot(spread, terms, preferred_element_type=jnp.float32)

    me = lax.axis_index("clus")
    edge = slice(2 * cap * nvec, 2 * (cap + 1) * nvec)
    before = joined(x_ref[jnp.maximum(me - 1, 0)][edge].astype(jnp.float32), nvec)
    after = joined(x_ref[jnp.minimum(me + 1, peers - 1)][edge].astype(jnp.float32), nvec)
    before = jnp.where(me > 0, before, 0.0).astype(jnp.bfloat16)
    after = jnp.where(me < peers - 1, after, 0.0).astype(jnp.bfloat16)
    rows = [before] + [src_ref[s] for s in range(clusters)] + [after]
    for s in range(clusters):
        total = jnp.dot(
            jnp.concatenate(rows[s : s + 3], axis=1),
            near_ref[s].reshape(3 * leaf, leaf),
            preferred_element_type=jnp.float32,
        )
        out_ref[s] = far_part[s * nvec : (s + 1) * nvec] + total


def cost(flops, moved):
    return pl.CostEstimate(flops=flops, bytes_accessed=moved, transcendentals=0)


def body(sources, near_blocks, far_u, far_v, send_list, far_slot, ret_list, ret_slot):
    clusters, nvec, leaf = sources.shape
    _, peers, cap = send_list.shape
    blocks, rank, _ = far_u.shape
    slots = peers * cap
    rows = 2 * (cap + 1) * nvec + nvec
    params = pltpu.CompilerParams(vmem_limit_bytes=8 * 2**20)
    pattern = pl.pallas_call(
        pattern_kernel,
        out_shape=jax.ShapeDtypeStruct((nvec, leaf // 2), jnp.float32),
        out_specs=VMEM,
        compiler_params=params,
        cost_estimate=cost(10**10, nvec * leaf * 2),
        name="pattern",
    )()
    message = pl.pallas_call(
        pack_kernel,
        out_shape=jax.ShapeDtypeStruct((peers, rows, leaf // 2), jnp.bfloat16),
        in_specs=[VMEM] * 4,
        out_specs=VMEM,
        compiler_params=params,
        cost_estimate=cost(10**10, peers * rows * leaf),
        name="pack",
    )(send_list[0].T, ret_list[0].T, sources, pattern)
    incoming = lax.all_to_all(message, "clus", split_axis=0, concat_axis=0, tiled=True)
    few = slots <= 32
    if few:
        scratch = [
            pltpu.VMEM((blocks * rank // leaf, leaf // rank * nvec, leaf), jnp.bfloat16),
            pltpu.VMEM((slots * nvec, blocks * rank), jnp.bfloat16),
        ]
    else:
        scratch = [
            pltpu.VMEM((blocks * rank // leaf, nvec, leaf), jnp.float32),
            pltpu.VMEM((slots, nvec, leaf), jnp.float32),
        ]
    returns = pl.pallas_call(
        far_kernel if few else far_many_kernel,
        out_shape=jax.ShapeDtypeStruct((peers, cap * nvec, leaf), jnp.bfloat16),
        in_specs=[ANY, ANY, VMEM, VMEM, VMEM],
        out_specs=VMEM,
        scratch_shapes=[
            pltpu.SMEM((blocks,), jnp.int32),
            pltpu.SMEM((blocks,), jnp.int32),
            pltpu.SemaphoreType.DMA((2,)),
            pltpu.VMEM((slots, nvec, leaf), jnp.float32),
        ]
        + scratch,
        compiler_params=pltpu.CompilerParams(vmem_limit_bytes=16 * 2**20),
        cost_estimate=cost(4 * blocks * 8 * nvec * leaf * rank, 4 * blocks * rank * leaf),
        name="far",
    )(far_slot, ret_slot, incoming, far_u, far_v)
    back = lax.all_to_all(returns, "clus", split_axis=0, concat_axis=0, tiled=True)
    return pl.pallas_call(
        sum_kernel,
        out_shape=jax.ShapeDtypeStruct((clusters, nvec, leaf), jnp.float32),
        in_specs=[VMEM] * 5,
        out_specs=VMEM,
        scratch_shapes=[pltpu.VMEM((slots * nvec, leaf // 2), jnp.float32)],
        compiler_params=params,
        cost_estimate=cost(2 * 3 * clusters * nvec * leaf * leaf, 6 * clusters * leaf * leaf),
        name="sum",
    )(back, sources, near_blocks, incoming, pattern)


def solution(mesh):
    placed = (
        P(("groups", "clus"), None, None),
        P(("groups", "clus"), None, None, None),
        P(("groups", "clus"), None, None),
        P(("groups", "clus"), None, None),
        P(("groups", "clus"), None, None),
        P(("groups", "clus")),
        P(("groups", "clus"), None, None),
        P(("groups", "clus")),
    )
    return jax.shard_map(
        body,
        mesh=mesh,
        in_specs=placed,
        out_specs=P(("groups", "clus"), None, None),
        check_vma=False,
    )
```

```python
import jax
import jax.numpy as jnp
from jax import lax
from jax.experimental import pallas as pl
from jax.experimental.pallas import tpu as pltpu
from jax.sharding import PartitionSpec as P

VMEM = pl.BlockSpec(memory_space=pltpu.VMEM)
ANY = pl.BlockSpec(memory_space=pl.ANY)
CHUNKS = 8


def halves(x):
    w = x.shape[1] // 2
    return [x[:, :w], x[:, w:]]


def pattern_kernel(out_ref):
    nvec, width = out_ref.shape
    lane = lax.broadcasted_iota(jnp.int32, (nvec, width), 1)
    sub = lax.broadcasted_iota(jnp.int32, (nvec, width), 0)
    out_ref[...] = jnp.where(lane % nvec == sub, lane // nvec, -2).astype(jnp.float32)


def pack_kernel(send_ref, ret_ref, src_ref, pattern_ref, out_ref):
    clusters, nvec, leaf = src_ref.shape
    cap, peers = send_ref.shape
    me = lax.axis_index("clus")
    rows = peers * nvec
    repeat = lax.broadcasted_iota(jnp.int32, (rows, peers), 0) // nvec
    repeat = (repeat == lax.broadcasted_iota(jnp.int32, (rows, peers), 1)).astype(jnp.bfloat16)

    def columns(list_ref):
        entries = list_ref[...].astype(jnp.float32).astype(jnp.bfloat16)
        return lax.dot_general(
            repeat, entries, (((1,), (1,)), ((), ())), preferred_element_type=jnp.float32
        )

    send = jnp.maximum(columns(send_ref), 0.0)
    ret = columns(ret_ref)
    row = lax.broadcasted_iota(jnp.int32, (rows, clusters * nvec), 0)
    lane = lax.broadcasted_iota(jnp.int32, (rows, clusters * nvec), 1)
    cluster = jnp.where(row % nvec == lane % nvec, lane // nvec, -2).astype(jnp.float32)
    source = src_ref[...].reshape(clusters * nvec, leaf)
    picked = []
    for k in range(cap):
        pick = jnp.where(send[:, k : k + 1] == cluster, 1.0, 0.0).astype(jnp.bfloat16)
        picked.append(jnp.dot(pick, source, preferred_element_type=jnp.float32))
    vector = lax.broadcasted_iota(jnp.int32, (rows, leaf // 2), 0) % nvec
    places = jnp.broadcast_to(ret[:, :1], (rows, leaf // 2))
    for k in range(1, cap):
        places = jnp.where(vector >= k * nvec // cap, ret[:, k : k + 1], places)
    first = src_ref[0].astype(jnp.float32)
    last = src_ref[clusters - 1].astype(jnp.float32)
    for p in range(peers):
        at = slice(p * nvec, (p + 1) * nvec)
        parts = []
        for k in range(cap):
            parts += halves(picked[k][at])
        parts += halves(jnp.where(p > me, last, first))
        parts.append(places[at])
        out_ref[p] = jnp.concatenate(parts, axis=0).astype(out_ref.dtype)


def joined(rows, nvec):
    return jnp.concatenate([rows[:nvec], rows[nvec:]], axis=1)


def load_slots(slots_any, dests_any, slot_ref, dest_ref, sems):
    copies = [
        pltpu.make_async_copy(slots_any, slot_ref, sems.at[0]),
        pltpu.make_async_copy(dests_any, dest_ref, sems.at[1]),
    ]
    for copy in copies:
        copy.start()
    return copies


def near_product(src_ref, near_ref, x_ref, near_out):
    clusters, nvec, leaf = src_ref.shape
    peers, rows, _ = x_ref.shape
    me = lax.axis_index("clus")
    edge = slice(rows - 3 * nvec, rows - nvec)
    before = joined(x_ref[jnp.maximum(me - 1, 0)][edge].astype(jnp.float32), nvec)
    after = joined(x_ref[jnp.minimum(me + 1, peers - 1)][edge].astype(jnp.float32), nvec)
    before = jnp.where(me > 0, before, 0.0).astype(jnp.bfloat16)
    after = jnp.where(me < peers - 1, after, 0.0).astype(jnp.bfloat16)
    sources = [before] + [src_ref[s] for s in range(clusters)] + [after]
    for s in range(clusters):
        near_out[s * nvec : (s + 1) * nvec] = jnp.dot(
            jnp.concatenate(sources[s : s + 3], axis=1),
            near_ref[s].reshape(3 * leaf, leaf),
            preferred_element_type=jnp.float32,
        )


def placement(x_ref, pattern_ref, place, place_out):
    nvec, width = pattern_ref.shape
    peers, rows, _ = x_ref.shape
    cap = place.shape[0] // (peers * nvec)
    cluster = pattern_ref[...]

    def step(p, carry):
        meta = x_ref[p, rows - nvec :, :].astype(jnp.float32)
        for k in range(cap):
            at = jnp.broadcast_to(meta[k * nvec // cap : k * nvec // cap + 1], (nvec, width))
            place[pl.ds((p * cap + k) * nvec, nvec)] = jnp.where(at == cluster, 1.0, 0.0)
        return carry

    lax.fori_loop(0, peers, step, 0, unroll=min(peers, 16))
    place_out[...] = place[...].T[: place_out.shape[0]].astype(jnp.bfloat16)


def widen_sources(x_ref, xf):
    peers = x_ref.shape[0]
    slots, nvec, _ = xf.shape
    cap = slots // peers

    def widen(p, carry):
        rows = x_ref[p].astype(jnp.float32)
        for k in range(cap):
            xf[p * cap + k] = joined(rows[2 * k * nvec : 2 * (k + 1) * nvec], nvec)
        return carry

    lax.fori_loop(0, peers, widen, 0, unroll=min(peers, 16))


def project(picked, u, owner, nvec, group):
    full = lax.dot_general(picked, u, (((1,), (1,)), ((), ())), preferred_element_type=jnp.float32)
    kept = full[:nvec]
    for i in range(1, group):
        kept = jnp.where(owner == i, full[i * nvec : (i + 1) * nvec], kept)
    return kept


def far_kernel(
    slots_any,
    dests_any,
    x_ref,
    u_ref,
    v_ref,
    src_ref,
    near_ref,
    pattern_ref,
    out_ref,
    near_out,
    place_out,
    slot_ref,
    dest_ref,
    sems,
    place,
    xf,
    picked, wide,
):
    peers = x_ref.shape[0]
    slots, nvec, leaf = xf.shape
    blocks, rank, _ = u_ref.shape
    group = leaf // rank
    groups = blocks // group
    per = groups // CHUNKS
    copies = load_slots(slots_any, dests_any, slot_ref, dest_ref, sems)
    widen_sources(x_ref, xf)
    near_product(src_ref, near_ref, x_ref, near_out)
    placement(x_ref, pattern_ref, place, place_out)
    for copy in copies:
        copy.wait()
    for g in range(groups):
        rows = [xf[slot_ref[g * group + i]] for i in range(group)]
        picked[g] = jnp.concatenate(rows, axis=0).astype(jnp.bfloat16)
    owner = lax.broadcasted_iota(jnp.int32, (nvec, leaf), 1) // rank
    total = None
    for c in range(CHUNKS):
        for g in range(c * per, (c + 1) * per):
            u = u_ref[g * group : (g + 1) * group].reshape(leaf, leaf)
            kept = project(picked[g], u, owner, nvec, group)
            dest = jnp.full((nvec, leaf), dest_ref[g * group], jnp.int32)
            for i in range(1, group):
                dest = jnp.where(owner == i, dest_ref[g * group + i], dest)
            dest = dest.astype(jnp.float32)
            kept = jnp.concatenate([kept, kept], axis=0).astype(jnp.bfloat16)
            dest = jnp.concatenate([dest, dest - 1.0], axis=0).astype(jnp.bfloat16)
            for o in range(0, slots, 2):
                wide[o * nvec : (o + 2) * nvec, g * leaf : (g + 1) * leaf] = jnp.where(
                    dest == jnp.bfloat16(o), kept, jnp.bfloat16(0)
                )
        v = v_ref[c * per * group : (c + 1) * per * group].reshape(per * leaf, leaf)
        part = jnp.dot(
            wide[:, c * per * leaf : (c + 1) * per * leaf], v, preferred_element_type=jnp.float32
        )
        total = part if total is None else total + part
    out_ref[...] = total.reshape(out_ref.shape).astype(out_ref.dtype)


def far_many_kernel(
    slots_any,
    dests_any,
    x_ref,
    u_ref,
    v_ref,
    src_ref,
    near_ref,
    pattern_ref,
    out_ref,
    near_out,
    place_out,
    slot_ref,
    dest_ref,
    sems,
    place,
    xf,
    coef, acc,
):
    slots, nvec, leaf = xf.shape
    blocks, rank, _ = u_ref.shape
    group = leaf // rank
    copies = load_slots(slots_any, dests_any, slot_ref, dest_ref, sems)
    widen_sources(x_ref, xf)
    near_product(src_ref, near_ref, x_ref, near_out)
    placement(x_ref, pattern_ref, place, place_out)
    for copy in copies:
        copy.wait()
    acc[...] = jnp.zeros_like(acc)
    owner = lax.broadcasted_iota(jnp.int32, (nvec, leaf), 1) // rank

    def forward(g, carry):
        rows = [xf[slot_ref[g * group + i]] for i in range(group)]
        picked = jnp.concatenate(rows, axis=0).astype(jnp.bfloat16)
        u = u_ref[pl.ds(g * group, group)].reshape(leaf, leaf)
        coef[g] = project(picked, u, owner, nvec, group)
        return carry

    def backward(g, carry):
        kept = coef[g]
        spread = jnp.concatenate(
            [jnp.where(owner == i, kept, 0.0) for i in range(group)], axis=0
        ).astype(jnp.bfloat16)
        v = v_ref[pl.ds(g * group, group)].reshape(leaf, leaf)
        terms = jnp.dot(spread, v, preferred_element_type=jnp.float32)
        for i in range(group):
            acc[dest_ref[g * group + i]] += terms[i * nvec : (i + 1) * nvec]
        return carry

    lax.fori_loop(0, blocks // group, forward, 0, unroll=4)
    lax.fori_loop(0, blocks // group, backward, 0, unroll=4)
    out_ref[...] = acc[...].reshape(out_ref.shape).astype(out_ref.dtype)


def sum_kernel(back_ref, near_ref, place_ref, out_ref):
    peers, rows, leaf = back_ref.shape
    terms = back_ref[...].reshape(peers * rows, leaf)
    total = near_ref[...] + jnp.dot(place_ref[...], terms, preferred_element_type=jnp.float32)
    out_ref[...] = total.reshape(out_ref.shape)


def cost(flops, moved):
    return pl.CostEstimate(flops=flops, bytes_accessed=moved, transcendentals=0)


def body(sources, near_blocks, far_u, far_v, send_list, far_slot, ret_list, ret_slot):
    clusters, nvec, leaf = sources.shape
    _, peers, cap = send_list.shape
    blocks, rank, _ = far_u.shape
    slots = peers * cap
    rows = 2 * (cap + 1) * nvec + nvec
    params = pltpu.CompilerParams(vmem_limit_bytes=8 * 2**20)
    pattern = pl.pallas_call(
        pattern_kernel,
        out_shape=jax.ShapeDtypeStruct((nvec, leaf // 2), jnp.float32),
        out_specs=VMEM,
        compiler_params=params,
        cost_estimate=cost(10**10, nvec * leaf * 2),
        name="pattern",
    )()
    message = pl.pallas_call(
        pack_kernel,
        out_shape=jax.ShapeDtypeStruct((peers, rows, leaf // 2), jnp.bfloat16),
        in_specs=[VMEM] * 4,
        out_specs=VMEM,
        compiler_params=params,
        cost_estimate=cost(10**10, peers * rows * leaf),
        name="pack",
    )(send_list[0].T, ret_list[0].T, sources, pattern)
    incoming = lax.all_to_all(message, "clus", split_axis=0, concat_axis=0, tiled=True)
    few = slots <= 32
    if few:
        scratch = [
            pltpu.VMEM((blocks * rank // leaf, leaf // rank * nvec, leaf), jnp.bfloat16),
            pltpu.VMEM((slots * nvec, blocks * rank), jnp.bfloat16),
        ]
    else:
        scratch = [
            pltpu.VMEM((blocks * rank // leaf, nvec, leaf), jnp.float32),
            pltpu.VMEM((slots, nvec, leaf), jnp.float32),
        ]
    returns, near_part, place = pl.pallas_call(
        far_kernel if few else far_many_kernel,
        out_shape=(
            jax.ShapeDtypeStruct((peers, cap * nvec, leaf), jnp.bfloat16),
            jax.ShapeDtypeStruct((clusters * nvec, leaf), jnp.float32),
            jax.ShapeDtypeStruct((clusters * nvec, slots * nvec), jnp.bfloat16),
        ),
        in_specs=[ANY, ANY] + [VMEM] * 6,
        out_specs=(VMEM, VMEM, VMEM),
        scratch_shapes=[
            pltpu.SMEM((blocks,), jnp.int32),
            pltpu.SMEM((blocks,), jnp.int32),
            pltpu.SemaphoreType.DMA((2,)),
            pltpu.VMEM((slots * nvec, leaf // 2), jnp.float32),
            pltpu.VMEM((slots, nvec, leaf), jnp.float32),
        ]
        + scratch,
        compiler_params=pltpu.CompilerParams(vmem_limit_bytes=16 * 2**20),
        cost_estimate=cost(4 * blocks * 8 * nvec * leaf * rank, 4 * blocks * rank * leaf),
        name="far",
    )(far_slot, ret_slot, incoming, far_u, far_v, sources, near_blocks, pattern)
    back = lax.all_to_all(returns, "clus", split_axis=0, concat_axis=0, tiled=True)
    return pl.pallas_call(
        sum_kernel,
        out_shape=jax.ShapeDtypeStruct((clusters, nvec, leaf), jnp.float32),
        in_specs=[VMEM] * 3,
        out_specs=VMEM,
        compiler_params=params,
        cost_estimate=cost(2 * clusters * nvec * slots * nvec * leaf, slots * nvec * leaf * 2),
        name="sum",
    )(back, near_part, place)


def solution(mesh):
    placed = (
        P(("groups", "clus"), None, None),
        P(("groups", "clus"), None, None, None),
        P(("groups", "clus"), None, None),
        P(("groups", "clus"), None, None),
        P(("groups", "clus"), None, None),
        P(("groups", "clus")),
        P(("groups", "clus"), None, None),
        P(("groups", "clus")),
    )
    return jax.shard_map(
        body,
        mesh=mesh,
        in_specs=placed,
        out_specs=P(("groups", "clus"), None, None),
        check_vma=False,
    )
```

```python
import jax
import jax.numpy as jnp
from jax import lax
from jax.experimental import pallas as pl
from jax.experimental.pallas import tpu as pltpu
from jax.sharding import PartitionSpec as P

VMEM = pl.BlockSpec(memory_space=pltpu.VMEM)
ANY = pl.BlockSpec(memory_space=pl.ANY)
CHUNKS = 8


def halves(x):
    w = x.shape[1] // 2
    return [x[:, :w], x[:, w:]]


def pattern_kernel(out_ref):
    nvec, width = out_ref.shape
    lane = lax.broadcasted_iota(jnp.int32, (nvec, width), 1)
    sub = lax.broadcasted_iota(jnp.int32, (nvec, width), 0)
    out_ref[...] = jnp.where(lane % nvec == sub, lane // nvec, -2).astype(jnp.float32)


def pack_kernel(send_ref, ret_ref, src_ref, pattern_ref, out_ref):
    clusters, nvec, leaf = src_ref.shape
    cap, peers = send_ref.shape
    me = lax.axis_index("clus")
    rows = peers * nvec
    peer = lax.broadcasted_iota(jnp.int32, (rows, peers), 0) // nvec
    kind = lax.broadcasted_iota(jnp.int32, (rows, peers), 0) % nvec // cap
    column = lax.broadcasted_iota(jnp.int32, (rows, peers), 1)

    def entries_at(list_ref, which):
        entries = list_ref[...].astype(jnp.float32).astype(jnp.bfloat16)
        return lax.dot_general(
            jnp.where(which == column, 1.0, 0.0).astype(jnp.bfloat16),
            entries,
            (((1,), (1,)), ((), ())),
            preferred_element_type=jnp.float32,
        )

    send = jnp.maximum(entries_at(send_ref, peer), 0.0)
    ret = entries_at(ret_ref, jnp.where(kind == 1, me - 1, jnp.where(kind == 2, me + 1, peer)))
    row = lax.broadcasted_iota(jnp.int32, (rows, clusters * nvec), 0)
    lane = lax.broadcasted_iota(jnp.int32, (rows, clusters * nvec), 1)
    cluster = jnp.where(row % nvec == lane % nvec, lane // nvec, -2).astype(jnp.float32)
    source = src_ref[...].reshape(clusters * nvec, leaf)
    picked = []
    for k in range(cap):
        pick = jnp.where(send[:, k : k + 1] == cluster, 1.0, 0.0).astype(jnp.bfloat16)
        picked.append(jnp.dot(pick, source, preferred_element_type=jnp.float32))
    vector = lax.broadcasted_iota(jnp.int32, (rows, leaf // 2), 0) % nvec
    places = jnp.broadcast_to(ret[:, :1], (rows, leaf // 2))
    for k in range(1, cap):
        places = jnp.where(vector % cap == k, ret[:, k : k + 1], places)
    first = src_ref[0].astype(jnp.float32)
    last = src_ref[clusters - 1].astype(jnp.float32)
    for p in range(peers):
        at = slice(p * nvec, (p + 1) * nvec)
        parts = []
        for k in range(cap):
            parts += halves(picked[k][at])
        edge = halves(jnp.where(p > me, last, first))[0]
        parts.append(jnp.where(jnp.abs(p - me) == 1, edge, places[at]))
        out_ref[p] = jnp.concatenate(parts, axis=0).astype(out_ref.dtype)


def joined(rows, nvec):
    return jnp.concatenate([rows[:nvec], rows[nvec:]], axis=1)


def load_slots(slots_any, dests_any, slot_ref, dest_ref, sems):
    copies = [
        pltpu.make_async_copy(slots_any, slot_ref, sems.at[0]),
        pltpu.make_async_copy(dests_any, dest_ref, sems.at[1]),
    ]
    for copy in copies:
        copy.start()
    return copies


def near_product(src_ref, near_ref, x_ref, near_out):
    clusters, nvec, leaf = src_ref.shape
    peers, rows, _ = x_ref.shape
    me = lax.axis_index("clus")
    before = x_ref[jnp.maximum(me - 1, 0)][rows - nvec :].astype(jnp.float32)
    after = x_ref[jnp.minimum(me + 1, peers - 1)][rows - nvec :].astype(jnp.float32)
    before = jnp.where(me > 0, before, 0.0)
    after = jnp.where(me < peers - 1, after, 0.0)
    before, after = [
        jnp.concatenate([x, jnp.zeros_like(x)], axis=1).astype(jnp.bfloat16)
        for x in (before, after)
    ]
    sources = [before] + [src_ref[s] for s in range(clusters)] + [after]
    for s in range(clusters):
        near_out[s * nvec : (s + 1) * nvec] = jnp.dot(
            jnp.concatenate(sources[s : s + 3], axis=1),
            near_ref[s].reshape(3 * leaf, leaf),
            preferred_element_type=jnp.float32,
        )


def placement(x_ref, pattern_ref, place, place_out):
    nvec, width = pattern_ref.shape
    peers, rows, _ = x_ref.shape
    cap = place.shape[0] // (peers * nvec)
    cluster = pattern_ref[...]
    me = lax.axis_index("clus")

    def step(p, carry):
        tile = x_ref[p, rows - nvec :, :].astype(jnp.float32)
        tile = jnp.where(jnp.abs(p - me) == 1, -1.0, tile)
        for k in range(cap):
            at = jnp.broadcast_to(tile[k : k + 1], (nvec, width))
            place[pl.ds((p * cap + k) * nvec, nvec)] = jnp.where(at == cluster, 1.0, 0.0)
        return carry

    lax.fori_loop(0, peers, step, 0, unroll=min(peers, 16))
    place_out[...] = place[...].T[: place_out.shape[0]].astype(jnp.bfloat16)


def widen_sources(x_ref, xf):
    peers = x_ref.shape[0]
    slots, nvec, _ = xf.shape
    cap = slots // peers

    def widen(p, carry):
        rows = x_ref[p].astype(jnp.float32)
        for k in range(cap):
            xf[p * cap + k] = joined(rows[2 * k * nvec : 2 * (k + 1) * nvec], nvec)
        return carry

    lax.fori_loop(0, peers, widen, 0, unroll=min(peers, 16))


def project(picked, u, owner, nvec, group):
    full = lax.dot_general(picked, u, (((1,), (1,)), ((), ())), preferred_element_type=jnp.float32)
    kept = full[:nvec]
    for i in range(1, group):
        kept = jnp.where(owner == i, full[i * nvec : (i + 1) * nvec], kept)
    return kept


def put_returns(total, x_ref, src_ref, out_ref):
    peers, rows, width = x_ref.shape
    clusters, nvec, _ = src_ref.shape
    each = total.shape[0] // peers
    cap = each // nvec
    me = lax.axis_index("clus")
    first = halves(src_ref[0].astype(jnp.float32))[1]
    last = halves(src_ref[clusters - 1].astype(jnp.float32))[1]
    sub = lax.broadcasted_iota(jnp.int32, (nvec, width), 0)
    for p in range(peers):
        before = x_ref[max(p - 1, 0), rows - nvec :, :].astype(jnp.float32)
        after = x_ref[min(p + 1, peers - 1), rows - nvec :, :].astype(jnp.float32)
        handed = jnp.where(sub // cap == 2, before, after)
        edge = jnp.where(p > me, last, first)
        parts = halves(total[p * each : (p + 1) * each])
        parts.append(jnp.where(jnp.abs(p - me) == 1, edge, handed))
        out_ref[p] = jnp.concatenate(parts, axis=0).astype(out_ref.dtype)


def far_kernel(
    slots_any,
    dests_any,
    x_ref,
    u_ref,
    v_ref,
    src_ref,
    near_ref,
    pattern_ref,
    out_ref,
    near_out,
    place_out,
    slot_ref,
    dest_ref,
    sems,
    place,
    xf,
    picked, wide,
):
    peers = x_ref.shape[0]
    slots, nvec, leaf = xf.shape
    blocks, rank, _ = u_ref.shape
    group = leaf // rank
    groups = blocks // group
    per = groups // CHUNKS
    copies = load_slots(slots_any, dests_any, slot_ref, dest_ref, sems)
    widen_sources(x_ref, xf)
    near_product(src_ref, near_ref, x_ref, near_out)
    placement(x_ref, pattern_ref, place, place_out)
    for copy in copies:
        copy.wait()
    for g in range(groups):
        rows = [xf[slot_ref[g * group + i]] for i in range(group)]
        picked[g] = jnp.concatenate(rows, axis=0).astype(jnp.bfloat16)
    owner = lax.broadcasted_iota(jnp.int32, (nvec, leaf), 1) // rank
    total = None
    for c in range(CHUNKS):
        for g in range(c * per, (c + 1) * per):
            u = u_ref[g * group : (g + 1) * group].reshape(leaf, leaf)
            kept = project(picked[g], u, owner, nvec, group)
            dest = jnp.full((nvec, leaf), dest_ref[g * group], jnp.int32)
            for i in range(1, group):
                dest = jnp.where(owner == i, dest_ref[g * group + i], dest)
            dest = dest.astype(jnp.float32)
            kept = jnp.concatenate([kept, kept], axis=0).astype(jnp.bfloat16)
            dest = jnp.concatenate([dest, dest - 1.0], axis=0).astype(jnp.bfloat16)
            for o in range(0, slots, 2):
                wide[o * nvec : (o + 2) * nvec, g * leaf : (g + 1) * leaf] = jnp.where(
                    dest == jnp.bfloat16(o), kept, jnp.bfloat16(0)
                )
        v = v_ref[c * per * group : (c + 1) * per * group].reshape(per * leaf, leaf)
        part = jnp.dot(
            wide[:, c * per * leaf : (c + 1) * per * leaf], v, preferred_element_type=jnp.float32
        )
        total = part if total is None else total + part
    put_returns(total, x_ref, src_ref, out_ref)


def far_many_kernel(
    slots_any,
    dests_any,
    x_ref,
    u_ref,
    v_ref,
    src_ref,
    near_ref,
    pattern_ref,
    out_ref,
    near_out,
    place_out,
    slot_ref,
    dest_ref,
    sems,
    place,
    xf,
    coef, acc,
):
    slots, nvec, leaf = xf.shape
    blocks, rank, _ = u_ref.shape
    group = leaf // rank
    copies = load_slots(slots_any, dests_any, slot_ref, dest_ref, sems)
    widen_sources(x_ref, xf)
    near_product(src_ref, near_ref, x_ref, near_out)
    placement(x_ref, pattern_ref, place, place_out)
    for copy in copies:
        copy.wait()
    acc[...] = jnp.zeros_like(acc)
    owner = lax.broadcasted_iota(jnp.int32, (nvec, leaf), 1) // rank

    def forward(g, carry):
        rows = [xf[slot_ref[g * group + i]] for i in range(group)]
        picked = jnp.concatenate(rows, axis=0).astype(jnp.bfloat16)
        u = u_ref[pl.ds(g * group, group)].reshape(leaf, leaf)
        coef[g] = project(picked, u, owner, nvec, group)
        return carry

    def backward(g, carry):
        kept = coef[g]
        spread = jnp.concatenate(
            [jnp.where(owner == i, kept, 0.0) for i in range(group)], axis=0
        ).astype(jnp.bfloat16)
        v = v_ref[pl.ds(g * group, group)].reshape(leaf, leaf)
        terms = jnp.dot(spread, v, preferred_element_type=jnp.float32)
        for i in range(group):
            acc[dest_ref[g * group + i]] += terms[i * nvec : (i + 1) * nvec]
        return carry

    lax.fori_loop(0, blocks // group, forward, 0, unroll=4)
    lax.fori_loop(0, blocks // group, backward, 0, unroll=4)
    put_returns(acc[...].reshape(slots * nvec, leaf), x_ref, src_ref, out_ref)


def sum_kernel(back_ref, near_out_ref, place_ref, near_ref, out_ref):
    peers, rows, width = back_ref.shape
    clusters, nvec, leaf = out_ref.shape
    each = (rows - nvec) // 2
    cap = each // nvec
    me = lax.axis_index("clus")
    terms = jnp.concatenate(
        [back_ref[:, i * each : (i + 1) * each, :].reshape(peers * each, width) for i in range(2)],
        axis=1,
    )
    total = near_out_ref[...] + jnp.dot(
        place_ref[...], terms, preferred_element_type=jnp.float32
    )

    relay = jnp.where(me + 3 < peers, me + 3, me - 3)
    tile = back_ref[relay][rows - nvec :].astype(jnp.float32)
    before = back_ref[jnp.maximum(me - 1, 0)].astype(jnp.float32)
    after = back_ref[jnp.minimum(me + 1, peers - 1)].astype(jnp.float32)
    row = lax.broadcasted_iota(jnp.int32, (clusters * nvec, width), 0)
    lane = lax.broadcasted_iota(jnp.int32, (clusters * nvec, width), 1)
    named = jnp.full((1, width), -1.0, jnp.float32)
    for i in range(2 * cap):
        k, alive = (i + 2 * cap, me > 0) if i < cap else (i, me < peers - 1)
        entry = jnp.where(alive, tile[k : k + 1], -1.0)
        named = jnp.where(lane[:1] // nvec == i, entry, named)
    match = (named == (row // nvec).astype(jnp.float32)) & (lane % nvec == row % nvec)
    match = jnp.where(match, 1.0, 0.0)[:, : 2 * each].astype(jnp.bfloat16)
    sides = jnp.concatenate(
        [
            jnp.concatenate([side[:each], side[each : 2 * each]], axis=1)
            for side in (before, after)
        ],
        axis=0,
    ).astype(jnp.bfloat16)
    total += jnp.dot(match, sides, preferred_element_type=jnp.float32)

    edges = []
    for side, alive, at in ((before, me > 0, (0, 0)), (after, me < peers - 1, (clusters - 1, 2))):
        edge = jnp.where(alive, side[2 * each :], 0.0).astype(jnp.bfloat16)
        edges.append(
            jnp.dot(edge, near_ref[at[0], at[1], width:, :], preferred_element_type=jnp.float32)
        )
    for s in range(clusters):
        part = total[s * nvec : (s + 1) * nvec]
        if s == 0:
            part += edges[0]
        if s == clusters - 1:
            part += edges[1]
        out_ref[s] = part


def cost(flops, moved):
    return pl.CostEstimate(flops=flops, bytes_accessed=moved, transcendentals=0)


def body(sources, near_blocks, far_u, far_v, send_list, far_slot, ret_list, ret_slot):
    clusters, nvec, leaf = sources.shape
    _, peers, cap = send_list.shape
    blocks, rank, _ = far_u.shape
    slots = peers * cap
    rows = 2 * cap * nvec + nvec
    params = pltpu.CompilerParams(vmem_limit_bytes=8 * 2**20)
    pattern = pl.pallas_call(
        pattern_kernel,
        out_shape=jax.ShapeDtypeStruct((nvec, leaf // 2), jnp.float32),
        out_specs=VMEM,
        compiler_params=params,
        cost_estimate=cost(10**10, nvec * leaf * 2),
        name="pattern",
    )()
    message = pl.pallas_call(
        pack_kernel,
        out_shape=jax.ShapeDtypeStruct((peers, rows, leaf // 2), jnp.bfloat16),
        in_specs=[VMEM] * 4,
        out_specs=VMEM,
        compiler_params=params,
        cost_estimate=cost(10**10, peers * rows * leaf),
        name="pack",
    )(send_list[0].T, ret_list[0].T, sources, pattern)
    incoming = lax.all_to_all(message, "clus", split_axis=0, concat_axis=0, tiled=True)
    few = slots <= 32
    if few:
        scratch = [
            pltpu.VMEM((blocks * rank // leaf, leaf // rank * nvec, leaf), jnp.bfloat16),
            pltpu.VMEM((slots * nvec, blocks * rank), jnp.bfloat16),
        ]
    else:
        scratch = [
            pltpu.VMEM((blocks * rank // leaf, nvec, leaf), jnp.float32),
            pltpu.VMEM((slots, nvec, leaf), jnp.float32),
        ]
    returns, near_part, place = pl.pallas_call(
        far_kernel if few else far_many_kernel,
        out_shape=(
            jax.ShapeDtypeStruct((peers, rows, leaf // 2), jnp.bfloat16),
            jax.ShapeDtypeStruct((clusters * nvec, leaf), jnp.float32),
            jax.ShapeDtypeStruct((clusters * nvec, slots * nvec), jnp.bfloat16),
        ),
        in_specs=[ANY, ANY] + [VMEM] * 6,
        out_specs=(VMEM, VMEM, VMEM),
        scratch_shapes=[
            pltpu.SMEM((blocks,), jnp.int32),
            pltpu.SMEM((blocks,), jnp.int32),
            pltpu.SemaphoreType.DMA((2,)),
            pltpu.VMEM((slots * nvec, leaf // 2), jnp.float32),
            pltpu.VMEM((slots, nvec, leaf), jnp.float32),
        ]
        + scratch,
        compiler_params=pltpu.CompilerParams(vmem_limit_bytes=16 * 2**20),
        cost_estimate=cost(4 * blocks * 8 * nvec * leaf * rank, 4 * blocks * rank * leaf),
        name="far",
    )(far_slot, ret_slot, incoming, far_u, far_v, sources, near_blocks, pattern)
    back = lax.all_to_all(returns, "clus", split_axis=0, concat_axis=0, tiled=True)
    return pl.pallas_call(
        sum_kernel,
        out_shape=jax.ShapeDtypeStruct((clusters, nvec, leaf), jnp.float32),
        in_specs=[VMEM] * 4,
        out_specs=VMEM,
        compiler_params=params,
        cost_estimate=cost(2 * clusters * nvec * slots * nvec * leaf, slots * nvec * leaf * 2),
        name="sum",
    )(back, near_part, place, near_blocks)


def solution(mesh):
    placed = (
        P(("groups", "clus"), None, None),
        P(("groups", "clus"), None, None, None),
        P(("groups", "clus"), None, None),
        P(("groups", "clus"), None, None),
        P(("groups", "clus"), None, None),
        P(("groups", "clus")),
        P(("groups", "clus"), None, None),
        P(("groups", "clus")),
    )
    return jax.shard_map(
        body,
        mesh=mesh,
        in_specs=placed,
        out_specs=P(("groups", "clus"), None, None),
        check_vma=False,
    )
```

```python
import jax
import jax.numpy as jnp
from jax import lax
from jax.experimental import pallas as pl
from jax.experimental.pallas import tpu as pltpu
from jax.sharding import PartitionSpec as P

VMEM = pl.BlockSpec(memory_space=pltpu.VMEM)
ANY = pl.BlockSpec(memory_space=pl.ANY)
CHUNKS = 4


def halves(x):
    w = x.shape[1] // 2
    return [x[:, :w], x[:, w:]]


def pattern_kernel(out_ref):
    nvec, width = out_ref.shape
    lane = lax.broadcasted_iota(jnp.int32, (nvec, width), 1)
    sub = lax.broadcasted_iota(jnp.int32, (nvec, width), 0)
    out_ref[...] = jnp.where(lane % nvec == sub, lane // nvec, -2).astype(jnp.float32)


def pack_kernel(send_ref, ret_ref, src_ref, pattern_ref, out_ref):
    clusters, nvec, leaf = src_ref.shape
    cap, peers = send_ref.shape
    me = lax.axis_index("clus")
    rows = peers * nvec
    peer = lax.broadcasted_iota(jnp.int32, (rows, peers), 0) // nvec
    kind = lax.broadcasted_iota(jnp.int32, (rows, peers), 0) % nvec // cap
    column = lax.broadcasted_iota(jnp.int32, (rows, peers), 1)

    def entries_at(list_ref, which):
        entries = list_ref[...].astype(jnp.float32).astype(jnp.bfloat16)
        return lax.dot_general(
            jnp.where(which == column, 1.0, 0.0).astype(jnp.bfloat16),
            entries,
            (((1,), (1,)), ((), ())),
            preferred_element_type=jnp.float32,
        )

    send = jnp.maximum(entries_at(send_ref, peer), 0.0)
    ret = entries_at(ret_ref, jnp.where(kind == 1, me - 1, jnp.where(kind == 2, me + 1, peer)))
    row = lax.broadcasted_iota(jnp.int32, (rows, clusters * nvec), 0)
    lane = lax.broadcasted_iota(jnp.int32, (rows, clusters * nvec), 1)
    cluster = jnp.where(row % nvec == lane % nvec, lane // nvec, -2).astype(jnp.float32)
    source = src_ref[...].reshape(clusters * nvec, leaf)
    picked = []
    for k in range(cap):
        pick = jnp.where(send[:, k : k + 1] == cluster, 1.0, 0.0).astype(jnp.bfloat16)
        picked.append(jnp.dot(pick, source, preferred_element_type=jnp.float32))
    vector = lax.broadcasted_iota(jnp.int32, (rows, leaf // 2), 0) % nvec
    places = jnp.broadcast_to(ret[:, :1], (rows, leaf // 2))
    for k in range(1, cap):
        places = jnp.where(vector % cap == k, ret[:, k : k + 1], places)
    first = src_ref[0].astype(jnp.float32)
    last = src_ref[clusters - 1].astype(jnp.float32)
    for p in range(peers):
        at = slice(p * nvec, (p + 1) * nvec)
        parts = []
        for k in range(cap):
            parts += halves(picked[k][at])
        edge = halves(jnp.where(p > me, last, first))[0]
        parts.append(jnp.where(jnp.abs(p - me) == 1, edge, places[at]))
        out_ref[p] = jnp.concatenate(parts, axis=0).astype(out_ref.dtype)


def joined(rows, nvec):
    return jnp.concatenate([rows[:nvec], rows[nvec:]], axis=1)


def load_slots(slots_any, dests_any, slot_ref, dest_ref, sems):
    copies = [
        pltpu.make_async_copy(slots_any, slot_ref, sems.at[0]),
        pltpu.make_async_copy(dests_any, dest_ref, sems.at[1]),
    ]
    for copy in copies:
        copy.start()
    return copies


def near_product(src_ref, near_ref, x_ref, near_out):
    clusters, nvec, leaf = src_ref.shape
    peers, rows, _ = x_ref.shape
    me = lax.axis_index("clus")
    before = x_ref[jnp.maximum(me - 1, 0)][rows - nvec :].astype(jnp.float32)
    after = x_ref[jnp.minimum(me + 1, peers - 1)][rows - nvec :].astype(jnp.float32)
    before = jnp.where(me > 0, before, 0.0)
    after = jnp.where(me < peers - 1, after, 0.0)
    before, after = [
        jnp.concatenate([x, jnp.zeros_like(x)], axis=1).astype(jnp.bfloat16)
        for x in (before, after)
    ]
    sources = [before] + [src_ref[s] for s in range(clusters)] + [after]
    for s in range(clusters):
        near_out[s * nvec : (s + 1) * nvec] = jnp.dot(
            jnp.concatenate(sources[s : s + 3], axis=1),
            near_ref[s].reshape(3 * leaf, leaf),
            preferred_element_type=jnp.float32,
        )


def placement(x_ref, pattern_ref, place, place_out):
    nvec, width = pattern_ref.shape
    peers, rows, _ = x_ref.shape
    cap = place.shape[0] // (peers * nvec)
    cluster = pattern_ref[...]
    me = lax.axis_index("clus")

    def step(p, carry):
        tile = x_ref[p, rows - nvec :, :].astype(jnp.float32)
        tile = jnp.where(jnp.abs(p - me) == 1, -1.0, tile)
        for k in range(cap):
            at = jnp.broadcast_to(tile[k : k + 1], (nvec, width))
            place[pl.ds((p * cap + k) * nvec, nvec)] = jnp.where(at == cluster, 1.0, 0.0)
        return carry

    lax.fori_loop(0, peers, step, 0, unroll=min(peers, 16))
    place_out[...] = place[...].T[: place_out.shape[0]].astype(jnp.bfloat16)


def widen_sources(x_ref, xf):
    peers = x_ref.shape[0]
    slots, nvec, _ = xf.shape
    cap = slots // peers

    def widen(p, carry):
        rows = x_ref[p].astype(jnp.float32)
        for k in range(cap):
            xf[p * cap + k] = joined(rows[2 * k * nvec : 2 * (k + 1) * nvec], nvec)
        return carry

    lax.fori_loop(0, peers, widen, 0, unroll=min(peers, 16))


def project(picked, u, owner, nvec, group):
    full = lax.dot_general(picked, u, (((1,), (1,)), ((), ())), preferred_element_type=jnp.float32)
    kept = full[:nvec]
    for i in range(1, group):
        kept = jnp.where(owner == i, full[i * nvec : (i + 1) * nvec], kept)
    return kept


def put_returns(total, x_ref, src_ref, out_ref):
    peers, rows, width = x_ref.shape
    clusters, nvec, _ = src_ref.shape
    each = total.shape[0] // peers
    cap = each // nvec
    me = lax.axis_index("clus")
    first = halves(src_ref[0].astype(jnp.float32))[1]
    last = halves(src_ref[clusters - 1].astype(jnp.float32))[1]
    sub = lax.broadcasted_iota(jnp.int32, (nvec, width), 0)
    for p in range(peers):
        before = x_ref[max(p - 1, 0), rows - nvec :, :].astype(jnp.float32)
        after = x_ref[min(p + 1, peers - 1), rows - nvec :, :].astype(jnp.float32)
        handed = jnp.where(sub // cap == 2, before, after)
        edge = jnp.where(p > me, last, first)
        parts = halves(total[p * each : (p + 1) * each])
        parts.append(jnp.where(jnp.abs(p - me) == 1, edge, handed))
        out_ref[p] = jnp.concatenate(parts, axis=0).astype(out_ref.dtype)


def far_kernel(
    slots_any,
    dests_any,
    x_ref,
    u_ref,
    v_ref,
    src_ref,
    near_ref,
    pattern_ref,
    out_ref,
    near_out,
    place_out,
    slot_ref,
    dest_ref,
    sems,
    place,
    xf,
    picked, wide,
):
    peers = x_ref.shape[0]
    slots, nvec, leaf = xf.shape
    blocks, rank, _ = u_ref.shape
    group = leaf // rank
    groups = blocks // group
    per = groups // CHUNKS
    copies = load_slots(slots_any, dests_any, slot_ref, dest_ref, sems)
    widen_sources(x_ref, xf)
    placement(x_ref, pattern_ref, place, place_out)
    for copy in copies:
        copy.wait()
    near_product(src_ref, near_ref, x_ref, near_out)
    for g in range(groups):
        rows = [xf[slot_ref[g * group + i]] for i in range(group)]
        picked[g] = jnp.concatenate(rows, axis=0).astype(jnp.bfloat16)
    owner = lax.broadcasted_iota(jnp.int32, (nvec, leaf), 1) // rank
    total = None
    for c in range(CHUNKS):
        for g in range(c * per, (c + 1) * per):
            u = u_ref[g * group : (g + 1) * group].reshape(leaf, leaf)
            kept = project(picked[g], u, owner, nvec, group)
            dest = jnp.full((nvec, leaf), dest_ref[g * group], jnp.int32)
            for i in range(1, group):
                dest = jnp.where(owner == i, dest_ref[g * group + i], dest)
            dest = dest.astype(jnp.float32)
            kept = jnp.concatenate([kept, kept], axis=0).astype(jnp.bfloat16)
            dest = jnp.concatenate([dest, dest - 1.0], axis=0).astype(jnp.bfloat16)
            for o in range(0, slots, 2):
                wide[o * nvec : (o + 2) * nvec, g * leaf : (g + 1) * leaf] = jnp.where(
                    dest == jnp.bfloat16(o), kept, jnp.bfloat16(0)
                )
        v = v_ref[c * per * group : (c + 1) * per * group].reshape(per * leaf, leaf)
        part = jnp.dot(
            wide[:, c * per * leaf : (c + 1) * per * leaf], v, preferred_element_type=jnp.float32
        )
        total = part if total is None else total + part
    put_returns(total, x_ref, src_ref, out_ref)


def far_many_kernel(
    slots_any,
    dests_any,
    x_ref,
    u_ref,
    v_ref,
    src_ref,
    near_ref,
    pattern_ref,
    out_ref,
    near_out,
    place_out,
    slot_ref,
    dest_ref,
    sems,
    place,
    xf,
    coef, acc,
):
    slots, nvec, leaf = xf.shape
    blocks, rank, _ = u_ref.shape
    group = leaf // rank
    copies = load_slots(slots_any, dests_any, slot_ref, dest_ref, sems)
    widen_sources(x_ref, xf)
    placement(x_ref, pattern_ref, place, place_out)
    for copy in copies:
        copy.wait()
    near_product(src_ref, near_ref, x_ref, near_out)
    acc[...] = jnp.zeros_like(acc)
    owner = lax.broadcasted_iota(jnp.int32, (nvec, leaf), 1) // rank

    def forward(g, carry):
        rows = [xf[slot_ref[g * group + i]] for i in range(group)]
        picked = jnp.concatenate(rows, axis=0).astype(jnp.bfloat16)
        u = u_ref[pl.ds(g * group, group)].reshape(leaf, leaf)
        coef[g] = project(picked, u, owner, nvec, group)
        return carry

    def backward(g, carry):
        kept = coef[g]
        spread = jnp.concatenate(
            [jnp.where(owner == i, kept, 0.0) for i in range(group)], axis=0
        ).astype(jnp.bfloat16)
        v = v_ref[pl.ds(g * group, group)].reshape(leaf, leaf)
        terms = jnp.dot(spread, v, preferred_element_type=jnp.float32)
        for i in range(group):
            acc[dest_ref[g * group + i]] += terms[i * nvec : (i + 1) * nvec]
        return carry

    lax.fori_loop(0, blocks // group, forward, 0, unroll=4)
    lax.fori_loop(0, blocks // group, backward, 0, unroll=4)
    put_returns(acc[...].reshape(slots * nvec, leaf), x_ref, src_ref, out_ref)


def sum_kernel(back_ref, near_out_ref, place_ref, near_ref, out_ref):
    peers, rows, width = back_ref.shape
    clusters, nvec, leaf = out_ref.shape
    each = (rows - nvec) // 2
    cap = each // nvec
    me = lax.axis_index("clus")
    terms = jnp.concatenate(
        [back_ref[:, i * each : (i + 1) * each, :].reshape(peers * each, width) for i in range(2)],
        axis=1,
    )
    total = near_out_ref[...] + jnp.dot(
        place_ref[...], terms, preferred_element_type=jnp.float32
    )

    relay = jnp.where(me + 3 < peers, me + 3, me - 3)
    tile = back_ref[relay][rows - nvec :].astype(jnp.float32)
    before = back_ref[jnp.maximum(me - 1, 0)].astype(jnp.float32)
    after = back_ref[jnp.minimum(me + 1, peers - 1)].astype(jnp.float32)
    row = lax.broadcasted_iota(jnp.int32, (clusters * nvec, width), 0)
    lane = lax.broadcasted_iota(jnp.int32, (clusters * nvec, width), 1)
    named = jnp.full((1, width), -1.0, jnp.float32)
    for i in range(2 * cap):
        k, alive = (i + 2 * cap, me > 0) if i < cap else (i, me < peers - 1)
        entry = jnp.where(alive, tile[k : k + 1], -1.0)
        named = jnp.where(lane[:1] // nvec == i, entry, named)
    match = (named == (row // nvec).astype(jnp.float32)) & (lane % nvec == row % nvec)
    match = jnp.where(match, 1.0, 0.0)[:, : 2 * each].astype(jnp.bfloat16)
    sides = jnp.concatenate(
        [
            jnp.concatenate([side[:each], side[each : 2 * each]], axis=1)
            for side in (before, after)
        ],
        axis=0,
    ).astype(jnp.bfloat16)
    total += jnp.dot(match, sides, preferred_element_type=jnp.float32)

    edges = []
    for side, alive, at in ((before, me > 0, (0, 0)), (after, me < peers - 1, (clusters - 1, 2))):
        edge = jnp.where(alive, side[2 * each :], 0.0).astype(jnp.bfloat16)
        edges.append(
            jnp.dot(edge, near_ref[at[0], at[1], width:, :], preferred_element_type=jnp.float32)
        )
    for s in range(clusters):
        part = total[s * nvec : (s + 1) * nvec]
        if s == 0:
            part += edges[0]
        if s == clusters - 1:
            part += edges[1]
        out_ref[s] = part


def cost(flops, moved):
    return pl.CostEstimate(flops=flops, bytes_accessed=moved, transcendentals=0)


def body(sources, near_blocks, far_u, far_v, send_list, far_slot, ret_list, ret_slot):
    clusters, nvec, leaf = sources.shape
    _, peers, cap = send_list.shape
    blocks, rank, _ = far_u.shape
    slots = peers * cap
    rows = 2 * cap * nvec + nvec
    params = pltpu.CompilerParams(vmem_limit_bytes=8 * 2**20)
    pattern = pl.pallas_call(
        pattern_kernel,
        out_shape=jax.ShapeDtypeStruct((nvec, leaf // 2), jnp.float32),
        out_specs=VMEM,
        compiler_params=params,
        cost_estimate=cost(10**10, nvec * leaf * 2),
        name="pattern",
    )()
    message = pl.pallas_call(
        pack_kernel,
        out_shape=jax.ShapeDtypeStruct((peers, rows, leaf // 2), jnp.bfloat16),
        in_specs=[VMEM] * 4,
        out_specs=VMEM,
        compiler_params=params,
        cost_estimate=cost(10**10, peers * rows * leaf),
        name="pack",
    )(send_list[0].T, ret_list[0].T, sources, pattern)
    incoming = lax.all_to_all(message, "clus", split_axis=0, concat_axis=0, tiled=True)
    few = slots <= 32
    if few:
        scratch = [
            pltpu.VMEM((blocks * rank // leaf, leaf // rank * nvec, leaf), jnp.bfloat16),
            pltpu.VMEM((slots * nvec, blocks * rank), jnp.bfloat16),
        ]
    else:
        scratch = [
            pltpu.VMEM((blocks * rank // leaf, nvec, leaf), jnp.float32),
            pltpu.VMEM((slots, nvec, leaf), jnp.float32),
        ]
    returns, near_part, place = pl.pallas_call(
        far_kernel if few else far_many_kernel,
        out_shape=(
            jax.ShapeDtypeStruct((peers, rows, leaf // 2), jnp.bfloat16),
            jax.ShapeDtypeStruct((clusters * nvec, leaf), jnp.float32),
            jax.ShapeDtypeStruct((clusters * nvec, slots * nvec), jnp.bfloat16),
        ),
        in_specs=[ANY, ANY] + [VMEM] * 6,
        out_specs=(VMEM, VMEM, VMEM),
        scratch_shapes=[
            pltpu.SMEM((blocks,), jnp.int32),
            pltpu.SMEM((blocks,), jnp.int32),
            pltpu.SemaphoreType.DMA((2,)),
            pltpu.VMEM((slots * nvec, leaf // 2), jnp.float32),
            pltpu.VMEM((slots, nvec, leaf), jnp.float32),
        ]
        + scratch,
        compiler_params=pltpu.CompilerParams(vmem_limit_bytes=16 * 2**20),
        cost_estimate=cost(4 * blocks * 8 * nvec * leaf * rank, 4 * blocks * rank * leaf),
        name="far",
    )(far_slot, ret_slot, incoming, far_u, far_v, sources, near_blocks, pattern)
    back = lax.all_to_all(returns, "clus", split_axis=0, concat_axis=0, tiled=True)
    return pl.pallas_call(
        sum_kernel,
        out_shape=jax.ShapeDtypeStruct((clusters, nvec, leaf), jnp.float32),
        in_specs=[VMEM] * 4,
        out_specs=VMEM,
        compiler_params=params,
        cost_estimate=cost(2 * clusters * nvec * slots * nvec * leaf, slots * nvec * leaf * 2),
        name="sum",
    )(back, near_part, place, near_blocks)


def solution(mesh):
    placed = (
        P(("groups", "clus"), None, None),
        P(("groups", "clus"), None, None, None),
        P(("groups", "clus"), None, None),
        P(("groups", "clus"), None, None),
        P(("groups", "clus"), None, None),
        P(("groups", "clus")),
        P(("groups", "clus"), None, None),
        P(("groups", "clus")),
    )
    return jax.shard_map(
        body,
        mesh=mesh,
        in_specs=placed,
        out_specs=P(("groups", "clus"), None, None),
        check_vma=False,
    )
```

```python
import jax
import jax.numpy as jnp
from jax import lax
from jax.experimental import pallas as pl
from jax.experimental.pallas import tpu as pltpu
from jax.sharding import PartitionSpec as P

VMEM = pl.BlockSpec(memory_space=pltpu.VMEM)
ANY = pl.BlockSpec(memory_space=pl.ANY)
CHUNKS = 16


def halves(x):
    w = x.shape[1] // 2
    return [x[:, :w], x[:, w:]]


def pattern_kernel(out_ref):
    nvec, width = out_ref.shape
    lane = lax.broadcasted_iota(jnp.int32, (nvec, width), 1)
    sub = lax.broadcasted_iota(jnp.int32, (nvec, width), 0)
    out_ref[...] = jnp.where(lane % nvec == sub, lane // nvec, -2).astype(jnp.float32)


def pack_kernel(send_ref, ret_ref, src_ref, pattern_ref, out_ref):
    clusters, nvec, leaf = src_ref.shape
    cap, peers = send_ref.shape
    me = lax.axis_index("clus")
    rows = peers * nvec
    peer = lax.broadcasted_iota(jnp.int32, (rows, peers), 0) // nvec
    kind = lax.broadcasted_iota(jnp.int32, (rows, peers), 0) % nvec // cap
    column = lax.broadcasted_iota(jnp.int32, (rows, peers), 1)

    def entries_at(list_ref, which):
        entries = list_ref[...].astype(jnp.float32).astype(jnp.bfloat16)
        return lax.dot_general(
            jnp.where(which == column, 1.0, 0.0).astype(jnp.bfloat16),
            entries,
            (((1,), (1,)), ((), ())),
            preferred_element_type=jnp.float32,
        )

    send = jnp.maximum(entries_at(send_ref, peer), 0.0)
    ret = entries_at(ret_ref, jnp.where(kind == 1, me - 1, jnp.where(kind == 2, me + 1, peer)))
    row = lax.broadcasted_iota(jnp.int32, (rows, clusters * nvec), 0)
    lane = lax.broadcasted_iota(jnp.int32, (rows, clusters * nvec), 1)
    cluster = jnp.where(row % nvec == lane % nvec, lane // nvec, -2).astype(jnp.float32)
    source = src_ref[...].reshape(clusters * nvec, leaf)
    picked = []
    for k in range(cap):
        pick = jnp.where(send[:, k : k + 1] == cluster, 1.0, 0.0).astype(jnp.bfloat16)
        picked.append(jnp.dot(pick, source, preferred_element_type=jnp.float32))
    vector = lax.broadcasted_iota(jnp.int32, (rows, leaf // 2), 0) % nvec
    places = jnp.broadcast_to(ret[:, :1], (rows, leaf // 2))
    for k in range(1, cap):
        places = jnp.where(vector % cap == k, ret[:, k : k + 1], places)
    first = src_ref[0].astype(jnp.float32)
    last = src_ref[clusters - 1].astype(jnp.float32)
    for p in range(peers):
        at = slice(p * nvec, (p + 1) * nvec)
        parts = []
        for k in range(cap):
            parts += halves(picked[k][at])
        edge = halves(jnp.where(p > me, last, first))[0]
        parts.append(jnp.where(jnp.abs(p - me) == 1, edge, places[at]))
        out_ref[p] = jnp.concatenate(parts, axis=0).astype(out_ref.dtype)


def joined(rows, nvec):
    return jnp.concatenate([rows[:nvec], rows[nvec:]], axis=1)


def load_slots(slots_any, dests_any, slot_ref, dest_ref, sems):
    copies = [
        pltpu.make_async_copy(slots_any, slot_ref, sems.at[0]),
        pltpu.make_async_copy(dests_any, dest_ref, sems.at[1]),
    ]
    for copy in copies:
        copy.start()
    return copies


def near_product(src_ref, near_ref, x_ref, near_out):
    clusters, nvec, leaf = src_ref.shape
    peers, rows, _ = x_ref.shape
    me = lax.axis_index("clus")
    before = x_ref[jnp.maximum(me - 1, 0)][rows - nvec :].astype(jnp.float32)
    after = x_ref[jnp.minimum(me + 1, peers - 1)][rows - nvec :].astype(jnp.float32)
    before = jnp.where(me > 0, before, 0.0)
    after = jnp.where(me < peers - 1, after, 0.0)
    before, after = [
        jnp.concatenate([x, jnp.zeros_like(x)], axis=1).astype(jnp.bfloat16)
        for x in (before, after)
    ]
    sources = [before] + [src_ref[s] for s in range(clusters)] + [after]
    for s in range(clusters):
        near_out[s * nvec : (s + 1) * nvec] = jnp.dot(
            jnp.concatenate(sources[s : s + 3], axis=1),
            near_ref[s].reshape(3 * leaf, leaf),
            preferred_element_type=jnp.float32,
        )


def placement(x_ref, pattern_ref, place, place_out):
    nvec, width = pattern_ref.shape
    peers, rows, _ = x_ref.shape
    cap = place.shape[0] // (peers * nvec)
    cluster = pattern_ref[...]
    me = lax.axis_index("clus")

    def step(p, carry):
        tile = x_ref[p, rows - nvec :, :].astype(jnp.float32)
        tile = jnp.where(jnp.abs(p - me) == 1, -1.0, tile)
        for k in range(cap):
            at = jnp.broadcast_to(tile[k : k + 1], (nvec, width))
            place[pl.ds((p * cap + k) * nvec, nvec)] = jnp.where(at == cluster, 1.0, 0.0)
        return carry

    lax.fori_loop(0, peers, step, 0, unroll=min(peers, 16))
    place_out[...] = place[...].T[: place_out.shape[0]].astype(jnp.bfloat16)


def widen_sources(x_ref, xf):
    peers = x_ref.shape[0]
    slots, nvec, _ = xf.shape
    cap = slots // peers

    def widen(p, carry):
        rows = x_ref[p].astype(jnp.float32)
        for k in range(cap):
            xf[p * cap + k] = joined(rows[2 * k * nvec : 2 * (k + 1) * nvec], nvec)
        return carry

    lax.fori_loop(0, peers, widen, 0, unroll=min(peers, 16))


def project(picked, u, owner, nvec, group):
    full = lax.dot_general(picked, u, (((1,), (1,)), ((), ())), preferred_element_type=jnp.float32)
    kept = full[:nvec]
    for i in range(1, group):
        kept = jnp.where(owner == i, full[i * nvec : (i + 1) * nvec], kept)
    return kept


def put_returns(total, x_ref, src_ref, out_ref):
    peers, rows, width = x_ref.shape
    clusters, nvec, _ = src_ref.shape
    each = total.shape[0] // peers
    cap = each // nvec
    me = lax.axis_index("clus")
    first = halves(src_ref[0].astype(jnp.float32))[1]
    last = halves(src_ref[clusters - 1].astype(jnp.float32))[1]
    sub = lax.broadcasted_iota(jnp.int32, (nvec, width), 0)
    for p in range(peers):
        before = x_ref[max(p - 1, 0), rows - nvec :, :].astype(jnp.float32)
        after = x_ref[min(p + 1, peers - 1), rows - nvec :, :].astype(jnp.float32)
        handed = jnp.where(sub // cap == 2, before, after)
        edge = jnp.where(p > me, last, first)
        parts = halves(total[p * each : (p + 1) * each])
        parts.append(jnp.where(jnp.abs(p - me) == 1, edge, handed))
        out_ref[p] = jnp.concatenate(parts, axis=0).astype(out_ref.dtype)


def far_kernel(
    slots_any,
    dests_any,
    x_ref,
    u_ref,
    v_ref,
    src_ref,
    near_ref,
    pattern_ref,
    out_ref,
    near_out,
    place_out,
    slot_ref,
    dest_ref,
    sems,
    place,
    xf,
    picked, wide,
):
    peers = x_ref.shape[0]
    slots, nvec, leaf = xf.shape
    blocks, rank, _ = u_ref.shape
    group = leaf // rank
    groups = blocks // group
    per = groups // CHUNKS
    copies = load_slots(slots_any, dests_any, slot_ref, dest_ref, sems)
    widen_sources(x_ref, xf)
    placement(x_ref, pattern_ref, place, place_out)
    for copy in copies:
        copy.wait()
    near_product(src_ref, near_ref, x_ref, near_out)
    for g in range(groups):
        rows = [xf[slot_ref[g * group + i]] for i in range(group)]
        picked[g] = jnp.concatenate(rows, axis=0).astype(jnp.bfloat16)
    owner = lax.broadcasted_iota(jnp.int32, (nvec, leaf), 1) // rank
    total = None
    for c in range(CHUNKS):
        for g in range(c * per, (c + 1) * per):
            u = u_ref[g * group : (g + 1) * group].reshape(leaf, leaf)
            kept = project(picked[g], u, owner, nvec, group)
            dest = jnp.full((nvec, leaf), dest_ref[g * group], jnp.int32)
            for i in range(1, group):
                dest = jnp.where(owner == i, dest_ref[g * group + i], dest)
            dest = dest.astype(jnp.float32)
            kept = jnp.concatenate([kept, kept], axis=0).astype(jnp.bfloat16)
            dest = jnp.concatenate([dest, dest - 1.0], axis=0).astype(jnp.bfloat16)
            for o in range(0, slots, 2):
                wide[o * nvec : (o + 2) * nvec, g * leaf : (g + 1) * leaf] = jnp.where(
                    dest == jnp.bfloat16(o), kept, jnp.bfloat16(0)
                )
        v = v_ref[c * per * group : (c + 1) * per * group].reshape(per * leaf, leaf)
        part = jnp.dot(
            wide[:, c * per * leaf : (c + 1) * per * leaf], v, preferred_element_type=jnp.float32
        )
        total = part if total is None else total + part
    put_returns(total, x_ref, src_ref, out_ref)


def far_many_kernel(
    slots_any,
    dests_any,
    x_ref,
    u_ref,
    v_ref,
    src_ref,
    near_ref,
    pattern_ref,
    out_ref,
    near_out,
    place_out,
    slot_ref,
    dest_ref,
    sems,
    place,
    xf,
    coef, acc,
):
    slots, nvec, leaf = xf.shape
    blocks, rank, _ = u_ref.shape
    group = leaf // rank
    copies = load_slots(slots_any, dests_any, slot_ref, dest_ref, sems)
    widen_sources(x_ref, xf)
    placement(x_ref, pattern_ref, place, place_out)
    for copy in copies:
        copy.wait()
    near_product(src_ref, near_ref, x_ref, near_out)
    acc[...] = jnp.zeros_like(acc)
    owner = lax.broadcasted_iota(jnp.int32, (nvec, leaf), 1) // rank

    def forward(g, carry):
        rows = [xf[slot_ref[g * group + i]] for i in range(group)]
        picked = jnp.concatenate(rows, axis=0).astype(jnp.bfloat16)
        u = u_ref[pl.ds(g * group, group)].reshape(leaf, leaf)
        coef[g] = project(picked, u, owner, nvec, group)
        return carry

    def backward(g, carry):
        kept = coef[g]
        spread = jnp.concatenate(
            [jnp.where(owner == i, kept, 0.0) for i in range(group)], axis=0
        ).astype(jnp.bfloat16)
        v = v_ref[pl.ds(g * group, group)].reshape(leaf, leaf)
        terms = jnp.dot(spread, v, preferred_element_type=jnp.float32)
        for i in range(group):
            acc[dest_ref[g * group + i]] += terms[i * nvec : (i + 1) * nvec]
        return carry

    lax.fori_loop(0, blocks // group, forward, 0, unroll=4)
    lax.fori_loop(0, blocks // group, backward, 0, unroll=4)
    put_returns(acc[...].reshape(slots * nvec, leaf), x_ref, src_ref, out_ref)


def sum_kernel(back_ref, near_out_ref, place_ref, near_ref, out_ref):
    peers, rows, width = back_ref.shape
    clusters, nvec, leaf = out_ref.shape
    each = (rows - nvec) // 2
    cap = each // nvec
    me = lax.axis_index("clus")
    terms = jnp.concatenate(
        [back_ref[:, i * each : (i + 1) * each, :].reshape(peers * each, width) for i in range(2)],
        axis=1,
    )
    total = near_out_ref[...] + jnp.dot(
        place_ref[...], terms, preferred_element_type=jnp.float32
    )

    relay = jnp.where(me + 3 < peers, me + 3, me - 3)
    tile = back_ref[relay][rows - nvec :].astype(jnp.float32)
    before = back_ref[jnp.maximum(me - 1, 0)].astype(jnp.float32)
    after = back_ref[jnp.minimum(me + 1, peers - 1)].astype(jnp.float32)
    row = lax.broadcasted_iota(jnp.int32, (clusters * nvec, width), 0)
    lane = lax.broadcasted_iota(jnp.int32, (clusters * nvec, width), 1)
    named = jnp.full((1, width), -1.0, jnp.float32)
    for i in range(2 * cap):
        k, alive = (i + 2 * cap, me > 0) if i < cap else (i, me < peers - 1)
        entry = jnp.where(alive, tile[k : k + 1], -1.0)
        named = jnp.where(lane[:1] // nvec == i, entry, named)
    match = (named == (row // nvec).astype(jnp.float32)) & (lane % nvec == row % nvec)
    match = jnp.where(match, 1.0, 0.0)[:, : 2 * each].astype(jnp.bfloat16)
    sides = jnp.concatenate(
        [
            jnp.concatenate([side[:each], side[each : 2 * each]], axis=1)
            for side in (before, after)
        ],
        axis=0,
    ).astype(jnp.bfloat16)
    total += jnp.dot(match, sides, preferred_element_type=jnp.float32)

    edges = []
    for side, alive, at in ((before, me > 0, (0, 0)), (after, me < peers - 1, (clusters - 1, 2))):
        edge = jnp.where(alive, side[2 * each :], 0.0).astype(jnp.bfloat16)
        edges.append(
            jnp.dot(edge, near_ref[at[0], at[1], width:, :], preferred_element_type=jnp.float32)
        )
    for s in range(clusters):
        part = total[s * nvec : (s + 1) * nvec]
        if s == 0:
            part += edges[0]
        if s == clusters - 1:
            part += edges[1]
        out_ref[s] = part


def cost(flops, moved):
    return pl.CostEstimate(flops=flops, bytes_accessed=moved, transcendentals=0)


def body(sources, near_blocks, far_u, far_v, send_list, far_slot, ret_list, ret_slot):
    clusters, nvec, leaf = sources.shape
    _, peers, cap = send_list.shape
    blocks, rank, _ = far_u.shape
    slots = peers * cap
    rows = 2 * cap * nvec + nvec
    params = pltpu.CompilerParams(vmem_limit_bytes=8 * 2**20)
    pattern = pl.pallas_call(
        pattern_kernel,
        out_shape=jax.ShapeDtypeStruct((nvec, leaf // 2), jnp.float32),
        out_specs=VMEM,
        compiler_params=params,
        cost_estimate=cost(10**10, nvec * leaf * 2),
        name="pattern",
    )()
    message = pl.pallas_call(
        pack_kernel,
        out_shape=jax.ShapeDtypeStruct((peers, rows, leaf // 2), jnp.bfloat16),
        in_specs=[VMEM] * 4,
        out_specs=VMEM,
        compiler_params=params,
        cost_estimate=cost(10**10, peers * rows * leaf),
        name="pack",
    )(send_list[0].T, ret_list[0].T, sources, pattern)
    incoming = lax.all_to_all(message, "clus", split_axis=0, concat_axis=0, tiled=True)
    few = slots <= 32
    if few:
        scratch = [
            pltpu.VMEM((blocks * rank // leaf, leaf // rank * nvec, leaf), jnp.bfloat16),
            pltpu.VMEM((slots * nvec, blocks * rank), jnp.bfloat16),
        ]
    else:
        scratch = [
            pltpu.VMEM((blocks * rank // leaf, nvec, leaf), jnp.float32),
            pltpu.VMEM((slots, nvec, leaf), jnp.float32),
        ]
    returns, near_part, place = pl.pallas_call(
        far_kernel if few else far_many_kernel,
        out_shape=(
            jax.ShapeDtypeStruct((peers, rows, leaf // 2), jnp.bfloat16),
            jax.ShapeDtypeStruct((clusters * nvec, leaf), jnp.float32),
            jax.ShapeDtypeStruct((clusters * nvec, slots * nvec), jnp.bfloat16),
        ),
        in_specs=[ANY, ANY] + [VMEM] * 6,
        out_specs=(VMEM, VMEM, VMEM),
        scratch_shapes=[
            pltpu.SMEM((blocks,), jnp.int32),
            pltpu.SMEM((blocks,), jnp.int32),
            pltpu.SemaphoreType.DMA((2,)),
            pltpu.VMEM((slots * nvec, leaf // 2), jnp.float32),
            pltpu.VMEM((slots, nvec, leaf), jnp.float32),
        ]
        + scratch,
        compiler_params=pltpu.CompilerParams(vmem_limit_bytes=16 * 2**20),
        cost_estimate=cost(4 * blocks * 8 * nvec * leaf * rank, 4 * blocks * rank * leaf),
        name="far",
    )(far_slot, ret_slot, incoming, far_u, far_v, sources, near_blocks, pattern)
    back = lax.all_to_all(returns, "clus", split_axis=0, concat_axis=0, tiled=True)
    return pl.pallas_call(
        sum_kernel,
        out_shape=jax.ShapeDtypeStruct((clusters, nvec, leaf), jnp.float32),
        in_specs=[VMEM] * 4,
        out_specs=VMEM,
        compiler_params=params,
        cost_estimate=cost(2 * clusters * nvec * slots * nvec * leaf, slots * nvec * leaf * 2),
        name="sum",
    )(back, near_part, place, near_blocks)


def solution(mesh):
    placed = (
        P(("groups", "clus"), None, None),
        P(("groups", "clus"), None, None, None),
        P(("groups", "clus"), None, None),
        P(("groups", "clus"), None, None),
        P(("groups", "clus"), None, None),
        P(("groups", "clus")),
        P(("groups", "clus"), None, None),
        P(("groups", "clus")),
    )
    return jax.shard_map(
        body,
        mesh=mesh,
        in_specs=placed,
        out_specs=P(("groups", "clus"), None, None),
        check_vma=False,
    )
```

```python
import jax
import jax.numpy as jnp
from jax import lax
from jax.experimental import pallas as pl
from jax.experimental.pallas import tpu as pltpu
from jax.sharding import PartitionSpec as P

VMEM = pl.BlockSpec(memory_space=pltpu.VMEM)
ANY = pl.BlockSpec(memory_space=pl.ANY)
CHUNKS = 16


def halves(x):
    w = x.shape[1] // 2
    return [x[:, :w], x[:, w:]]


def pattern_kernel(out_ref):
    nvec, width = out_ref.shape
    lane = lax.broadcasted_iota(jnp.int32, (nvec, width), 1)
    sub = lax.broadcasted_iota(jnp.int32, (nvec, width), 0)
    out_ref[...] = jnp.where(lane % nvec == sub, lane // nvec, -2).astype(jnp.float32)


def pack_kernel(send_ref, ret_ref, src_ref, pattern_ref, out_ref):
    clusters, nvec, leaf = src_ref.shape
    cap, peers = send_ref.shape
    me = lax.axis_index("clus")
    rows = peers * nvec
    peer = lax.broadcasted_iota(jnp.int32, (rows, peers), 0) // nvec
    kind = lax.broadcasted_iota(jnp.int32, (rows, peers), 0) % nvec // cap
    column = lax.broadcasted_iota(jnp.int32, (rows, peers), 1)

    def entries_at(list_ref, which):
        entries = list_ref[...].astype(jnp.float32).astype(jnp.bfloat16)
        return lax.dot_general(
            jnp.where(which == column, 1.0, 0.0).astype(jnp.bfloat16),
            entries,
            (((1,), (1,)), ((), ())),
            preferred_element_type=jnp.float32,
        )

    send = jnp.maximum(entries_at(send_ref, peer), 0.0)
    ret = entries_at(ret_ref, jnp.where(kind == 1, me - 1, jnp.where(kind == 2, me + 1, peer)))
    row = lax.broadcasted_iota(jnp.int32, (rows, clusters * nvec), 0)
    lane = lax.broadcasted_iota(jnp.int32, (rows, clusters * nvec), 1)
    cluster = jnp.where(row % nvec == lane % nvec, lane // nvec, -2).astype(jnp.float32)
    source = src_ref[...].reshape(clusters * nvec, leaf)
    picked = []
    for k in range(cap):
        pick = jnp.where(send[:, k : k + 1] == cluster, 1.0, 0.0).astype(jnp.bfloat16)
        picked.append(jnp.dot(pick, source, preferred_element_type=jnp.float32))
    vector = lax.broadcasted_iota(jnp.int32, (rows, leaf // 2), 0) % nvec
    places = jnp.broadcast_to(ret[:, :1], (rows, leaf // 2))
    for k in range(1, cap):
        places = jnp.where(vector % cap == k, ret[:, k : k + 1], places)
    first = src_ref[0].astype(jnp.float32)
    last = src_ref[clusters - 1].astype(jnp.float32)
    for p in range(peers):
        at = slice(p * nvec, (p + 1) * nvec)
        parts = []
        for k in range(cap):
            parts += halves(picked[k][at])
        edge = halves(jnp.where(p > me, last, first))[0]
        parts.append(jnp.where(jnp.abs(p - me) == 1, edge, places[at]))
        out_ref[p] = jnp.concatenate(parts, axis=0).astype(out_ref.dtype)


def joined(rows, nvec):
    return jnp.concatenate([rows[:nvec], rows[nvec:]], axis=1)


def load_slots(slots_any, dests_any, slot_ref, dest_ref, sems):
    copies = [
        pltpu.make_async_copy(slots_any, slot_ref, sems.at[0]),
        pltpu.make_async_copy(dests_any, dest_ref, sems.at[1]),
    ]
    for copy in copies:
        copy.start()
    return copies


def near_product(src_ref, near_ref, x_ref, near_out):
    clusters, nvec, leaf = src_ref.shape
    peers, rows, _ = x_ref.shape
    me = lax.axis_index("clus")
    before = x_ref[jnp.maximum(me - 1, 0)][rows - nvec :].astype(jnp.float32)
    after = x_ref[jnp.minimum(me + 1, peers - 1)][rows - nvec :].astype(jnp.float32)
    before = jnp.where(me > 0, before, 0.0)
    after = jnp.where(me < peers - 1, after, 0.0)
    before, after = [
        jnp.concatenate([x, jnp.zeros_like(x)], axis=1).astype(jnp.bfloat16)
        for x in (before, after)
    ]
    sources = [before] + [src_ref[s] for s in range(clusters)] + [after]
    for s in range(clusters):
        near_out[s * nvec : (s + 1) * nvec] = jnp.dot(
            jnp.concatenate(sources[s : s + 3], axis=1),
            near_ref[s].reshape(3 * leaf, leaf),
            preferred_element_type=jnp.float32,
        )


def placement(x_ref, pattern_ref, place, place_out):
    nvec, width = pattern_ref.shape
    peers, rows, _ = x_ref.shape
    cap = place.shape[0] // (peers * nvec)
    cluster = pattern_ref[...]
    me = lax.axis_index("clus")

    def step(p, carry):
        tile = x_ref[p, rows - nvec :, :].astype(jnp.float32)
        tile = jnp.where(jnp.abs(p - me) == 1, -1.0, tile)
        for k in range(cap):
            at = jnp.broadcast_to(tile[k : k + 1], (nvec, width))
            place[pl.ds((p * cap + k) * nvec, nvec)] = jnp.where(at == cluster, 1.0, 0.0)
        return carry

    lax.fori_loop(0, peers, step, 0, unroll=min(peers, 16))
    place_out[...] = place[...].T[: place_out.shape[0]].astype(jnp.bfloat16)


def widen_sources(x_ref, xf):
    peers = x_ref.shape[0]
    slots, nvec, _ = xf.shape
    cap = slots // peers

    def widen(p, carry):
        rows = x_ref[p].astype(jnp.float32)
        for k in range(cap):
            xf[p * cap + k] = joined(rows[2 * k * nvec : 2 * (k + 1) * nvec], nvec)
        return carry

    lax.fori_loop(0, peers, widen, 0, unroll=min(peers, 16))


def project(picked, u, owner, nvec, group):
    full = lax.dot_general(picked, u, (((1,), (1,)), ((), ())), preferred_element_type=jnp.float32)
    kept = full[:nvec]
    for i in range(1, group):
        kept = jnp.where(owner == i, full[i * nvec : (i + 1) * nvec], kept)
    return kept


def put_returns(total, x_ref, src_ref, out_ref):
    peers, rows, width = x_ref.shape
    clusters, nvec, _ = src_ref.shape
    each = total.shape[0] // peers
    cap = each // nvec
    me = lax.axis_index("clus")
    first = halves(src_ref[0].astype(jnp.float32))[1]
    last = halves(src_ref[clusters - 1].astype(jnp.float32))[1]
    sub = lax.broadcasted_iota(jnp.int32, (nvec, width), 0)
    for p in range(peers):
        before = x_ref[max(p - 1, 0), rows - nvec :, :].astype(jnp.float32)
        after = x_ref[min(p + 1, peers - 1), rows - nvec :, :].astype(jnp.float32)
        handed = jnp.where(sub // cap == 2, before, after)
        edge = jnp.where(p > me, last, first)
        parts = halves(total[p * each : (p + 1) * each])
        parts.append(jnp.where(jnp.abs(p - me) == 1, edge, handed))
        out_ref[p] = jnp.concatenate(parts, axis=0).astype(out_ref.dtype)


def far_kernel(
    slots_any,
    dests_any,
    x_ref,
    u_ref,
    v_ref,
    src_ref,
    near_ref,
    pattern_ref,
    out_ref,
    near_out,
    place_out,
    slot_ref,
    dest_ref,
    sems,
    place,
    xf,
    picked, wide,
):
    peers = x_ref.shape[0]
    slots, nvec, leaf = xf.shape
    blocks, rank, _ = u_ref.shape
    group = leaf // rank
    groups = blocks // group
    per = groups // CHUNKS
    copies = load_slots(slots_any, dests_any, slot_ref, dest_ref, sems)
    widen_sources(x_ref, xf)
    placement(x_ref, pattern_ref, place, place_out)
    for copy in copies:
        copy.wait()
    near_product(src_ref, near_ref, x_ref, near_out)
    for g in range(groups):
        rows = [xf[slot_ref[g * group + i]] for i in range(group)]
        picked[g] = jnp.concatenate(rows, axis=0).astype(jnp.bfloat16)
    owner = lax.broadcasted_iota(jnp.int32, (nvec, leaf), 1) // rank

    def coefficients(c):
        return [
            project(
                picked[g],
                u_ref[g * group : (g + 1) * group].reshape(leaf, leaf),
                owner,
                nvec,
                group,
            )
            for g in range(c * per, (c + 1) * per)
        ]

    total = None
    ahead = coefficients(0)
    for c in range(CHUNKS):
        now, ahead = ahead, coefficients(c + 1) if c + 1 < CHUNKS else None
        for g, kept in zip(range(c * per, (c + 1) * per), now):
            dest = jnp.full((nvec, leaf), dest_ref[g * group], jnp.int32)
            for i in range(1, group):
                dest = jnp.where(owner == i, dest_ref[g * group + i], dest)
            dest = dest.astype(jnp.float32)
            kept = jnp.concatenate([kept, kept], axis=0).astype(jnp.bfloat16)
            dest = jnp.concatenate([dest, dest - 1.0], axis=0).astype(jnp.bfloat16)
            for o in range(0, slots, 2):
                wide[o * nvec : (o + 2) * nvec, g * leaf : (g + 1) * leaf] = jnp.where(
                    dest == jnp.bfloat16(o), kept, jnp.bfloat16(0)
                )
        v = v_ref[c * per * group : (c + 1) * per * group].reshape(per * leaf, leaf)
        part = jnp.dot(
            wide[:, c * per * leaf : (c + 1) * per * leaf], v, preferred_element_type=jnp.float32
        )
        total = part if total is None else total + part
    put_returns(total, x_ref, src_ref, out_ref)


def far_many_kernel(
    slots_any,
    dests_any,
    x_ref,
    u_ref,
    v_ref,
    src_ref,
    near_ref,
    pattern_ref,
    out_ref,
    near_out,
    place_out,
    slot_ref,
    dest_ref,
    sems,
    place,
    xf,
    coef, acc,
):
    slots, nvec, leaf = xf.shape
    blocks, rank, _ = u_ref.shape
    group = leaf // rank
    copies = load_slots(slots_any, dests_any, slot_ref, dest_ref, sems)
    widen_sources(x_ref, xf)
    placement(x_ref, pattern_ref, place, place_out)
    for copy in copies:
        copy.wait()
    near_product(src_ref, near_ref, x_ref, near_out)
    acc[...] = jnp.zeros_like(acc)
    owner = lax.broadcasted_iota(jnp.int32, (nvec, leaf), 1) // rank

    def forward(g, carry):
        rows = [xf[slot_ref[g * group + i]] for i in range(group)]
        picked = jnp.concatenate(rows, axis=0).astype(jnp.bfloat16)
        u = u_ref[pl.ds(g * group, group)].reshape(leaf, leaf)
        coef[g] = project(picked, u, owner, nvec, group)
        return carry

    def backward(g, carry):
        kept = coef[g]
        spread = jnp.concatenate(
            [jnp.where(owner == i, kept, 0.0) for i in range(group)], axis=0
        ).astype(jnp.bfloat16)
        v = v_ref[pl.ds(g * group, group)].reshape(leaf, leaf)
        terms = jnp.dot(spread, v, preferred_element_type=jnp.float32)
        for i in range(group):
            acc[dest_ref[g * group + i]] += terms[i * nvec : (i + 1) * nvec]
        return carry

    lax.fori_loop(0, blocks // group, forward, 0, unroll=4)
    lax.fori_loop(0, blocks // group, backward, 0, unroll=4)
    put_returns(acc[...].reshape(slots * nvec, leaf), x_ref, src_ref, out_ref)


def sum_kernel(back_ref, near_out_ref, place_ref, near_ref, out_ref):
    peers, rows, width = back_ref.shape
    clusters, nvec, leaf = out_ref.shape
    each = (rows - nvec) // 2
    cap = each // nvec
    me = lax.axis_index("clus")
    terms = jnp.concatenate(
        [back_ref[:, i * each : (i + 1) * each, :].reshape(peers * each, width) for i in range(2)],
        axis=1,
    )
    total = near_out_ref[...] + jnp.dot(
        place_ref[...], terms, preferred_element_type=jnp.float32
    )

    relay = jnp.where(me + 3 < peers, me + 3, me - 3)
    tile = back_ref[relay][rows - nvec :].astype(jnp.float32)
    before = back_ref[jnp.maximum(me - 1, 0)].astype(jnp.float32)
    after = back_ref[jnp.minimum(me + 1, peers - 1)].astype(jnp.float32)
    row = lax.broadcasted_iota(jnp.int32, (clusters * nvec, width), 0)
    lane = lax.broadcasted_iota(jnp.int32, (clusters * nvec, width), 1)
    named = jnp.full((1, width), -1.0, jnp.float32)
    for i in range(2 * cap):
        k, alive = (i + 2 * cap, me > 0) if i < cap else (i, me < peers - 1)
        entry = jnp.where(alive, tile[k : k + 1], -1.0)
        named = jnp.where(lane[:1] // nvec == i, entry, named)
    match = (named == (row // nvec).astype(jnp.float32)) & (lane % nvec == row % nvec)
    match = jnp.where(match, 1.0, 0.0)[:, : 2 * each].astype(jnp.bfloat16)
    sides = jnp.concatenate(
        [
            jnp.concatenate([side[:each], side[each : 2 * each]], axis=1)
            for side in (before, after)
        ],
        axis=0,
    ).astype(jnp.bfloat16)
    total += jnp.dot(match, sides, preferred_element_type=jnp.float32)

    edges = []
    for side, alive, at in ((before, me > 0, (0, 0)), (after, me < peers - 1, (clusters - 1, 2))):
        edge = jnp.where(alive, side[2 * each :], 0.0).astype(jnp.bfloat16)
        edges.append(
            jnp.dot(edge, near_ref[at[0], at[1], width:, :], preferred_element_type=jnp.float32)
        )
    for s in range(clusters):
        part = total[s * nvec : (s + 1) * nvec]
        if s == 0:
            part += edges[0]
        if s == clusters - 1:
            part += edges[1]
        out_ref[s] = part


def cost(flops, moved):
    return pl.CostEstimate(flops=flops, bytes_accessed=moved, transcendentals=0)


def body(sources, near_blocks, far_u, far_v, send_list, far_slot, ret_list, ret_slot):
    clusters, nvec, leaf = sources.shape
    _, peers, cap = send_list.shape
    blocks, rank, _ = far_u.shape
    slots = peers * cap
    rows = 2 * cap * nvec + nvec
    params = pltpu.CompilerParams(vmem_limit_bytes=8 * 2**20)
    pattern = pl.pallas_call(
        pattern_kernel,
        out_shape=jax.ShapeDtypeStruct((nvec, leaf // 2), jnp.float32),
        out_specs=VMEM,
        compiler_params=params,
        cost_estimate=cost(10**10, nvec * leaf * 2),
        name="pattern",
    )()
    message = pl.pallas_call(
        pack_kernel,
        out_shape=jax.ShapeDtypeStruct((peers, rows, leaf // 2), jnp.bfloat16),
        in_specs=[VMEM] * 4,
        out_specs=VMEM,
        compiler_params=params,
        cost_estimate=cost(10**10, peers * rows * leaf),
        name="pack",
    )(send_list[0].T, ret_list[0].T, sources, pattern)
    incoming = lax.all_to_all(message, "clus", split_axis=0, concat_axis=0, tiled=True)
    few = slots <= 32
    if few:
        scratch = [
            pltpu.VMEM((blocks * rank // leaf, leaf // rank * nvec, leaf), jnp.bfloat16),
            pltpu.VMEM((slots * nvec, blocks * rank), jnp.bfloat16),
        ]
    else:
        scratch = [
            pltpu.VMEM((blocks * rank // leaf, nvec, leaf), jnp.float32),
            pltpu.VMEM((slots, nvec, leaf), jnp.float32),
        ]
    returns, near_part, place = pl.pallas_call(
        far_kernel if few else far_many_kernel,
        out_shape=(
            jax.ShapeDtypeStruct((peers, rows, leaf // 2), jnp.bfloat16),
            jax.ShapeDtypeStruct((clusters * nvec, leaf), jnp.float32),
            jax.ShapeDtypeStruct((clusters * nvec, slots * nvec), jnp.bfloat16),
        ),
        in_specs=[ANY, ANY] + [VMEM] * 6,
        out_specs=(VMEM, VMEM, VMEM),
        scratch_shapes=[
            pltpu.SMEM((blocks,), jnp.int32),
            pltpu.SMEM((blocks,), jnp.int32),
            pltpu.SemaphoreType.DMA((2,)),
            pltpu.VMEM((slots * nvec, leaf // 2), jnp.float32),
            pltpu.VMEM((slots, nvec, leaf), jnp.float32),
        ]
        + scratch,
        compiler_params=pltpu.CompilerParams(vmem_limit_bytes=16 * 2**20),
        cost_estimate=cost(4 * blocks * 8 * nvec * leaf * rank, 4 * blocks * rank * leaf),
        name="far",
    )(far_slot, ret_slot, incoming, far_u, far_v, sources, near_blocks, pattern)
    back = lax.all_to_all(returns, "clus", split_axis=0, concat_axis=0, tiled=True)
    return pl.pallas_call(
        sum_kernel,
        out_shape=jax.ShapeDtypeStruct((clusters, nvec, leaf), jnp.float32),
        in_specs=[VMEM] * 4,
        out_specs=VMEM,
        compiler_params=params,
        cost_estimate=cost(2 * clusters * nvec * slots * nvec * leaf, slots * nvec * leaf * 2),
        name="sum",
    )(back, near_part, place, near_blocks)


def solution(mesh):
    placed = (
        P(("groups", "clus"), None, None),
        P(("groups", "clus"), None, None, None),
        P(("groups", "clus"), None, None),
        P(("groups", "clus"), None, None),
        P(("groups", "clus"), None, None),
        P(("groups", "clus")),
        P(("groups", "clus"), None, None),
        P(("groups", "clus")),
    )
    return jax.shard_map(
        body,
        mesh=mesh,
        in_specs=placed,
        out_specs=P(("groups", "clus"), None, None),
        check_vma=False,
    )
```

```python
import jax
import jax.numpy as jnp
from jax import lax
from jax.experimental import pallas as pl
from jax.experimental.pallas import tpu as pltpu
from jax.sharding import PartitionSpec as P

VMEM = pl.BlockSpec(memory_space=pltpu.VMEM)
ANY = pl.BlockSpec(memory_space=pl.ANY)
CHUNKS = 16


def halves(x):
    w = x.shape[1] // 2
    return [x[:, :w], x[:, w:]]


def pattern_kernel(out_ref):
    nvec, width = out_ref.shape
    lane = lax.broadcasted_iota(jnp.int32, (nvec, width), 1)
    sub = lax.broadcasted_iota(jnp.int32, (nvec, width), 0)
    out_ref[...] = jnp.where(lane % nvec == sub, lane // nvec, -2).astype(jnp.float32)


def pack_kernel(send_ref, ret_ref, src_ref, pattern_ref, out_ref):
    clusters, nvec, leaf = src_ref.shape
    cap, peers = send_ref.shape
    me = lax.axis_index("clus")
    rows = peers * nvec
    peer = lax.broadcasted_iota(jnp.int32, (rows, peers), 0) // nvec
    kind = lax.broadcasted_iota(jnp.int32, (rows, peers), 0) % nvec // cap
    column = lax.broadcasted_iota(jnp.int32, (rows, peers), 1)

    def entries_at(list_ref, which):
        entries = list_ref[...].astype(jnp.float32).astype(jnp.bfloat16)
        return lax.dot_general(
            jnp.where(which == column, 1.0, 0.0).astype(jnp.bfloat16),
            entries,
            (((1,), (1,)), ((), ())),
            preferred_element_type=jnp.float32,
        )

    send = jnp.maximum(entries_at(send_ref, peer), 0.0)
    ret = entries_at(ret_ref, jnp.where(kind == 1, me - 1, jnp.where(kind == 2, me + 1, peer)))
    row = lax.broadcasted_iota(jnp.int32, (rows, clusters * nvec), 0)
    lane = lax.broadcasted_iota(jnp.int32, (rows, clusters * nvec), 1)
    cluster = jnp.where(row % nvec == lane % nvec, lane // nvec, -2).astype(jnp.float32)
    source = src_ref[...].reshape(clusters * nvec, leaf)
    picked = []
    for k in range(cap):
        pick = jnp.where(send[:, k : k + 1] == cluster, 1.0, 0.0).astype(jnp.bfloat16)
        picked.append(jnp.dot(pick, source, preferred_element_type=jnp.float32))
    vector = lax.broadcasted_iota(jnp.int32, (rows, leaf // 2), 0) % nvec
    places = jnp.broadcast_to(ret[:, :1], (rows, leaf // 2))
    for k in range(1, cap):
        places = jnp.where(vector % cap == k, ret[:, k : k + 1], places)
    first = src_ref[0].astype(jnp.float32)
    last = src_ref[clusters - 1].astype(jnp.float32)
    for p in range(peers):
        at = slice(p * nvec, (p + 1) * nvec)
        parts = []
        for k in range(cap):
            parts += halves(picked[k][at])
        edge = halves(jnp.where(p > me, last, first))[0]
        parts.append(jnp.where(jnp.abs(p - me) == 1, edge, places[at]))
        out_ref[p] = jnp.concatenate(parts, axis=0).astype(out_ref.dtype)


def joined(rows, nvec):
    return jnp.concatenate([rows[:nvec], rows[nvec:]], axis=1)


def load_slots(slots_any, dests_any, slot_ref, dest_ref, sems):
    copies = [
        pltpu.make_async_copy(slots_any, slot_ref, sems.at[0]),
        pltpu.make_async_copy(dests_any, dest_ref, sems.at[1]),
    ]
    for copy in copies:
        copy.start()
    return copies


def near_product(src_ref, near_ref, x_ref, near_out):
    clusters, nvec, leaf = src_ref.shape
    peers, rows, _ = x_ref.shape
    me = lax.axis_index("clus")
    before = x_ref[jnp.maximum(me - 1, 0)][rows - nvec :].astype(jnp.float32)
    after = x_ref[jnp.minimum(me + 1, peers - 1)][rows - nvec :].astype(jnp.float32)
    before = jnp.where(me > 0, before, 0.0)
    after = jnp.where(me < peers - 1, after, 0.0)
    before, after = [
        jnp.concatenate([x, jnp.zeros_like(x)], axis=1).astype(jnp.bfloat16)
        for x in (before, after)
    ]
    sources = [before] + [src_ref[s] for s in range(clusters)] + [after]
    for s in range(clusters):
        near_out[s * nvec : (s + 1) * nvec] = jnp.dot(
            jnp.concatenate(sources[s : s + 3], axis=1),
            near_ref[s].reshape(3 * leaf, leaf),
            preferred_element_type=jnp.float32,
        )


def placement(x_ref, pattern_ref, place, place_out):
    nvec, width = pattern_ref.shape
    peers, rows, _ = x_ref.shape
    cap = place.shape[0] // (peers * nvec)
    cluster = pattern_ref[...]
    me = lax.axis_index("clus")

    def step(p, carry):
        tile = x_ref[p, rows - nvec :, :].astype(jnp.float32)
        tile = jnp.where(jnp.abs(p - me) == 1, -1.0, tile)
        for k in range(cap):
            at = jnp.broadcast_to(tile[k : k + 1], (nvec, width))
            place[pl.ds((p * cap + k) * nvec, nvec)] = jnp.where(at == cluster, 1.0, 0.0)
        return carry

    lax.fori_loop(0, peers, step, 0, unroll=min(peers, 16))
    place_out[...] = place[...].T[: place_out.shape[0]].astype(jnp.bfloat16)


def widen_sources(x_ref, xf):
    peers = x_ref.shape[0]
    slots, nvec, _ = xf.shape
    cap = slots // peers

    def widen(p, carry):
        rows = x_ref[p].astype(jnp.float32)
        for k in range(cap):
            xf[p * cap + k] = joined(rows[2 * k * nvec : 2 * (k + 1) * nvec], nvec)
        return carry

    lax.fori_loop(0, peers, widen, 0, unroll=min(peers, 16))


def project(picked, u, owner, nvec, group):
    full = lax.dot_general(picked, u, (((1,), (1,)), ((), ())), preferred_element_type=jnp.float32)
    kept = full[:nvec]
    for i in range(1, group):
        kept = jnp.where(owner == i, full[i * nvec : (i + 1) * nvec], kept)
    return kept


def put_returns(total, x_ref, src_ref, out_ref):
    peers, rows, width = x_ref.shape
    clusters, nvec, _ = src_ref.shape
    each = total.shape[0] // peers
    cap = each // nvec
    me = lax.axis_index("clus")
    first = halves(src_ref[0].astype(jnp.float32))[1]
    last = halves(src_ref[clusters - 1].astype(jnp.float32))[1]
    sub = lax.broadcasted_iota(jnp.int32, (nvec, width), 0)
    for p in range(peers):
        before = x_ref[max(p - 1, 0), rows - nvec :, :].astype(jnp.float32)
        after = x_ref[min(p + 1, peers - 1), rows - nvec :, :].astype(jnp.float32)
        handed = jnp.where(sub // cap == 2, before, after)
        edge = jnp.where(p > me, last, first)
        parts = halves(total[p * each : (p + 1) * each])
        parts.append(jnp.where(jnp.abs(p - me) == 1, edge, handed))
        out_ref[p] = jnp.concatenate(parts, axis=0).astype(out_ref.dtype)


def far_kernel(
    slots_any,
    dests_any,
    x_ref,
    u_ref,
    v_ref,
    src_ref,
    near_ref,
    pattern_ref,
    out_ref,
    near_out,
    place_out,
    slot_ref,
    dest_ref,
    sems,
    place,
    xf,
    wide,
):
    peers = x_ref.shape[0]
    slots, nvec, leaf = xf.shape
    blocks, rank, _ = u_ref.shape
    group = leaf // rank
    groups = blocks // group
    per = groups // CHUNKS
    copies = load_slots(slots_any, dests_any, slot_ref, dest_ref, sems)
    widen_sources(x_ref, xf)
    placement(x_ref, pattern_ref, place, place_out)
    for copy in copies:
        copy.wait()
    near_product(src_ref, near_ref, x_ref, near_out)
    owner = lax.broadcasted_iota(jnp.int32, (nvec, leaf), 1) // rank

    def coefficients(c):
        kept = []
        for g in range(c * per, (c + 1) * per):
            rows = [xf[slot_ref[g * group + i]] for i in range(group)]
            rows = jnp.concatenate(rows, axis=0).astype(jnp.bfloat16)
            u = u_ref[g * group : (g + 1) * group].reshape(leaf, leaf)
            kept.append(project(rows, u, owner, nvec, group))
        return kept

    total = None
    ahead = coefficients(0)
    for c in range(CHUNKS):
        now, ahead = ahead, coefficients(c + 1) if c + 1 < CHUNKS else None
        for g, kept in zip(range(c * per, (c + 1) * per), now):
            dest = jnp.full((nvec, leaf), dest_ref[g * group], jnp.int32)
            for i in range(1, group):
                dest = jnp.where(owner == i, dest_ref[g * group + i], dest)
            dest = dest.astype(jnp.float32)
            kept = jnp.concatenate([kept, kept], axis=0).astype(jnp.bfloat16)
            dest = jnp.concatenate([dest, dest - 1.0], axis=0).astype(jnp.bfloat16)
            for o in range(0, slots, 2):
                wide[o * nvec : (o + 2) * nvec, g * leaf : (g + 1) * leaf] = jnp.where(
                    dest == jnp.bfloat16(o), kept, jnp.bfloat16(0)
                )
        v = v_ref[c * per * group : (c + 1) * per * group].reshape(per * leaf, leaf)
        part = jnp.dot(
            wide[:, c * per * leaf : (c + 1) * per * leaf], v, preferred_element_type=jnp.float32
        )
        total = part if total is None else total + part
    put_returns(total, x_ref, src_ref, out_ref)


def far_many_kernel(
    slots_any,
    dests_any,
    x_ref,
    u_ref,
    v_ref,
    src_ref,
    near_ref,
    pattern_ref,
    out_ref,
    near_out,
    place_out,
    slot_ref,
    dest_ref,
    sems,
    place,
    xf,
    coef, acc,
):
    slots, nvec, leaf = xf.shape
    blocks, rank, _ = u_ref.shape
    group = leaf // rank
    copies = load_slots(slots_any, dests_any, slot_ref, dest_ref, sems)
    widen_sources(x_ref, xf)
    placement(x_ref, pattern_ref, place, place_out)
    for copy in copies:
        copy.wait()
    near_product(src_ref, near_ref, x_ref, near_out)
    acc[...] = jnp.zeros_like(acc)
    owner = lax.broadcasted_iota(jnp.int32, (nvec, leaf), 1) // rank

    def forward(g, carry):
        rows = [xf[slot_ref[g * group + i]] for i in range(group)]
        picked = jnp.concatenate(rows, axis=0).astype(jnp.bfloat16)
        u = u_ref[pl.ds(g * group, group)].reshape(leaf, leaf)
        coef[g] = project(picked, u, owner, nvec, group)
        return carry

    def backward(g, carry):
        kept = coef[g]
        spread = jnp.concatenate(
            [jnp.where(owner == i, kept, 0.0) for i in range(group)], axis=0
        ).astype(jnp.bfloat16)
        v = v_ref[pl.ds(g * group, group)].reshape(leaf, leaf)
        terms = jnp.dot(spread, v, preferred_element_type=jnp.float32)
        for i in range(group):
            acc[dest_ref[g * group + i]] += terms[i * nvec : (i + 1) * nvec]
        return carry

    lax.fori_loop(0, blocks // group, forward, 0, unroll=4)
    lax.fori_loop(0, blocks // group, backward, 0, unroll=4)
    put_returns(acc[...].reshape(slots * nvec, leaf), x_ref, src_ref, out_ref)


def sum_kernel(back_ref, near_out_ref, place_ref, near_ref, out_ref):
    peers, rows, width = back_ref.shape
    clusters, nvec, leaf = out_ref.shape
    each = (rows - nvec) // 2
    cap = each // nvec
    me = lax.axis_index("clus")
    terms = jnp.concatenate(
        [back_ref[:, i * each : (i + 1) * each, :].reshape(peers * each, width) for i in range(2)],
        axis=1,
    )
    total = near_out_ref[...] + jnp.dot(
        place_ref[...], terms, preferred_element_type=jnp.float32
    )

    relay = jnp.where(me + 3 < peers, me + 3, me - 3)
    tile = back_ref[relay][rows - nvec :].astype(jnp.float32)
    before = back_ref[jnp.maximum(me - 1, 0)].astype(jnp.float32)
    after = back_ref[jnp.minimum(me + 1, peers - 1)].astype(jnp.float32)
    row = lax.broadcasted_iota(jnp.int32, (clusters * nvec, width), 0)
    lane = lax.broadcasted_iota(jnp.int32, (clusters * nvec, width), 1)
    named = jnp.full((1, width), -1.0, jnp.float32)
    for i in range(2 * cap):
        k, alive = (i + 2 * cap, me > 0) if i < cap else (i, me < peers - 1)
        entry = jnp.where(alive, tile[k : k + 1], -1.0)
        named = jnp.where(lane[:1] // nvec == i, entry, named)
    match = (named == (row // nvec).astype(jnp.float32)) & (lane % nvec == row % nvec)
    match = jnp.where(match, 1.0, 0.0)[:, : 2 * each].astype(jnp.bfloat16)
    sides = jnp.concatenate(
        [
            jnp.concatenate([side[:each], side[each : 2 * each]], axis=1)
            for side in (before, after)
        ],
        axis=0,
    ).astype(jnp.bfloat16)
    total += jnp.dot(match, sides, preferred_element_type=jnp.float32)

    edges = []
    for side, alive, at in ((before, me > 0, (0, 0)), (after, me < peers - 1, (clusters - 1, 2))):
        edge = jnp.where(alive, side[2 * each :], 0.0).astype(jnp.bfloat16)
        edges.append(
            jnp.dot(edge, near_ref[at[0], at[1], width:, :], preferred_element_type=jnp.float32)
        )
    for s in range(clusters):
        part = total[s * nvec : (s + 1) * nvec]
        if s == 0:
            part += edges[0]
        if s == clusters - 1:
            part += edges[1]
        out_ref[s] = part


def cost(flops, moved):
    return pl.CostEstimate(flops=flops, bytes_accessed=moved, transcendentals=0)


def body(sources, near_blocks, far_u, far_v, send_list, far_slot, ret_list, ret_slot):
    clusters, nvec, leaf = sources.shape
    _, peers, cap = send_list.shape
    blocks, rank, _ = far_u.shape
    slots = peers * cap
    rows = 2 * cap * nvec + nvec
    params = pltpu.CompilerParams(vmem_limit_bytes=8 * 2**20)
    pattern = pl.pallas_call(
        pattern_kernel,
        out_shape=jax.ShapeDtypeStruct((nvec, leaf // 2), jnp.float32),
        out_specs=VMEM,
        compiler_params=params,
        cost_estimate=cost(10**10, nvec * leaf * 2),
        name="pattern",
    )()
    message = pl.pallas_call(
        pack_kernel,
        out_shape=jax.ShapeDtypeStruct((peers, rows, leaf // 2), jnp.bfloat16),
        in_specs=[VMEM] * 4,
        out_specs=VMEM,
        compiler_params=params,
        cost_estimate=cost(10**10, peers * rows * leaf),
        name="pack",
    )(send_list[0].T, ret_list[0].T, sources, pattern)
    incoming = lax.all_to_all(message, "clus", split_axis=0, concat_axis=0, tiled=True)
    few = slots <= 32
    if few:
        scratch = [
            pltpu.VMEM((slots * nvec, blocks * rank), jnp.bfloat16),
        ]
    else:
        scratch = [
            pltpu.VMEM((blocks * rank // leaf, nvec, leaf), jnp.float32),
            pltpu.VMEM((slots, nvec, leaf), jnp.float32),
        ]
    returns, near_part, place = pl.pallas_call(
        far_kernel if few else far_many_kernel,
        out_shape=(
            jax.ShapeDtypeStruct((peers, rows, leaf // 2), jnp.bfloat16),
            jax.ShapeDtypeStruct((clusters * nvec, leaf), jnp.float32),
            jax.ShapeDtypeStruct((clusters * nvec, slots * nvec), jnp.bfloat16),
        ),
        in_specs=[ANY, ANY] + [VMEM] * 6,
        out_specs=(VMEM, VMEM, VMEM),
        scratch_shapes=[
            pltpu.SMEM((blocks,), jnp.int32),
            pltpu.SMEM((blocks,), jnp.int32),
            pltpu.SemaphoreType.DMA((2,)),
            pltpu.VMEM((slots * nvec, leaf // 2), jnp.float32),
            pltpu.VMEM((slots, nvec, leaf), jnp.float32),
        ]
        + scratch,
        compiler_params=pltpu.CompilerParams(vmem_limit_bytes=16 * 2**20),
        cost_estimate=cost(4 * blocks * 8 * nvec * leaf * rank, 4 * blocks * rank * leaf),
        name="far",
    )(far_slot, ret_slot, incoming, far_u, far_v, sources, near_blocks, pattern)
    back = lax.all_to_all(returns, "clus", split_axis=0, concat_axis=0, tiled=True)
    return pl.pallas_call(
        sum_kernel,
        out_shape=jax.ShapeDtypeStruct((clusters, nvec, leaf), jnp.float32),
        in_specs=[VMEM] * 4,
        out_specs=VMEM,
        compiler_params=params,
        cost_estimate=cost(2 * clusters * nvec * slots * nvec * leaf, slots * nvec * leaf * 2),
        name="sum",
    )(back, near_part, place, near_blocks)


def solution(mesh):
    placed = (
        P(("groups", "clus"), None, None),
        P(("groups", "clus"), None, None, None),
        P(("groups", "clus"), None, None),
        P(("groups", "clus"), None, None),
        P(("groups", "clus"), None, None),
        P(("groups", "clus")),
        P(("groups", "clus"), None, None),
        P(("groups", "clus")),
    )
    return jax.shard_map(
        body,
        mesh=mesh,
        in_specs=placed,
        out_specs=P(("groups", "clus"), None, None),
        check_vma=False,
    )
```

```python
import jax
import jax.numpy as jnp
from jax import lax
from jax.experimental import pallas as pl
from jax.experimental.pallas import tpu as pltpu
from jax.sharding import PartitionSpec as P

VMEM = pl.BlockSpec(memory_space=pltpu.VMEM)
ANY = pl.BlockSpec(memory_space=pl.ANY)
CHUNKS = 16


def halves(x):
    w = x.shape[1] // 2
    return [x[:, :w], x[:, w:]]


def pattern_kernel(out_ref):
    nvec, width = out_ref.shape
    lane = lax.broadcasted_iota(jnp.int32, (nvec, width), 1)
    sub = lax.broadcasted_iota(jnp.int32, (nvec, width), 0)
    out_ref[...] = jnp.where(lane % nvec == sub, lane // nvec, -2).astype(jnp.float32)


def pack_kernel(send_ref, ret_ref, src_ref, pattern_ref, out_ref):
    clusters, nvec, leaf = src_ref.shape
    cap, peers = send_ref.shape
    me = lax.axis_index("clus")
    rows = peers * nvec
    peer = lax.broadcasted_iota(jnp.int32, (rows, peers), 0) // nvec
    kind = lax.broadcasted_iota(jnp.int32, (rows, peers), 0) % nvec // cap
    column = lax.broadcasted_iota(jnp.int32, (rows, peers), 1)

    def entries_at(list_ref, which):
        entries = list_ref[...].astype(jnp.float32).astype(jnp.bfloat16)
        return lax.dot_general(
            jnp.where(which == column, 1.0, 0.0).astype(jnp.bfloat16),
            entries,
            (((1,), (1,)), ((), ())),
            preferred_element_type=jnp.float32,
        )

    send = jnp.maximum(entries_at(send_ref, peer), 0.0)
    ret = entries_at(ret_ref, jnp.where(kind == 1, me - 1, jnp.where(kind == 2, me + 1, peer)))
    row = lax.broadcasted_iota(jnp.int32, (rows, clusters * nvec), 0)
    lane = lax.broadcasted_iota(jnp.int32, (rows, clusters * nvec), 1)
    cluster = jnp.where(row % nvec == lane % nvec, lane // nvec, -2).astype(jnp.float32)
    source = src_ref[...].reshape(clusters * nvec, leaf)
    picked = []
    for k in range(cap):
        pick = jnp.where(send[:, k : k + 1] == cluster, 1.0, 0.0).astype(jnp.bfloat16)
        picked.append(jnp.dot(pick, source, preferred_element_type=jnp.float32))
    vector = lax.broadcasted_iota(jnp.int32, (rows, leaf // 2), 0) % nvec
    places = jnp.broadcast_to(ret[:, :1], (rows, leaf // 2))
    for k in range(1, cap):
        places = jnp.where(vector % cap == k, ret[:, k : k + 1], places)
    first = src_ref[0].astype(jnp.float32)
    last = src_ref[clusters - 1].astype(jnp.float32)
    for p in range(peers):
        at = slice(p * nvec, (p + 1) * nvec)
        parts = []
        for k in range(cap):
            parts += halves(picked[k][at])
        edge = halves(jnp.where(p > me, last, first))[0]
        parts.append(jnp.where(jnp.abs(p - me) == 1, edge, places[at]))
        out_ref[p] = jnp.concatenate(parts, axis=0).astype(out_ref.dtype)


def joined(rows, nvec):
    return jnp.concatenate([rows[:nvec], rows[nvec:]], axis=1)


def load_slots(slots_any, dests_any, slot_ref, dest_ref, sems):
    copies = [
        pltpu.make_async_copy(slots_any, slot_ref, sems.at[0]),
        pltpu.make_async_copy(dests_any, dest_ref, sems.at[1]),
    ]
    for copy in copies:
        copy.start()
    return copies


def near_product(src_ref, near_ref, x_ref, near_out):
    clusters, nvec, leaf = src_ref.shape
    peers, rows, _ = x_ref.shape
    me = lax.axis_index("clus")
    before = x_ref[jnp.maximum(me - 1, 0)][rows - nvec :].astype(jnp.float32)
    after = x_ref[jnp.minimum(me + 1, peers - 1)][rows - nvec :].astype(jnp.float32)
    before = jnp.where(me > 0, before, 0.0)
    after = jnp.where(me < peers - 1, after, 0.0)
    before, after = [
        jnp.concatenate([x, jnp.zeros_like(x)], axis=1).astype(jnp.bfloat16)
        for x in (before, after)
    ]
    sources = [before] + [src_ref[s] for s in range(clusters)] + [after]
    for s in range(clusters):
        near_out[s * nvec : (s + 1) * nvec] = jnp.dot(
            jnp.concatenate(sources[s : s + 3], axis=1),
            near_ref[s].reshape(3 * leaf, leaf),
            preferred_element_type=jnp.float32,
        )


def placement(x_ref, pattern_ref, place, place_out):
    nvec, width = pattern_ref.shape
    peers, rows, _ = x_ref.shape
    cap = place.shape[0] // (peers * nvec)
    cluster = pattern_ref[...]
    me = lax.axis_index("clus")

    def step(p, carry):
        tile = x_ref[p, rows - nvec :, :].astype(jnp.float32)
        tile = jnp.where(jnp.abs(p - me) == 1, -1.0, tile)
        for k in range(cap):
            at = jnp.broadcast_to(tile[k : k + 1], (nvec, width))
            place[pl.ds((p * cap + k) * nvec, nvec)] = jnp.where(at == cluster, 1.0, 0.0)
        return carry

    lax.fori_loop(0, peers, step, 0, unroll=min(peers, 16))
    place_out[...] = place[...].T[: place_out.shape[0]].astype(jnp.bfloat16)


def widen_sources(x_ref, xf):
    peers = x_ref.shape[0]
    slots, nvec, _ = xf.shape
    cap = slots // peers

    def widen(p, carry):
        rows = x_ref[p].astype(jnp.float32)
        for k in range(cap):
            xf[p * cap + k] = joined(rows[2 * k * nvec : 2 * (k + 1) * nvec], nvec)
        return carry

    lax.fori_loop(0, peers, widen, 0, unroll=min(peers, 16))


def project(picked, u, owner, nvec, group):
    full = lax.dot_general(picked, u, (((1,), (1,)), ((), ())), preferred_element_type=jnp.float32)
    kept = full[:nvec]
    for i in range(1, group):
        kept = jnp.where(owner == i, full[i * nvec : (i + 1) * nvec], kept)
    return kept


def put_returns(total, x_ref, src_ref, out_ref):
    peers, rows, width = x_ref.shape
    clusters, nvec, _ = src_ref.shape
    each = total.shape[0] // peers
    cap = each // nvec
    me = lax.axis_index("clus")
    first = halves(src_ref[0].astype(jnp.float32))[1]
    last = halves(src_ref[clusters - 1].astype(jnp.float32))[1]
    sub = lax.broadcasted_iota(jnp.int32, (nvec, width), 0)
    for p in range(peers):
        before = x_ref[max(p - 1, 0), rows - nvec :, :].astype(jnp.float32)
        after = x_ref[min(p + 1, peers - 1), rows - nvec :, :].astype(jnp.float32)
        handed = jnp.where(sub // cap == 2, before, after)
        edge = jnp.where(p > me, last, first)
        parts = halves(total[p * each : (p + 1) * each])
        parts.append(jnp.where(jnp.abs(p - me) == 1, edge, handed))
        out_ref[p] = jnp.concatenate(parts, axis=0).astype(out_ref.dtype)


def far_kernel(
    slots_any,
    dests_any,
    x_ref,
    u_ref,
    v_ref,
    src_ref,
    near_ref,
    pattern_ref,
    out_ref,
    near_out,
    place_out,
    slot_ref,
    dest_ref,
    sems,
    place,
    xf,
    picked,
    acc,
):
    peers = x_ref.shape[0]
    slots, nvec, leaf = xf.shape
    blocks, rank, _ = u_ref.shape
    group = leaf // rank
    groups = blocks // group
    per = groups // CHUNKS
    copies = load_slots(slots_any, dests_any, slot_ref, dest_ref, sems)
    widen_sources(x_ref, xf)
    placement(x_ref, pattern_ref, place, place_out)
    for copy in copies:
        copy.wait()
    near_product(src_ref, near_ref, x_ref, near_out)
    for g in range(groups):
        rows = [xf[slot_ref[g * group + i]] for i in range(group)]
        picked[g] = jnp.concatenate(rows, axis=0).astype(jnp.bfloat16)
    owner = lax.broadcasted_iota(jnp.int32, (nvec, leaf), 1) // rank

    def coefficients(c):
        return [
            project(
                picked[g],
                u_ref[g * group : (g + 1) * group].reshape(leaf, leaf),
                owner,
                nvec,
                group,
            )
            for g in range(c * per, (c + 1) * per)
        ]

    acc[...] = jnp.zeros_like(acc)
    ahead = coefficients(0)
    for c in range(CHUNKS):
        now, ahead = ahead, coefficients(c + 1) if c + 1 < CHUNKS else None
        for g, kept in zip(range(c * per, (c + 1) * per), now):
            ats = [dest_ref[g * group + i] for i in range(group)]
            dest = jnp.full((nvec, leaf), ats[0], jnp.int32)
            for i in range(1, group):
                dest = jnp.where(owner == i, ats[i], dest)
            same = [jnp.where(dest == at, kept, 0.0) for at in ats]
            v = v_ref[g * group : (g + 1) * group].reshape(leaf, leaf)
            terms = jnp.dot(
                jnp.concatenate(same, axis=0).astype(jnp.bfloat16),
                v,
                preferred_element_type=jnp.float32,
            )
            sums = [acc[at] + terms[i * nvec : (i + 1) * nvec] for i, at in enumerate(ats)]
            for at, value in zip(ats, sums):
                acc[at] = value
    put_returns(acc[...].reshape(slots * nvec, leaf), x_ref, src_ref, out_ref)


def far_many_kernel(
    slots_any,
    dests_any,
    x_ref,
    u_ref,
    v_ref,
    src_ref,
    near_ref,
    pattern_ref,
    out_ref,
    near_out,
    place_out,
    slot_ref,
    dest_ref,
    sems,
    place,
    xf,
    coef,
    acc,
):
    slots, nvec, leaf = xf.shape
    blocks, rank, _ = u_ref.shape
    group = leaf // rank
    copies = load_slots(slots_any, dests_any, slot_ref, dest_ref, sems)
    widen_sources(x_ref, xf)
    placement(x_ref, pattern_ref, place, place_out)
    for copy in copies:
        copy.wait()
    near_product(src_ref, near_ref, x_ref, near_out)
    acc[...] = jnp.zeros_like(acc)
    owner = lax.broadcasted_iota(jnp.int32, (nvec, leaf), 1) // rank

    def forward(g, carry):
        rows = [xf[slot_ref[g * group + i]] for i in range(group)]
        picked = jnp.concatenate(rows, axis=0).astype(jnp.bfloat16)
        u = u_ref[pl.ds(g * group, group)].reshape(leaf, leaf)
        coef[g] = project(picked, u, owner, nvec, group)
        return carry

    def backward(g, carry):
        kept = coef[g]
        spread = jnp.concatenate(
            [jnp.where(owner == i, kept, 0.0) for i in range(group)], axis=0
        ).astype(jnp.bfloat16)
        v = v_ref[pl.ds(g * group, group)].reshape(leaf, leaf)
        terms = jnp.dot(spread, v, preferred_element_type=jnp.float32)
        for i in range(group):
            acc[dest_ref[g * group + i]] += terms[i * nvec : (i + 1) * nvec]
        return carry

    lax.fori_loop(0, blocks // group, forward, 0, unroll=4)
    lax.fori_loop(0, blocks // group, backward, 0, unroll=4)
    put_returns(acc[...].reshape(slots * nvec, leaf), x_ref, src_ref, out_ref)


def sum_kernel(back_ref, near_out_ref, place_ref, near_ref, out_ref):
    peers, rows, width = back_ref.shape
    clusters, nvec, leaf = out_ref.shape
    each = (rows - nvec) // 2
    cap = each // nvec
    me = lax.axis_index("clus")
    terms = jnp.concatenate(
        [back_ref[:, i * each : (i + 1) * each, :].reshape(peers * each, width) for i in range(2)],
        axis=1,
    )
    total = near_out_ref[...] + jnp.dot(
        place_ref[...], terms, preferred_element_type=jnp.float32
    )

    relay = jnp.where(me + 3 < peers, me + 3, me - 3)
    tile = back_ref[relay][rows - nvec :].astype(jnp.float32)
    before = back_ref[jnp.maximum(me - 1, 0)].astype(jnp.float32)
    after = back_ref[jnp.minimum(me + 1, peers - 1)].astype(jnp.float32)
    row = lax.broadcasted_iota(jnp.int32, (clusters * nvec, width), 0)
    lane = lax.broadcasted_iota(jnp.int32, (clusters * nvec, width), 1)
    named = jnp.full((1, width), -1.0, jnp.float32)
    for i in range(2 * cap):
        k, alive = (i + 2 * cap, me > 0) if i < cap else (i, me < peers - 1)
        entry = jnp.where(alive, tile[k : k + 1], -1.0)
        named = jnp.where(lane[:1] // nvec == i, entry, named)
    match = (named == (row // nvec).astype(jnp.float32)) & (lane % nvec == row % nvec)
    match = jnp.where(match, 1.0, 0.0)[:, : 2 * each].astype(jnp.bfloat16)
    sides = jnp.concatenate(
        [
            jnp.concatenate([side[:each], side[each : 2 * each]], axis=1)
            for side in (before, after)
        ],
        axis=0,
    ).astype(jnp.bfloat16)
    total += jnp.dot(match, sides, preferred_element_type=jnp.float32)

    edges = []
    for side, alive, at in ((before, me > 0, (0, 0)), (after, me < peers - 1, (clusters - 1, 2))):
        edge = jnp.where(alive, side[2 * each :], 0.0).astype(jnp.bfloat16)
        edges.append(
            jnp.dot(edge, near_ref[at[0], at[1], width:, :], preferred_element_type=jnp.float32)
        )
    for s in range(clusters):
        part = total[s * nvec : (s + 1) * nvec]
        if s == 0:
            part += edges[0]
        if s == clusters - 1:
            part += edges[1]
        out_ref[s] = part


def cost(flops, moved):
    return pl.CostEstimate(flops=flops, bytes_accessed=moved, transcendentals=0)


def body(sources, near_blocks, far_u, far_v, send_list, far_slot, ret_list, ret_slot):
    clusters, nvec, leaf = sources.shape
    _, peers, cap = send_list.shape
    blocks, rank, _ = far_u.shape
    slots = peers * cap
    rows = 2 * cap * nvec + nvec
    params = pltpu.CompilerParams(vmem_limit_bytes=8 * 2**20)
    pattern = pl.pallas_call(
        pattern_kernel,
        out_shape=jax.ShapeDtypeStruct((nvec, leaf // 2), jnp.float32),
        out_specs=VMEM,
        compiler_params=params,
        cost_estimate=cost(10**10, nvec * leaf * 2),
        name="pattern",
    )()
    message = pl.pallas_call(
        pack_kernel,
        out_shape=jax.ShapeDtypeStruct((peers, rows, leaf // 2), jnp.bfloat16),
        in_specs=[VMEM] * 4,
        out_specs=VMEM,
        compiler_params=params,
        cost_estimate=cost(10**10, peers * rows * leaf),
        name="pack",
    )(send_list[0].T, ret_list[0].T, sources, pattern)
    incoming = lax.all_to_all(message, "clus", split_axis=0, concat_axis=0, tiled=True)
    few = slots <= 32
    if few:
        scratch = [
            pltpu.VMEM((blocks * rank // leaf, leaf // rank * nvec, leaf), jnp.bfloat16),
            pltpu.VMEM((slots, nvec, leaf), jnp.float32),
        ]
    else:
        scratch = [
            pltpu.VMEM((blocks * rank // leaf, nvec, leaf), jnp.float32),
            pltpu.VMEM((slots, nvec, leaf), jnp.float32),
        ]
    returns, near_part, place = pl.pallas_call(
        far_kernel if few else far_many_kernel,
        out_shape=(
            jax.ShapeDtypeStruct((peers, rows, leaf // 2), jnp.bfloat16),
            jax.ShapeDtypeStruct((clusters * nvec, leaf), jnp.float32),
            jax.ShapeDtypeStruct((clusters * nvec, slots * nvec), jnp.bfloat16),
        ),
        in_specs=[ANY, ANY] + [VMEM] * 6,
        out_specs=(VMEM, VMEM, VMEM),
        scratch_shapes=[
            pltpu.SMEM((blocks,), jnp.int32),
            pltpu.SMEM((blocks,), jnp.int32),
            pltpu.SemaphoreType.DMA((2,)),
            pltpu.VMEM((slots * nvec, leaf // 2), jnp.float32),
            pltpu.VMEM((slots, nvec, leaf), jnp.float32),
        ]
        + scratch,
        compiler_params=pltpu.CompilerParams(vmem_limit_bytes=16 * 2**20),
        cost_estimate=cost(4 * blocks * 8 * nvec * leaf * rank, 4 * blocks * rank * leaf),
        name="far",
    )(far_slot, ret_slot, incoming, far_u, far_v, sources, near_blocks, pattern)
    back = lax.all_to_all(returns, "clus", split_axis=0, concat_axis=0, tiled=True)
    return pl.pallas_call(
        sum_kernel,
        out_shape=jax.ShapeDtypeStruct((clusters, nvec, leaf), jnp.float32),
        in_specs=[VMEM] * 4,
        out_specs=VMEM,
        compiler_params=params,
        cost_estimate=cost(2 * clusters * nvec * slots * nvec * leaf, slots * nvec * leaf * 2),
        name="sum",
    )(back, near_part, place, near_blocks)


def solution(mesh):
    placed = (
        P(("groups", "clus"), None, None),
        P(("groups", "clus"), None, None, None),
        P(("groups", "clus"), None, None),
        P(("groups", "clus"), None, None),
        P(("groups", "clus"), None, None),
        P(("groups", "clus")),
        P(("groups", "clus"), None, None),
        P(("groups", "clus")),
    )
    return jax.shard_map(
        body,
        mesh=mesh,
        in_specs=placed,
        out_specs=P(("groups", "clus"), None, None),
        check_vma=False,
    )
```

```python
import jax
import jax.numpy as jnp
from jax import lax
from jax.experimental import pallas as pl
from jax.experimental.pallas import tpu as pltpu
from jax.sharding import PartitionSpec as P

VMEM = pl.BlockSpec(memory_space=pltpu.VMEM)
ANY = pl.BlockSpec(memory_space=pl.ANY)


def halves(x):
    w = x.shape[1] // 2
    return [x[:, :w], x[:, w:]]


def pattern_kernel(out_ref):
    nvec, width = out_ref.shape
    lane = lax.broadcasted_iota(jnp.int32, (nvec, width), 1)
    sub = lax.broadcasted_iota(jnp.int32, (nvec, width), 0)
    out_ref[...] = jnp.where(lane % nvec == sub, lane // nvec, -2).astype(jnp.float32)


def pack_kernel(send_ref, ret_ref, src_ref, pattern_ref, out_ref):
    clusters, nvec, leaf = src_ref.shape
    cap, peers = send_ref.shape
    me = lax.axis_index("clus")
    rows = peers * nvec
    peer = lax.broadcasted_iota(jnp.int32, (rows, peers), 0) // nvec
    kind = lax.broadcasted_iota(jnp.int32, (rows, peers), 0) % nvec // cap
    column = lax.broadcasted_iota(jnp.int32, (rows, peers), 1)

    def entries_at(list_ref, which):
        entries = list_ref[...].astype(jnp.float32).astype(jnp.bfloat16)
        return lax.dot_general(
            jnp.where(which == column, 1.0, 0.0).astype(jnp.bfloat16),
            entries,
            (((1,), (1,)), ((), ())),
            preferred_element_type=jnp.float32,
        )

    send = jnp.maximum(entries_at(send_ref, peer), 0.0)
    ret = entries_at(ret_ref, jnp.where(kind == 1, me - 1, jnp.where(kind == 2, me + 1, peer)))
    row = lax.broadcasted_iota(jnp.int32, (rows, clusters * nvec), 0)
    lane = lax.broadcasted_iota(jnp.int32, (rows, clusters * nvec), 1)
    cluster = jnp.where(row % nvec == lane % nvec, lane // nvec, -2).astype(jnp.float32)
    source = src_ref[...].reshape(clusters * nvec, leaf)
    picked = []
    for k in range(cap):
        pick = jnp.where(send[:, k : k + 1] == cluster, 1.0, 0.0).astype(jnp.bfloat16)
        picked.append(jnp.dot(pick, source, preferred_element_type=jnp.float32))
    vector = lax.broadcasted_iota(jnp.int32, (rows, leaf // 2), 0) % nvec
    places = jnp.broadcast_to(ret[:, :1], (rows, leaf // 2))
    for k in range(1, cap):
        places = jnp.where(vector % cap == k, ret[:, k : k + 1], places)
    first = src_ref[0].astype(jnp.float32)
    last = src_ref[clusters - 1].astype(jnp.float32)
    for p in range(peers):
        at = slice(p * nvec, (p + 1) * nvec)
        parts = []
        for k in range(cap):
            parts += halves(picked[k][at])
        edge = halves(jnp.where(p > me, last, first))[0]
        parts.append(jnp.where(jnp.abs(p - me) == 1, edge, places[at]))
        out_ref[p] = jnp.concatenate(parts, axis=0).astype(out_ref.dtype)


def joined(rows, nvec):
    return jnp.concatenate([rows[:nvec], rows[nvec:]], axis=1)


def load_slots(slots_any, dests_any, slot_ref, dest_ref, sems):
    copies = [
        pltpu.make_async_copy(slots_any, slot_ref, sems.at[0]),
        pltpu.make_async_copy(dests_any, dest_ref, sems.at[1]),
    ]
    for copy in copies:
        copy.start()
    return copies


def near_product(src_ref, near_ref, x_ref, near_out):
    clusters, nvec, leaf = src_ref.shape
    peers, rows, _ = x_ref.shape
    me = lax.axis_index("clus")
    before = x_ref[jnp.maximum(me - 1, 0)][rows - nvec :].astype(jnp.float32)
    after = x_ref[jnp.minimum(me + 1, peers - 1)][rows - nvec :].astype(jnp.float32)
    before = jnp.where(me > 0, before, 0.0)
    after = jnp.where(me < peers - 1, after, 0.0)
    before, after = [
        jnp.concatenate([x, jnp.zeros_like(x)], axis=1).astype(jnp.bfloat16)
        for x in (before, after)
    ]
    sources = [before] + [src_ref[s] for s in range(clusters)] + [after]
    for s in range(clusters):
        near_out[s * nvec : (s + 1) * nvec] = jnp.dot(
            jnp.concatenate(sources[s : s + 3], axis=1),
            near_ref[s].reshape(3 * leaf, leaf),
            preferred_element_type=jnp.float32,
        )


def placement(x_ref, pattern_ref, place, place_out):
    nvec, width = pattern_ref.shape
    peers, rows, _ = x_ref.shape
    cap = place.shape[0] // (peers * nvec)
    cluster = pattern_ref[...]
    me = lax.axis_index("clus")

    def step(p, carry):
        tile = x_ref[p, rows - nvec :, :].astype(jnp.float32)
        tile = jnp.where(jnp.abs(p - me) == 1, -1.0, tile)
        for k in range(cap):
            at = jnp.broadcast_to(tile[k : k + 1], (nvec, width))
            place[pl.ds((p * cap + k) * nvec, nvec)] = jnp.where(at == cluster, 1.0, 0.0)
        return carry

    lax.fori_loop(0, peers, step, 0, unroll=min(peers, 16))
    place_out[...] = place[...].T[: place_out.shape[0]].astype(jnp.bfloat16)


def widen_sources(x_ref, xf):
    peers = x_ref.shape[0]
    slots, nvec, _ = xf.shape
    cap = slots // peers

    def widen(p, carry):
        rows = x_ref[p].astype(jnp.float32)
        for k in range(cap):
            xf[p * cap + k] = joined(rows[2 * k * nvec : 2 * (k + 1) * nvec], nvec)
        return carry

    lax.fori_loop(0, peers, widen, 0, unroll=min(peers, 16))


def project(picked, u, owner, nvec, group):
    full = lax.dot_general(picked, u, (((1,), (1,)), ((), ())), preferred_element_type=jnp.float32)
    kept = full[:nvec]
    for i in range(1, group):
        kept = jnp.where(owner == i, full[i * nvec : (i + 1) * nvec], kept)
    return kept


def put_returns(total, x_ref, src_ref, out_ref):
    peers, rows, width = x_ref.shape
    clusters, nvec, _ = src_ref.shape
    each = total.shape[0] // peers
    cap = each // nvec
    me = lax.axis_index("clus")
    first = halves(src_ref[0].astype(jnp.float32))[1]
    last = halves(src_ref[clusters - 1].astype(jnp.float32))[1]
    sub = lax.broadcasted_iota(jnp.int32, (nvec, width), 0)
    for p in range(peers):
        before = x_ref[max(p - 1, 0), rows - nvec :, :].astype(jnp.float32)
        after = x_ref[min(p + 1, peers - 1), rows - nvec :, :].astype(jnp.float32)
        handed = jnp.where(sub // cap == 2, before, after)
        edge = jnp.where(p > me, last, first)
        parts = halves(total[p * each : (p + 1) * each])
        parts.append(jnp.where(jnp.abs(p - me) == 1, edge, handed))
        out_ref[p] = jnp.concatenate(parts, axis=0).astype(out_ref.dtype)


def far_kernel(
    slots_any,
    dests_any,
    x_ref,
    u_ref,
    v_ref,
    src_ref,
    near_ref,
    pattern_ref,
    out_ref,
    near_out,
    place_out,
    slot_ref,
    dest_ref,
    sems,
    place,
    xf,
    picked,
    acc,
):
    peers = x_ref.shape[0]
    slots, nvec, leaf = xf.shape
    blocks, rank, _ = u_ref.shape
    group = leaf // rank
    groups = blocks // group
    copies = load_slots(slots_any, dests_any, slot_ref, dest_ref, sems)
    widen_sources(x_ref, xf)
    placement(x_ref, pattern_ref, place, place_out)
    for copy in copies:
        copy.wait()
    near_product(src_ref, near_ref, x_ref, near_out)
    for g in range(groups):
        rows = [xf[slot_ref[g * group + i]] for i in range(group)]
        picked[g] = jnp.concatenate(rows, axis=0).astype(jnp.bfloat16)
    owner = lax.broadcasted_iota(jnp.int32, (nvec, leaf), 1) // rank

    def coefficients(g):
        u = u_ref[g * group : (g + 1) * group].reshape(leaf, leaf)
        return project(picked[g], u, owner, nvec, group)

    def contributions(g, kept, ats):
        dest = jnp.full((nvec, leaf), ats[0], jnp.int32)
        for i in range(1, group):
            dest = jnp.where(owner == i, ats[i], dest)
        same = [jnp.where(dest == at, kept, 0.0) for at in ats]
        return jnp.dot(
            jnp.concatenate(same, axis=0).astype(jnp.bfloat16),
            v_ref[g * group : (g + 1) * group].reshape(leaf, leaf),
            preferred_element_type=jnp.float32,
        )

    def accumulate(terms, ats):
        sums = [acc[at] + terms[i * nvec : (i + 1) * nvec] for i, at in enumerate(ats)]
        for at, value in zip(ats, sums):
            acc[at] = value

    acc[...] = jnp.zeros_like(acc)
    kept, late = coefficients(0), None
    for g in range(groups):
        ahead = coefficients(g + 1) if g + 1 < groups else None
        ats = [dest_ref[g * group + i] for i in range(group)]
        terms = contributions(g, kept, ats)
        if late is not None:
            accumulate(*late)
        kept, late = ahead, (terms, ats)
    accumulate(*late)
    put_returns(acc[...].reshape(slots * nvec, leaf), x_ref, src_ref, out_ref)


def sum_kernel(back_ref, near_out_ref, place_ref, near_ref, out_ref):
    peers, rows, width = back_ref.shape
    clusters, nvec, leaf = out_ref.shape
    each = (rows - nvec) // 2
    cap = each // nvec
    me = lax.axis_index("clus")
    terms = jnp.concatenate(
        [back_ref[:, i * each : (i + 1) * each, :].reshape(peers * each, width) for i in range(2)],
        axis=1,
    )
    total = near_out_ref[...] + jnp.dot(
        place_ref[...], terms, preferred_element_type=jnp.float32
    )

    relay = jnp.where(me + 3 < peers, me + 3, me - 3)
    tile = back_ref[relay][rows - nvec :].astype(jnp.float32)
    before = back_ref[jnp.maximum(me - 1, 0)].astype(jnp.float32)
    after = back_ref[jnp.minimum(me + 1, peers - 1)].astype(jnp.float32)
    row = lax.broadcasted_iota(jnp.int32, (clusters * nvec, width), 0)
    lane = lax.broadcasted_iota(jnp.int32, (clusters * nvec, width), 1)
    named = jnp.full((1, width), -1.0, jnp.float32)
    for i in range(2 * cap):
        k, alive = (i + 2 * cap, me > 0) if i < cap else (i, me < peers - 1)
        entry = jnp.where(alive, tile[k : k + 1], -1.0)
        named = jnp.where(lane[:1] // nvec == i, entry, named)
    match = (named == (row // nvec).astype(jnp.float32)) & (lane % nvec == row % nvec)
    match = jnp.where(match, 1.0, 0.0)[:, : 2 * each].astype(jnp.bfloat16)
    sides = jnp.concatenate(
        [
            jnp.concatenate([side[:each], side[each : 2 * each]], axis=1)
            for side in (before, after)
        ],
        axis=0,
    ).astype(jnp.bfloat16)
    total += jnp.dot(match, sides, preferred_element_type=jnp.float32)

    edges = []
    for side, alive, at in ((before, me > 0, (0, 0)), (after, me < peers - 1, (clusters - 1, 2))):
        edge = jnp.where(alive, side[2 * each :], 0.0).astype(jnp.bfloat16)
        edges.append(
            jnp.dot(edge, near_ref[at[0], at[1], width:, :], preferred_element_type=jnp.float32)
        )
    for s in range(clusters):
        part = total[s * nvec : (s + 1) * nvec]
        if s == 0:
            part += edges[0]
        if s == clusters - 1:
            part += edges[1]
        out_ref[s] = part


def cost(flops, moved):
    return pl.CostEstimate(flops=flops, bytes_accessed=moved, transcendentals=0)


def body(sources, near_blocks, far_u, far_v, send_list, far_slot, ret_list, ret_slot):
    clusters, nvec, leaf = sources.shape
    _, peers, cap = send_list.shape
    blocks, rank, _ = far_u.shape
    slots = peers * cap
    rows = 2 * cap * nvec + nvec
    params = pltpu.CompilerParams(vmem_limit_bytes=8 * 2**20)
    pattern = pl.pallas_call(
        pattern_kernel,
        out_shape=jax.ShapeDtypeStruct((nvec, leaf // 2), jnp.float32),
        out_specs=VMEM,
        compiler_params=params,
        cost_estimate=cost(10**10, nvec * leaf * 2),
        name="pattern",
    )()
    message = pl.pallas_call(
        pack_kernel,
        out_shape=jax.ShapeDtypeStruct((peers, rows, leaf // 2), jnp.bfloat16),
        in_specs=[VMEM] * 4,
        out_specs=VMEM,
        compiler_params=params,
        cost_estimate=cost(10**10, peers * rows * leaf),
        name="pack",
    )(send_list[0].T, ret_list[0].T, sources, pattern)
    incoming = lax.all_to_all(message, "clus", split_axis=0, concat_axis=0, tiled=True)
    returns, near_part, place = pl.pallas_call(
        far_kernel,
        out_shape=(
            jax.ShapeDtypeStruct((peers, rows, leaf // 2), jnp.bfloat16),
            jax.ShapeDtypeStruct((clusters * nvec, leaf), jnp.float32),
            jax.ShapeDtypeStruct((clusters * nvec, slots * nvec), jnp.bfloat16),
        ),
        in_specs=[ANY, ANY] + [VMEM] * 6,
        out_specs=(VMEM, VMEM, VMEM),
        scratch_shapes=[
            pltpu.SMEM((blocks,), jnp.int32),
            pltpu.SMEM((blocks,), jnp.int32),
            pltpu.SemaphoreType.DMA((2,)),
            pltpu.VMEM((slots * nvec, leaf // 2), jnp.float32),
            pltpu.VMEM((slots, nvec, leaf), jnp.float32),
            pltpu.VMEM((blocks * rank // leaf, leaf // rank * nvec, leaf), jnp.bfloat16),
            pltpu.VMEM((slots, nvec, leaf), jnp.float32),
        ],
        compiler_params=pltpu.CompilerParams(vmem_limit_bytes=16 * 2**20),
        cost_estimate=cost(4 * blocks * 8 * nvec * leaf * rank, 4 * blocks * rank * leaf),
        name="far",
    )(far_slot, ret_slot, incoming, far_u, far_v, sources, near_blocks, pattern)
    back = lax.all_to_all(returns, "clus", split_axis=0, concat_axis=0, tiled=True)
    return pl.pallas_call(
        sum_kernel,
        out_shape=jax.ShapeDtypeStruct((clusters, nvec, leaf), jnp.float32),
        in_specs=[VMEM] * 4,
        out_specs=VMEM,
        compiler_params=params,
        cost_estimate=cost(2 * clusters * nvec * slots * nvec * leaf, slots * nvec * leaf * 2),
        name="sum",
    )(back, near_part, place, near_blocks)


def solution(mesh):
    placed = (
        P(("groups", "clus"), None, None),
        P(("groups", "clus"), None, None, None),
        P(("groups", "clus"), None, None),
        P(("groups", "clus"), None, None),
        P(("groups", "clus"), None, None),
        P(("groups", "clus")),
        P(("groups", "clus"), None, None),
        P(("groups", "clus")),
    )
    return jax.shard_map(
        body,
        mesh=mesh,
        in_specs=placed,
        out_specs=P(("groups", "clus"), None, None),
        check_vma=False,
    )
```

```python
import jax
import jax.numpy as jnp
from jax import lax
from jax.experimental import pallas as pl
from jax.experimental.pallas import tpu as pltpu
from jax.sharding import PartitionSpec as P

VMEM = pl.BlockSpec(memory_space=pltpu.VMEM)
CHUNK = 4
ANY = pl.BlockSpec(memory_space=pl.ANY)


def halves(x):
    w = x.shape[1] // 2
    return [x[:, :w], x[:, w:]]


def pattern_kernel(out_ref):
    nvec, width = out_ref.shape
    lane = lax.broadcasted_iota(jnp.int32, (nvec, width), 1)
    sub = lax.broadcasted_iota(jnp.int32, (nvec, width), 0)
    out_ref[...] = jnp.where(lane % nvec == sub, lane // nvec, -2).astype(jnp.float32)


def pack_kernel(send_ref, ret_ref, src_ref, pattern_ref, out_ref):
    clusters, nvec, leaf = src_ref.shape
    cap, peers = send_ref.shape
    me = lax.axis_index("clus")
    rows = peers * nvec
    peer = lax.broadcasted_iota(jnp.int32, (rows, peers), 0) // nvec
    kind = lax.broadcasted_iota(jnp.int32, (rows, peers), 0) % nvec // cap
    column = lax.broadcasted_iota(jnp.int32, (rows, peers), 1)

    def entries_at(list_ref, which):
        entries = list_ref[...].astype(jnp.float32).astype(jnp.bfloat16)
        return lax.dot_general(
            jnp.where(which == column, 1.0, 0.0).astype(jnp.bfloat16),
            entries,
            (((1,), (1,)), ((), ())),
            preferred_element_type=jnp.float32,
        )

    send = jnp.maximum(entries_at(send_ref, peer), 0.0)
    ret = entries_at(ret_ref, jnp.where(kind == 1, me - 1, jnp.where(kind == 2, me + 1, peer)))
    row = lax.broadcasted_iota(jnp.int32, (rows, clusters * nvec), 0)
    lane = lax.broadcasted_iota(jnp.int32, (rows, clusters * nvec), 1)
    cluster = jnp.where(row % nvec == lane % nvec, lane // nvec, -2).astype(jnp.float32)
    source = src_ref[...].reshape(clusters * nvec, leaf)
    picked = []
    for k in range(cap):
        pick = jnp.where(send[:, k : k + 1] == cluster, 1.0, 0.0).astype(jnp.bfloat16)
        picked.append(jnp.dot(pick, source, preferred_element_type=jnp.float32))
    vector = lax.broadcasted_iota(jnp.int32, (rows, leaf // 2), 0) % nvec
    places = jnp.broadcast_to(ret[:, :1], (rows, leaf // 2))
    for k in range(1, cap):
        places = jnp.where(vector % cap == k, ret[:, k : k + 1], places)
    first = src_ref[0].astype(jnp.float32)
    last = src_ref[clusters - 1].astype(jnp.float32)
    for p in range(peers):
        at = slice(p * nvec, (p + 1) * nvec)
        parts = []
        for k in range(cap):
            parts += halves(picked[k][at])
        edge = halves(jnp.where(p > me, last, first))[0]
        parts.append(jnp.where(jnp.abs(p - me) == 1, edge, places[at]))
        out_ref[p] = jnp.concatenate(parts, axis=0).astype(out_ref.dtype)


def joined(rows, nvec):
    return jnp.concatenate([rows[:nvec], rows[nvec:]], axis=1)


def load_slots(slots_any, dests_any, slot_ref, dest_ref, sems):
    copies = [
        pltpu.make_async_copy(slots_any, slot_ref, sems.at[0]),
        pltpu.make_async_copy(dests_any, dest_ref, sems.at[1]),
    ]
    for copy in copies:
        copy.start()
    return copies


def near_product(src_ref, near_ref, x_ref, near_out):
    clusters, nvec, leaf = src_ref.shape
    peers, rows, _ = x_ref.shape
    me = lax.axis_index("clus")
    before = x_ref[jnp.maximum(me - 1, 0)][rows - nvec :].astype(jnp.float32)
    after = x_ref[jnp.minimum(me + 1, peers - 1)][rows - nvec :].astype(jnp.float32)
    before = jnp.where(me > 0, before, 0.0)
    after = jnp.where(me < peers - 1, after, 0.0)
    before, after = [
        jnp.concatenate([x, jnp.zeros_like(x)], axis=1).astype(jnp.bfloat16)
        for x in (before, after)
    ]
    sources = [before] + [src_ref[s] for s in range(clusters)] + [after]
    for s in range(clusters):
        near_out[s * nvec : (s + 1) * nvec] = jnp.dot(
            jnp.concatenate(sources[s : s + 3], axis=1),
            near_ref[s].reshape(3 * leaf, leaf),
            preferred_element_type=jnp.float32,
        )


def placement(x_ref, pattern_ref, place, place_out):
    nvec, width = pattern_ref.shape
    peers, rows, _ = x_ref.shape
    cap = place.shape[0] // (peers * nvec)
    cluster = pattern_ref[...]
    me = lax.axis_index("clus")

    def step(p, carry):
        tile = x_ref[p, rows - nvec :, :].astype(jnp.float32)
        tile = jnp.where(jnp.abs(p - me) == 1, -1.0, tile)
        for k in range(cap):
            at = jnp.broadcast_to(tile[k : k + 1], (nvec, width))
            place[pl.ds((p * cap + k) * nvec, nvec)] = jnp.where(at == cluster, 1.0, 0.0)
        return carry

    lax.fori_loop(0, peers, step, 0, unroll=min(peers, 16))
    place_out[...] = place[...].T[: place_out.shape[0]].astype(jnp.bfloat16)


def widen_sources(x_ref, xf):
    peers = x_ref.shape[0]
    slots, nvec, _ = xf.shape
    cap = slots // peers

    def widen(p, carry):
        rows = x_ref[p].astype(jnp.float32)
        for k in range(cap):
            xf[p * cap + k] = joined(rows[2 * k * nvec : 2 * (k + 1) * nvec], nvec)
        return carry

    lax.fori_loop(0, peers, widen, 0, unroll=min(peers, 16))


def project(picked, u, owner, nvec, group):
    full = lax.dot_general(picked, u, (((1,), (1,)), ((), ())), preferred_element_type=jnp.float32)
    kept = full[:nvec]
    for i in range(1, group):
        kept = jnp.where(owner == i, full[i * nvec : (i + 1) * nvec], kept)
    return kept


def put_returns(total, x_ref, src_ref, out_ref):
    peers, rows, width = x_ref.shape
    clusters, nvec, _ = src_ref.shape
    each = total.shape[0] // peers
    cap = each // nvec
    me = lax.axis_index("clus")
    first = halves(src_ref[0].astype(jnp.float32))[1]
    last = halves(src_ref[clusters - 1].astype(jnp.float32))[1]
    sub = lax.broadcasted_iota(jnp.int32, (nvec, width), 0)
    for p in range(peers):
        before = x_ref[max(p - 1, 0), rows - nvec :, :].astype(jnp.float32)
        after = x_ref[min(p + 1, peers - 1), rows - nvec :, :].astype(jnp.float32)
        handed = jnp.where(sub // cap == 2, before, after)
        edge = jnp.where(p > me, last, first)
        parts = halves(total[p * each : (p + 1) * each])
        parts.append(jnp.where(jnp.abs(p - me) == 1, edge, handed))
        out_ref[p] = jnp.concatenate(parts, axis=0).astype(out_ref.dtype)


def far_kernel(
    slots_any,
    dests_any,
    x_ref,
    u_ref,
    v_ref,
    src_ref,
    near_ref,
    pattern_ref,
    out_ref,
    near_out,
    place_out,
    slot_ref,
    dest_ref,
    sems,
    place,
    xf,
    picked,
    acc,
):
    peers = x_ref.shape[0]
    slots, nvec, leaf = xf.shape
    blocks, rank, _ = u_ref.shape
    group = leaf // rank
    groups = blocks // group
    copies = load_slots(slots_any, dests_any, slot_ref, dest_ref, sems)
    widen_sources(x_ref, xf)
    placement(x_ref, pattern_ref, place, place_out)
    for copy in copies:
        copy.wait()
    near_product(src_ref, near_ref, x_ref, near_out)
    for g in range(groups):
        rows = [xf[slot_ref[g * group + i]] for i in range(group)]
        picked[g] = jnp.concatenate(rows, axis=0).astype(jnp.bfloat16)
    owner = lax.broadcasted_iota(jnp.int32, (nvec, leaf), 1) // rank

    def coefficients(g):
        u = u_ref[g * group : (g + 1) * group].reshape(leaf, leaf)
        return project(picked[g], u, owner, nvec, group)

    def contributions(g, kept, ats):
        dest = jnp.full((nvec, leaf), ats[0], jnp.int32)
        for i in range(1, group):
            dest = jnp.where(owner == i, ats[i], dest)
        same = [jnp.where(dest == at, kept, 0.0) for at in ats]
        return jnp.dot(
            jnp.concatenate(same, axis=0).astype(jnp.bfloat16),
            v_ref[g * group : (g + 1) * group].reshape(leaf, leaf),
            preferred_element_type=jnp.float32,
        )

    def accumulate(terms, ats):
        sums = [acc[at] + terms[i * nvec : (i + 1) * nvec] for i, at in enumerate(ats)]
        for at, value in zip(ats, sums):
            acc[at] = value

    acc[...] = jnp.zeros_like(acc)
    chunks = [range(first, min(first + CHUNK, groups)) for first in range(0, groups, CHUNK)]
    ahead = [coefficients(g) for g in chunks[0]]
    for c, chunk in enumerate(chunks):
        kept = ahead
        if c + 1 < len(chunks):
            ahead = [coefficients(g) for g in chunks[c + 1]]
        ats = [[dest_ref[g * group + i] for i in range(group)] for g in chunk]
        terms = [contributions(g, k, at) for g, k, at in zip(chunk, kept, ats)]
        for term, at in zip(terms, ats):
            accumulate(term, at)
    put_returns(acc[...].reshape(slots * nvec, leaf), x_ref, src_ref, out_ref)


def sum_kernel(back_ref, near_out_ref, place_ref, near_ref, out_ref):
    peers, rows, width = back_ref.shape
    clusters, nvec, leaf = out_ref.shape
    each = (rows - nvec) // 2
    cap = each // nvec
    me = lax.axis_index("clus")
    terms = jnp.concatenate(
        [back_ref[:, i * each : (i + 1) * each, :].reshape(peers * each, width) for i in range(2)],
        axis=1,
    )
    total = near_out_ref[...] + jnp.dot(
        place_ref[...], terms, preferred_element_type=jnp.float32
    )

    relay = jnp.where(me + 3 < peers, me + 3, me - 3)
    tile = back_ref[relay][rows - nvec :].astype(jnp.float32)
    before = back_ref[jnp.maximum(me - 1, 0)].astype(jnp.float32)
    after = back_ref[jnp.minimum(me + 1, peers - 1)].astype(jnp.float32)
    row = lax.broadcasted_iota(jnp.int32, (clusters * nvec, width), 0)
    lane = lax.broadcasted_iota(jnp.int32, (clusters * nvec, width), 1)
    named = jnp.full((1, width), -1.0, jnp.float32)
    for i in range(2 * cap):
        k, alive = (i + 2 * cap, me > 0) if i < cap else (i, me < peers - 1)
        entry = jnp.where(alive, tile[k : k + 1], -1.0)
        named = jnp.where(lane[:1] // nvec == i, entry, named)
    match = (named == (row // nvec).astype(jnp.float32)) & (lane % nvec == row % nvec)
    match = jnp.where(match, 1.0, 0.0)[:, : 2 * each].astype(jnp.bfloat16)
    sides = jnp.concatenate(
        [
            jnp.concatenate([side[:each], side[each : 2 * each]], axis=1)
            for side in (before, after)
        ],
        axis=0,
    ).astype(jnp.bfloat16)
    total += jnp.dot(match, sides, preferred_element_type=jnp.float32)

    edges = []
    for side, alive, at in ((before, me > 0, (0, 0)), (after, me < peers - 1, (clusters - 1, 2))):
        edge = jnp.where(alive, side[2 * each :], 0.0).astype(jnp.bfloat16)
        edges.append(
            jnp.dot(edge, near_ref[at[0], at[1], width:, :], preferred_element_type=jnp.float32)
        )
    for s in range(clusters):
        part = total[s * nvec : (s + 1) * nvec]
        if s == 0:
            part += edges[0]
        if s == clusters - 1:
            part += edges[1]
        out_ref[s] = part


def cost(flops, moved):
    return pl.CostEstimate(flops=flops, bytes_accessed=moved, transcendentals=0)


def body(sources, near_blocks, far_u, far_v, send_list, far_slot, ret_list, ret_slot):
    clusters, nvec, leaf = sources.shape
    _, peers, cap = send_list.shape
    blocks, rank, _ = far_u.shape
    slots = peers * cap
    rows = 2 * cap * nvec + nvec
    params = pltpu.CompilerParams(vmem_limit_bytes=8 * 2**20)
    pattern = pl.pallas_call(
        pattern_kernel,
        out_shape=jax.ShapeDtypeStruct((nvec, leaf // 2), jnp.float32),
        out_specs=VMEM,
        compiler_params=params,
        cost_estimate=cost(10**10, nvec * leaf * 2),
        name="pattern",
    )()
    message = pl.pallas_call(
        pack_kernel,
        out_shape=jax.ShapeDtypeStruct((peers, rows, leaf // 2), jnp.bfloat16),
        in_specs=[VMEM] * 4,
        out_specs=VMEM,
        compiler_params=params,
        cost_estimate=cost(10**10, peers * rows * leaf),
        name="pack",
    )(send_list[0].T, ret_list[0].T, sources, pattern)
    incoming = lax.all_to_all(message, "clus", split_axis=0, concat_axis=0, tiled=True)
    returns, near_part, place = pl.pallas_call(
        far_kernel,
        out_shape=(
            jax.ShapeDtypeStruct((peers, rows, leaf // 2), jnp.bfloat16),
            jax.ShapeDtypeStruct((clusters * nvec, leaf), jnp.float32),
            jax.ShapeDtypeStruct((clusters * nvec, slots * nvec), jnp.bfloat16),
        ),
        in_specs=[ANY, ANY] + [VMEM] * 6,
        out_specs=(VMEM, VMEM, VMEM),
        scratch_shapes=[
            pltpu.SMEM((blocks,), jnp.int32),
            pltpu.SMEM((blocks,), jnp.int32),
            pltpu.SemaphoreType.DMA((2,)),
            pltpu.VMEM((slots * nvec, leaf // 2), jnp.float32),
            pltpu.VMEM((slots, nvec, leaf), jnp.float32),
            pltpu.VMEM((blocks * rank // leaf, leaf // rank * nvec, leaf), jnp.bfloat16),
            pltpu.VMEM((slots, nvec, leaf), jnp.float32),
        ],
        compiler_params=pltpu.CompilerParams(vmem_limit_bytes=16 * 2**20),
        cost_estimate=cost(4 * blocks * 8 * nvec * leaf * rank, 4 * blocks * rank * leaf),
        name="far",
    )(far_slot, ret_slot, incoming, far_u, far_v, sources, near_blocks, pattern)
    back = lax.all_to_all(returns, "clus", split_axis=0, concat_axis=0, tiled=True)
    return pl.pallas_call(
        sum_kernel,
        out_shape=jax.ShapeDtypeStruct((clusters, nvec, leaf), jnp.float32),
        in_specs=[VMEM] * 4,
        out_specs=VMEM,
        compiler_params=params,
        cost_estimate=cost(2 * clusters * nvec * slots * nvec * leaf, slots * nvec * leaf * 2),
        name="sum",
    )(back, near_part, place, near_blocks)


def solution(mesh):
    placed = (
        P(("groups", "clus"), None, None),
        P(("groups", "clus"), None, None, None),
        P(("groups", "clus"), None, None),
        P(("groups", "clus"), None, None),
        P(("groups", "clus"), None, None),
        P(("groups", "clus")),
        P(("groups", "clus"), None, None),
        P(("groups", "clus")),
    )
    return jax.shard_map(
        body,
        mesh=mesh,
        in_specs=placed,
        out_specs=P(("groups", "clus"), None, None),
        check_vma=False,
    )
```

```python
import jax
import jax.numpy as jnp
from jax import lax
from jax.experimental import pallas as pl
from jax.experimental.pallas import tpu as pltpu
from jax.sharding import PartitionSpec as P

VMEM = pl.BlockSpec(memory_space=pltpu.VMEM)
CHUNK = 8
ANY = pl.BlockSpec(memory_space=pl.ANY)


def halves(x):
    w = x.shape[1] // 2
    return [x[:, :w], x[:, w:]]


def pattern_kernel(out_ref):
    nvec, width = out_ref.shape
    lane = lax.broadcasted_iota(jnp.int32, (nvec, width), 1)
    sub = lax.broadcasted_iota(jnp.int32, (nvec, width), 0)
    out_ref[...] = jnp.where(lane % nvec == sub, lane // nvec, -2).astype(jnp.float32)


def pack_kernel(send_ref, ret_ref, src_ref, pattern_ref, out_ref):
    clusters, nvec, leaf = src_ref.shape
    cap, peers = send_ref.shape
    me = lax.axis_index("clus")
    rows = peers * nvec
    peer = lax.broadcasted_iota(jnp.int32, (rows, peers), 0) // nvec
    kind = lax.broadcasted_iota(jnp.int32, (rows, peers), 0) % nvec // cap
    column = lax.broadcasted_iota(jnp.int32, (rows, peers), 1)

    def entries_at(list_ref, which):
        entries = list_ref[...].astype(jnp.float32).astype(jnp.bfloat16)
        return lax.dot_general(
            jnp.where(which == column, 1.0, 0.0).astype(jnp.bfloat16),
            entries,
            (((1,), (1,)), ((), ())),
            preferred_element_type=jnp.float32,
        )

    send = jnp.maximum(entries_at(send_ref, peer), 0.0)
    ret = entries_at(ret_ref, jnp.where(kind == 1, me - 1, jnp.where(kind == 2, me + 1, peer)))
    row = lax.broadcasted_iota(jnp.int32, (rows, clusters * nvec), 0)
    lane = lax.broadcasted_iota(jnp.int32, (rows, clusters * nvec), 1)
    cluster = jnp.where(row % nvec == lane % nvec, lane // nvec, -2).astype(jnp.float32)
    source = src_ref[...].reshape(clusters * nvec, leaf)
    picked = []
    for k in range(cap):
        pick = jnp.where(send[:, k : k + 1] == cluster, 1.0, 0.0).astype(jnp.bfloat16)
        picked.append(jnp.dot(pick, source, preferred_element_type=jnp.float32))
    vector = lax.broadcasted_iota(jnp.int32, (rows, leaf // 2), 0) % nvec
    places = jnp.broadcast_to(ret[:, :1], (rows, leaf // 2))
    for k in range(1, cap):
        places = jnp.where(vector % cap == k, ret[:, k : k + 1], places)
    first = src_ref[0].astype(jnp.float32)
    last = src_ref[clusters - 1].astype(jnp.float32)
    for p in range(peers):
        at = slice(p * nvec, (p + 1) * nvec)
        parts = []
        for k in range(cap):
            parts += halves(picked[k][at])
        edge = halves(jnp.where(p > me, last, first))[0]
        parts.append(jnp.where(jnp.abs(p - me) == 1, edge, places[at]))
        out_ref[p] = jnp.concatenate(parts, axis=0).astype(out_ref.dtype)


def joined(rows, nvec):
    return jnp.concatenate([rows[:nvec], rows[nvec:]], axis=1)


def load_slots(slots_any, dests_any, slot_ref, dest_ref, sems):
    copies = [
        pltpu.make_async_copy(slots_any, slot_ref, sems.at[0]),
        pltpu.make_async_copy(dests_any, dest_ref, sems.at[1]),
    ]
    for copy in copies:
        copy.start()
    return copies


def near_product(src_ref, near_ref, x_ref, near_out):
    clusters, nvec, leaf = src_ref.shape
    peers, rows, _ = x_ref.shape
    me = lax.axis_index("clus")
    before = x_ref[jnp.maximum(me - 1, 0)][rows - nvec :].astype(jnp.float32)
    after = x_ref[jnp.minimum(me + 1, peers - 1)][rows - nvec :].astype(jnp.float32)
    before = jnp.where(me > 0, before, 0.0)
    after = jnp.where(me < peers - 1, after, 0.0)
    before, after = [
        jnp.concatenate([x, jnp.zeros_like(x)], axis=1).astype(jnp.bfloat16)
        for x in (before, after)
    ]
    sources = [before] + [src_ref[s] for s in range(clusters)] + [after]
    for s in range(clusters):
        near_out[s * nvec : (s + 1) * nvec] = jnp.dot(
            jnp.concatenate(sources[s : s + 3], axis=1),
            near_ref[s].reshape(3 * leaf, leaf),
            preferred_element_type=jnp.float32,
        )


def placement(x_ref, pattern_ref, place, place_out):
    nvec, width = pattern_ref.shape
    peers, rows, _ = x_ref.shape
    cap = place.shape[0] // (peers * nvec)
    cluster = pattern_ref[...]
    me = lax.axis_index("clus")

    def step(p, carry):
        tile = x_ref[p, rows - nvec :, :].astype(jnp.float32)
        tile = jnp.where(jnp.abs(p - me) == 1, -1.0, tile)
        for k in range(cap):
            at = jnp.broadcast_to(tile[k : k + 1], (nvec, width))
            place[pl.ds((p * cap + k) * nvec, nvec)] = jnp.where(at == cluster, 1.0, 0.0)
        return carry

    lax.fori_loop(0, peers, step, 0, unroll=min(peers, 16))
    place_out[...] = place[...].T[: place_out.shape[0]].astype(jnp.bfloat16)


def widen_sources(x_ref, xf):
    peers = x_ref.shape[0]
    slots, nvec, _ = xf.shape
    cap = slots // peers

    def widen(p, carry):
        rows = x_ref[p].astype(jnp.float32)
        for k in range(cap):
            xf[p * cap + k] = joined(rows[2 * k * nvec : 2 * (k + 1) * nvec], nvec)
        return carry

    lax.fori_loop(0, peers, widen, 0, unroll=min(peers, 16))


def project(picked, u, owner, nvec, group):
    full = lax.dot_general(picked, u, (((1,), (1,)), ((), ())), preferred_element_type=jnp.float32)
    kept = full[:nvec]
    for i in range(1, group):
        kept = jnp.where(owner == i, full[i * nvec : (i + 1) * nvec], kept)
    return kept


def put_returns(total, x_ref, src_ref, out_ref):
    peers, rows, width = x_ref.shape
    clusters, nvec, _ = src_ref.shape
    each = total.shape[0] // peers
    cap = each // nvec
    me = lax.axis_index("clus")
    first = halves(src_ref[0].astype(jnp.float32))[1]
    last = halves(src_ref[clusters - 1].astype(jnp.float32))[1]
    sub = lax.broadcasted_iota(jnp.int32, (nvec, width), 0)
    for p in range(peers):
        before = x_ref[max(p - 1, 0), rows - nvec :, :].astype(jnp.float32)
        after = x_ref[min(p + 1, peers - 1), rows - nvec :, :].astype(jnp.float32)
        handed = jnp.where(sub // cap == 2, before, after)
        edge = jnp.where(p > me, last, first)
        parts = halves(total[p * each : (p + 1) * each])
        parts.append(jnp.where(jnp.abs(p - me) == 1, edge, handed))
        out_ref[p] = jnp.concatenate(parts, axis=0).astype(out_ref.dtype)


def far_kernel(
    slots_any,
    dests_any,
    x_ref,
    u_ref,
    v_ref,
    src_ref,
    near_ref,
    pattern_ref,
    out_ref,
    near_out,
    place_out,
    slot_ref,
    dest_ref,
    sems,
    place,
    xf,
    picked,
    acc,
):
    peers = x_ref.shape[0]
    slots, nvec, leaf = xf.shape
    blocks, rank, _ = u_ref.shape
    group = leaf // rank
    groups = blocks // group
    copies = load_slots(slots_any, dests_any, slot_ref, dest_ref, sems)
    widen_sources(x_ref, xf)
    placement(x_ref, pattern_ref, place, place_out)
    for copy in copies:
        copy.wait()
    near_product(src_ref, near_ref, x_ref, near_out)
    for g in range(groups):
        rows = [xf[slot_ref[g * group + i]] for i in range(group)]
        picked[g] = jnp.concatenate(rows, axis=0).astype(jnp.bfloat16)
    owner = lax.broadcasted_iota(jnp.int32, (nvec, leaf), 1) // rank

    def coefficients(g):
        u = u_ref[g * group : (g + 1) * group].reshape(leaf, leaf)
        return project(picked[g], u, owner, nvec, group)

    def contributions(g, kept, ats):
        dest = jnp.full((nvec, leaf), ats[0], jnp.int32)
        for i in range(1, group):
            dest = jnp.where(owner == i, ats[i], dest)
        same = [jnp.where(dest == at, kept, 0.0) for at in ats]
        return jnp.dot(
            jnp.concatenate(same, axis=0).astype(jnp.bfloat16),
            v_ref[g * group : (g + 1) * group].reshape(leaf, leaf),
            preferred_element_type=jnp.float32,
        )

    def accumulate(terms, ats):
        sums = [acc[at] + terms[i * nvec : (i + 1) * nvec] for i, at in enumerate(ats)]
        for at, value in zip(ats, sums):
            acc[at] = value

    acc[...] = jnp.zeros_like(acc)
    chunks = [range(first, min(first + CHUNK, groups)) for first in range(0, groups, CHUNK)]
    ahead = [coefficients(g) for g in chunks[0]]
    for c, chunk in enumerate(chunks):
        kept = ahead
        if c + 1 < len(chunks):
            ahead = [coefficients(g) for g in chunks[c + 1]]
        ats = [[dest_ref[g * group + i] for i in range(group)] for g in chunk]
        terms = [contributions(g, k, at) for g, k, at in zip(chunk, kept, ats)]
        for term, at in zip(terms, ats):
            accumulate(term, at)
    put_returns(acc[...].reshape(slots * nvec, leaf), x_ref, src_ref, out_ref)


def sum_kernel(back_ref, near_out_ref, place_ref, near_ref, out_ref):
    peers, rows, width = back_ref.shape
    clusters, nvec, leaf = out_ref.shape
    each = (rows - nvec) // 2
    cap = each // nvec
    me = lax.axis_index("clus")
    terms = jnp.concatenate(
        [back_ref[:, i * each : (i + 1) * each, :].reshape(peers * each, width) for i in range(2)],
        axis=1,
    )
    total = near_out_ref[...] + jnp.dot(
        place_ref[...], terms, preferred_element_type=jnp.float32
    )

    relay = jnp.where(me + 3 < peers, me + 3, me - 3)
    tile = back_ref[relay][rows - nvec :].astype(jnp.float32)
    before = back_ref[jnp.maximum(me - 1, 0)].astype(jnp.float32)
    after = back_ref[jnp.minimum(me + 1, peers - 1)].astype(jnp.float32)
    row = lax.broadcasted_iota(jnp.int32, (clusters * nvec, width), 0)
    lane = lax.broadcasted_iota(jnp.int32, (clusters * nvec, width), 1)
    named = jnp.full((1, width), -1.0, jnp.float32)
    for i in range(2 * cap):
        k, alive = (i + 2 * cap, me > 0) if i < cap else (i, me < peers - 1)
        entry = jnp.where(alive, tile[k : k + 1], -1.0)
        named = jnp.where(lane[:1] // nvec == i, entry, named)
    match = (named == (row // nvec).astype(jnp.float32)) & (lane % nvec == row % nvec)
    match = jnp.where(match, 1.0, 0.0)[:, : 2 * each].astype(jnp.bfloat16)
    sides = jnp.concatenate(
        [
            jnp.concatenate([side[:each], side[each : 2 * each]], axis=1)
            for side in (before, after)
        ],
        axis=0,
    ).astype(jnp.bfloat16)
    total += jnp.dot(match, sides, preferred_element_type=jnp.float32)

    edges = []
    for side, alive, at in ((before, me > 0, (0, 0)), (after, me < peers - 1, (clusters - 1, 2))):
        edge = jnp.where(alive, side[2 * each :], 0.0).astype(jnp.bfloat16)
        edges.append(
            jnp.dot(edge, near_ref[at[0], at[1], width:, :], preferred_element_type=jnp.float32)
        )
    for s in range(clusters):
        part = total[s * nvec : (s + 1) * nvec]
        if s == 0:
            part += edges[0]
        if s == clusters - 1:
            part += edges[1]
        out_ref[s] = part


def cost(flops, moved):
    return pl.CostEstimate(flops=flops, bytes_accessed=moved, transcendentals=0)


def body(sources, near_blocks, far_u, far_v, send_list, far_slot, ret_list, ret_slot):
    clusters, nvec, leaf = sources.shape
    _, peers, cap = send_list.shape
    blocks, rank, _ = far_u.shape
    slots = peers * cap
    rows = 2 * cap * nvec + nvec
    params = pltpu.CompilerParams(vmem_limit_bytes=8 * 2**20)
    pattern = pl.pallas_call(
        pattern_kernel,
        out_shape=jax.ShapeDtypeStruct((nvec, leaf // 2), jnp.float32),
        out_specs=VMEM,
        compiler_params=params,
        cost_estimate=cost(10**10, nvec * leaf * 2),
        name="pattern",
    )()
    message = pl.pallas_call(
        pack_kernel,
        out_shape=jax.ShapeDtypeStruct((peers, rows, leaf // 2), jnp.bfloat16),
        in_specs=[VMEM] * 4,
        out_specs=VMEM,
        compiler_params=params,
        cost_estimate=cost(10**10, peers * rows * leaf),
        name="pack",
    )(send_list[0].T, ret_list[0].T, sources, pattern)
    incoming = lax.all_to_all(message, "clus", split_axis=0, concat_axis=0, tiled=True)
    returns, near_part, place = pl.pallas_call(
        far_kernel,
        out_shape=(
            jax.ShapeDtypeStruct((peers, rows, leaf // 2), jnp.bfloat16),
            jax.ShapeDtypeStruct((clusters * nvec, leaf), jnp.float32),
            jax.ShapeDtypeStruct((clusters * nvec, slots * nvec), jnp.bfloat16),
        ),
        in_specs=[ANY, ANY] + [VMEM] * 6,
        out_specs=(VMEM, VMEM, VMEM),
        scratch_shapes=[
            pltpu.SMEM((blocks,), jnp.int32),
            pltpu.SMEM((blocks,), jnp.int32),
            pltpu.SemaphoreType.DMA((2,)),
            pltpu.VMEM((slots * nvec, leaf // 2), jnp.float32),
            pltpu.VMEM((slots, nvec, leaf), jnp.float32),
            pltpu.VMEM((blocks * rank // leaf, leaf // rank * nvec, leaf), jnp.bfloat16),
            pltpu.VMEM((slots, nvec, leaf), jnp.float32),
        ],
        compiler_params=pltpu.CompilerParams(vmem_limit_bytes=16 * 2**20),
        cost_estimate=cost(4 * blocks * 8 * nvec * leaf * rank, 4 * blocks * rank * leaf),
        name="far",
    )(far_slot, ret_slot, incoming, far_u, far_v, sources, near_blocks, pattern)
    back = lax.all_to_all(returns, "clus", split_axis=0, concat_axis=0, tiled=True)
    return pl.pallas_call(
        sum_kernel,
        out_shape=jax.ShapeDtypeStruct((clusters, nvec, leaf), jnp.float32),
        in_specs=[VMEM] * 4,
        out_specs=VMEM,
        compiler_params=params,
        cost_estimate=cost(2 * clusters * nvec * slots * nvec * leaf, slots * nvec * leaf * 2),
        name="sum",
    )(back, near_part, place, near_blocks)


def solution(mesh):
    placed = (
        P(("groups", "clus"), None, None),
        P(("groups", "clus"), None, None, None),
        P(("groups", "clus"), None, None),
        P(("groups", "clus"), None, None),
        P(("groups", "clus"), None, None),
        P(("groups", "clus")),
        P(("groups", "clus"), None, None),
        P(("groups", "clus")),
    )
    return jax.shard_map(
        body,
        mesh=mesh,
        in_specs=placed,
        out_specs=P(("groups", "clus"), None, None),
        check_vma=False,
    )
```

```python
import jax
import jax.numpy as jnp
from jax import lax
from jax.experimental import pallas as pl
from jax.experimental.pallas import tpu as pltpu
from jax.sharding import PartitionSpec as P

VMEM = pl.BlockSpec(memory_space=pltpu.VMEM)
CHUNK = 4
ANY = pl.BlockSpec(memory_space=pl.ANY)


def halves(x):
    w = x.shape[1] // 2
    return [x[:, :w], x[:, w:]]


def pattern_kernel(out_ref):
    nvec, width = out_ref.shape
    lane = lax.broadcasted_iota(jnp.int32, (nvec, width), 1)
    sub = lax.broadcasted_iota(jnp.int32, (nvec, width), 0)
    out_ref[...] = jnp.where(lane % nvec == sub, lane // nvec, -2).astype(jnp.float32)


def pack_kernel(send_ref, ret_ref, src_ref, pattern_ref, out_ref):
    clusters, nvec, leaf = src_ref.shape
    cap, peers = send_ref.shape
    me = lax.axis_index("clus")
    rows = peers * nvec
    peer = lax.broadcasted_iota(jnp.int32, (rows, peers), 0) // nvec
    kind = lax.broadcasted_iota(jnp.int32, (rows, peers), 0) % nvec // cap
    column = lax.broadcasted_iota(jnp.int32, (rows, peers), 1)

    def entries_at(list_ref, which):
        entries = list_ref[...].astype(jnp.float32).astype(jnp.bfloat16)
        return lax.dot_general(
            jnp.where(which == column, 1.0, 0.0).astype(jnp.bfloat16),
            entries,
            (((1,), (1,)), ((), ())),
            preferred_element_type=jnp.float32,
        )

    send = jnp.maximum(entries_at(send_ref, peer), 0.0)
    ret = entries_at(ret_ref, jnp.where(kind == 1, me - 1, jnp.where(kind == 2, me + 1, peer)))
    row = lax.broadcasted_iota(jnp.int32, (rows, clusters * nvec), 0)
    lane = lax.broadcasted_iota(jnp.int32, (rows, clusters * nvec), 1)
    cluster = jnp.where(row % nvec == lane % nvec, lane // nvec, -2).astype(jnp.float32)
    source = src_ref[...].reshape(clusters * nvec, leaf)
    picked = []
    for k in range(cap):
        pick = jnp.where(send[:, k : k + 1] == cluster, 1.0, 0.0).astype(jnp.bfloat16)
        picked.append(jnp.dot(pick, source, preferred_element_type=jnp.float32))
    vector = lax.broadcasted_iota(jnp.int32, (rows, leaf // 2), 0) % nvec
    places = jnp.broadcast_to(ret[:, :1], (rows, leaf // 2))
    for k in range(1, cap):
        places = jnp.where(vector % cap == k, ret[:, k : k + 1], places)
    first = src_ref[0].astype(jnp.float32)
    last = src_ref[clusters - 1].astype(jnp.float32)
    for p in range(peers):
        at = slice(p * nvec, (p + 1) * nvec)
        parts = []
        for k in range(cap):
            parts += halves(picked[k][at])
        edge = halves(jnp.where(p > me, last, first))[0]
        parts.append(jnp.where(jnp.abs(p - me) == 1, edge, places[at]))
        out_ref[p] = jnp.concatenate(parts, axis=0).astype(out_ref.dtype)


def joined(rows, nvec):
    return jnp.concatenate([rows[:nvec], rows[nvec:]], axis=1)


def load_slots(slots_any, dests_any, slot_ref, dest_ref, sems):
    copies = [
        pltpu.make_async_copy(slots_any, slot_ref, sems.at[0]),
        pltpu.make_async_copy(dests_any, dest_ref, sems.at[1]),
    ]
    for copy in copies:
        copy.start()
    return copies


def near_product(src_ref, near_ref, x_ref, near_out):
    clusters, nvec, leaf = src_ref.shape
    peers, rows, _ = x_ref.shape
    me = lax.axis_index("clus")
    before = x_ref[jnp.maximum(me - 1, 0)][rows - nvec :].astype(jnp.float32)
    after = x_ref[jnp.minimum(me + 1, peers - 1)][rows - nvec :].astype(jnp.float32)
    before = jnp.where(me > 0, before, 0.0)
    after = jnp.where(me < peers - 1, after, 0.0)
    before, after = [
        jnp.concatenate([x, jnp.zeros_like(x)], axis=1).astype(jnp.bfloat16)
        for x in (before, after)
    ]
    sources = [before] + [src_ref[s] for s in range(clusters)] + [after]

    def product(s):
        near_out[s * nvec : (s + 1) * nvec] = jnp.dot(
            jnp.concatenate(sources[s : s + 3], axis=1),
            near_ref[s].reshape(3 * leaf, leaf),
            preferred_element_type=jnp.float32,
        )

    return product


def placement(x_ref, pattern_ref, place, place_out):
    nvec, width = pattern_ref.shape
    peers, rows, _ = x_ref.shape
    cap = place.shape[0] // (peers * nvec)
    cluster = pattern_ref[...]
    me = lax.axis_index("clus")

    def step(p, carry):
        tile = x_ref[p, rows - nvec :, :].astype(jnp.float32)
        tile = jnp.where(jnp.abs(p - me) == 1, -1.0, tile)
        for k in range(cap):
            at = jnp.broadcast_to(tile[k : k + 1], (nvec, width))
            place[pl.ds((p * cap + k) * nvec, nvec)] = jnp.where(at == cluster, 1.0, 0.0)
        return carry

    lax.fori_loop(0, peers, step, 0, unroll=min(peers, 16))
    place_out[...] = place[...].T[: place_out.shape[0]].astype(jnp.bfloat16)


def widen_sources(x_ref, xf):
    peers = x_ref.shape[0]
    slots, nvec, _ = xf.shape
    cap = slots // peers

    def widen(p, carry):
        rows = x_ref[p].astype(jnp.float32)
        for k in range(cap):
            xf[p * cap + k] = joined(rows[2 * k * nvec : 2 * (k + 1) * nvec], nvec)
        return carry

    lax.fori_loop(0, peers, widen, 0, unroll=min(peers, 16))


def project(picked, u, owner, nvec, group):
    full = lax.dot_general(picked, u, (((1,), (1,)), ((), ())), preferred_element_type=jnp.float32)
    kept = full[:nvec]
    for i in range(1, group):
        kept = jnp.where(owner == i, full[i * nvec : (i + 1) * nvec], kept)
    return kept


def put_returns(total, x_ref, src_ref, out_ref):
    peers, rows, width = x_ref.shape
    clusters, nvec, _ = src_ref.shape
    each = total.shape[0] // peers
    cap = each // nvec
    me = lax.axis_index("clus")
    first = halves(src_ref[0].astype(jnp.float32))[1]
    last = halves(src_ref[clusters - 1].astype(jnp.float32))[1]
    sub = lax.broadcasted_iota(jnp.int32, (nvec, width), 0)
    for p in range(peers):
        before = x_ref[max(p - 1, 0), rows - nvec :, :].astype(jnp.float32)
        after = x_ref[min(p + 1, peers - 1), rows - nvec :, :].astype(jnp.float32)
        handed = jnp.where(sub // cap == 2, before, after)
        edge = jnp.where(p > me, last, first)
        parts = halves(total[p * each : (p + 1) * each])
        parts.append(jnp.where(jnp.abs(p - me) == 1, edge, handed))
        out_ref[p] = jnp.concatenate(parts, axis=0).astype(out_ref.dtype)


def far_kernel(
    slots_any,
    dests_any,
    x_ref,
    u_ref,
    v_ref,
    src_ref,
    near_ref,
    pattern_ref,
    out_ref,
    near_out,
    place_out,
    slot_ref,
    dest_ref,
    sems,
    place,
    xf,
    picked,
    acc,
):
    peers = x_ref.shape[0]
    slots, nvec, leaf = xf.shape
    blocks, rank, _ = u_ref.shape
    group = leaf // rank
    groups = blocks // group
    copies = load_slots(slots_any, dests_any, slot_ref, dest_ref, sems)
    widen_sources(x_ref, xf)
    placement(x_ref, pattern_ref, place, place_out)
    for copy in copies:
        copy.wait()
    near = near_product(src_ref, near_ref, x_ref, near_out)
    clusters = src_ref.shape[0]
    for g in range(groups):
        rows = [xf[slot_ref[g * group + i]] for i in range(group)]
        picked[g] = jnp.concatenate(rows, axis=0).astype(jnp.bfloat16)
    owner = lax.broadcasted_iota(jnp.int32, (nvec, leaf), 1) // rank

    def coefficients(g):
        u = u_ref[g * group : (g + 1) * group].reshape(leaf, leaf)
        return project(picked[g], u, owner, nvec, group)

    def contributions(g, kept, ats):
        dest = jnp.full((nvec, leaf), ats[0], jnp.int32)
        for i in range(1, group):
            dest = jnp.where(owner == i, ats[i], dest)
        same = [jnp.where(dest == at, kept, 0.0) for at in ats]
        return jnp.dot(
            jnp.concatenate(same, axis=0).astype(jnp.bfloat16),
            v_ref[g * group : (g + 1) * group].reshape(leaf, leaf),
            preferred_element_type=jnp.float32,
        )

    def accumulate(terms, ats):
        sums = [acc[at] + terms[i * nvec : (i + 1) * nvec] for i, at in enumerate(ats)]
        for at, value in zip(ats, sums):
            acc[at] = value

    acc[...] = jnp.zeros_like(acc)
    chunks = [range(first, min(first + CHUNK, groups)) for first in range(0, groups, CHUNK)]
    ahead = [coefficients(g) for g in chunks[0]]
    for c, chunk in enumerate(chunks):
        kept = ahead
        if c + 1 < len(chunks):
            ahead = [coefficients(g) for g in chunks[c + 1]]
        ats = [[dest_ref[g * group + i] for i in range(group)] for g in chunk]
        terms = [contributions(g, k, at) for g, k, at in zip(chunk, kept, ats)]
        for s in range(c * clusters // len(chunks), (c + 1) * clusters // len(chunks)):
            near(s)
        for term, at in zip(terms, ats):
            accumulate(term, at)
    put_returns(acc[...].reshape(slots * nvec, leaf), x_ref, src_ref, out_ref)


def sum_kernel(back_ref, near_out_ref, place_ref, near_ref, out_ref):
    peers, rows, width = back_ref.shape
    clusters, nvec, leaf = out_ref.shape
    each = (rows - nvec) // 2
    cap = each // nvec
    me = lax.axis_index("clus")
    terms = jnp.concatenate(
        [back_ref[:, i * each : (i + 1) * each, :].reshape(peers * each, width) for i in range(2)],
        axis=1,
    )
    total = near_out_ref[...] + jnp.dot(
        place_ref[...], terms, preferred_element_type=jnp.float32
    )

    relay = jnp.where(me + 3 < peers, me + 3, me - 3)
    tile = back_ref[relay][rows - nvec :].astype(jnp.float32)
    before = back_ref[jnp.maximum(me - 1, 0)].astype(jnp.float32)
    after = back_ref[jnp.minimum(me + 1, peers - 1)].astype(jnp.float32)
    row = lax.broadcasted_iota(jnp.int32, (clusters * nvec, width), 0)
    lane = lax.broadcasted_iota(jnp.int32, (clusters * nvec, width), 1)
    named = jnp.full((1, width), -1.0, jnp.float32)
    for i in range(2 * cap):
        k, alive = (i + 2 * cap, me > 0) if i < cap else (i, me < peers - 1)
        entry = jnp.where(alive, tile[k : k + 1], -1.0)
        named = jnp.where(lane[:1] // nvec == i, entry, named)
    match = (named == (row // nvec).astype(jnp.float32)) & (lane % nvec == row % nvec)
    match = jnp.where(match, 1.0, 0.0)[:, : 2 * each].astype(jnp.bfloat16)
    sides = jnp.concatenate(
        [
            jnp.concatenate([side[:each], side[each : 2 * each]], axis=1)
            for side in (before, after)
        ],
        axis=0,
    ).astype(jnp.bfloat16)
    total += jnp.dot(match, sides, preferred_element_type=jnp.float32)

    edges = []
    for side, alive, at in ((before, me > 0, (0, 0)), (after, me < peers - 1, (clusters - 1, 2))):
        edge = jnp.where(alive, side[2 * each :], 0.0).astype(jnp.bfloat16)
        edges.append(
            jnp.dot(edge, near_ref[at[0], at[1], width:, :], preferred_element_type=jnp.float32)
        )
    for s in range(clusters):
        part = total[s * nvec : (s + 1) * nvec]
        if s == 0:
            part += edges[0]
        if s == clusters - 1:
            part += edges[1]
        out_ref[s] = part


def cost(flops, moved):
    return pl.CostEstimate(flops=flops, bytes_accessed=moved, transcendentals=0)


def body(sources, near_blocks, far_u, far_v, send_list, far_slot, ret_list, ret_slot):
    clusters, nvec, leaf = sources.shape
    _, peers, cap = send_list.shape
    blocks, rank, _ = far_u.shape
    slots = peers * cap
    rows = 2 * cap * nvec + nvec
    params = pltpu.CompilerParams(vmem_limit_bytes=8 * 2**20)
    pattern = pl.pallas_call(
        pattern_kernel,
        out_shape=jax.ShapeDtypeStruct((nvec, leaf // 2), jnp.float32),
        out_specs=VMEM,
        compiler_params=params,
        cost_estimate=cost(10**10, nvec * leaf * 2),
        name="pattern",
    )()
    message = pl.pallas_call(
        pack_kernel,
        out_shape=jax.ShapeDtypeStruct((peers, rows, leaf // 2), jnp.bfloat16),
        in_specs=[VMEM] * 4,
        out_specs=VMEM,
        compiler_params=params,
        cost_estimate=cost(10**10, peers * rows * leaf),
        name="pack",
    )(send_list[0].T, ret_list[0].T, sources, pattern)
    incoming = lax.all_to_all(message, "clus", split_axis=0, concat_axis=0, tiled=True)
    returns, near_part, place = pl.pallas_call(
        far_kernel,
        out_shape=(
            jax.ShapeDtypeStruct((peers, rows, leaf // 2), jnp.bfloat16),
            jax.ShapeDtypeStruct((clusters * nvec, leaf), jnp.float32),
            jax.ShapeDtypeStruct((clusters * nvec, slots * nvec), jnp.bfloat16),
        ),
        in_specs=[ANY, ANY] + [VMEM] * 6,
        out_specs=(VMEM, VMEM, VMEM),
        scratch_shapes=[
            pltpu.SMEM((blocks,), jnp.int32),
            pltpu.SMEM((blocks,), jnp.int32),
            pltpu.SemaphoreType.DMA((2,)),
            pltpu.VMEM((slots * nvec, leaf // 2), jnp.float32),
            pltpu.VMEM((slots, nvec, leaf), jnp.float32),
            pltpu.VMEM((blocks * rank // leaf, leaf // rank * nvec, leaf), jnp.bfloat16),
            pltpu.VMEM((slots, nvec, leaf), jnp.float32),
        ],
        compiler_params=pltpu.CompilerParams(vmem_limit_bytes=16 * 2**20),
        cost_estimate=cost(4 * blocks * 8 * nvec * leaf * rank, 4 * blocks * rank * leaf),
        name="far",
    )(far_slot, ret_slot, incoming, far_u, far_v, sources, near_blocks, pattern)
    back = lax.all_to_all(returns, "clus", split_axis=0, concat_axis=0, tiled=True)
    return pl.pallas_call(
        sum_kernel,
        out_shape=jax.ShapeDtypeStruct((clusters, nvec, leaf), jnp.float32),
        in_specs=[VMEM] * 4,
        out_specs=VMEM,
        compiler_params=params,
        cost_estimate=cost(2 * clusters * nvec * slots * nvec * leaf, slots * nvec * leaf * 2),
        name="sum",
    )(back, near_part, place, near_blocks)


def solution(mesh):
    placed = (
        P(("groups", "clus"), None, None),
        P(("groups", "clus"), None, None, None),
        P(("groups", "clus"), None, None),
        P(("groups", "clus"), None, None),
        P(("groups", "clus"), None, None),
        P(("groups", "clus")),
        P(("groups", "clus"), None, None),
        P(("groups", "clus")),
    )
    return jax.shard_map(
        body,
        mesh=mesh,
        in_specs=placed,
        out_specs=P(("groups", "clus"), None, None),
        check_vma=False,
    )
```

```python
import jax
import jax.numpy as jnp
from jax import lax
from jax.experimental import pallas as pl
from jax.experimental.pallas import tpu as pltpu
from jax.sharding import PartitionSpec as P

VMEM = pl.BlockSpec(memory_space=pltpu.VMEM)
CHUNK = 4
ANY = pl.BlockSpec(memory_space=pl.ANY)


def halves(x):
    w = x.shape[1] // 2
    return [x[:, :w], x[:, w:]]


def pattern_kernel(out_ref):
    nvec, width = out_ref.shape
    lane = lax.broadcasted_iota(jnp.int32, (nvec, width), 1)
    sub = lax.broadcasted_iota(jnp.int32, (nvec, width), 0)
    out_ref[...] = jnp.where(lane % nvec == sub, lane // nvec, -2).astype(jnp.float32)


def pack_kernel(send_ref, ret_ref, src_ref, pattern_ref, out_ref):
    clusters, nvec, leaf = src_ref.shape
    cap, peers = send_ref.shape
    me = lax.axis_index("clus")
    rows = peers * nvec
    peer = lax.broadcasted_iota(jnp.int32, (rows, peers), 0) // nvec
    kind = lax.broadcasted_iota(jnp.int32, (rows, peers), 0) % nvec // cap
    column = lax.broadcasted_iota(jnp.int32, (rows, peers), 1)

    def entries_at(list_ref, which):
        entries = list_ref[...].astype(jnp.float32).astype(jnp.bfloat16)
        return lax.dot_general(
            jnp.where(which == column, 1.0, 0.0).astype(jnp.bfloat16),
            entries,
            (((1,), (1,)), ((), ())),
            preferred_element_type=jnp.float32,
        )

    send = jnp.maximum(entries_at(send_ref, peer), 0.0)
    ret = entries_at(ret_ref, jnp.where(kind == 1, me - 1, jnp.where(kind == 2, me + 1, peer)))
    row = lax.broadcasted_iota(jnp.int32, (rows, clusters * nvec), 0)
    lane = lax.broadcasted_iota(jnp.int32, (rows, clusters * nvec), 1)
    cluster = jnp.where(row % nvec == lane % nvec, lane // nvec, -2).astype(jnp.float32)
    source = src_ref[...].reshape(clusters * nvec, leaf)
    picked = []
    for k in range(cap):
        pick = jnp.where(send[:, k : k + 1] == cluster, 1.0, 0.0).astype(jnp.bfloat16)
        picked.append(jnp.dot(pick, source, preferred_element_type=jnp.float32))
    vector = lax.broadcasted_iota(jnp.int32, (rows, leaf // 2), 0) % nvec
    places = jnp.broadcast_to(ret[:, :1], (rows, leaf // 2))
    for k in range(1, cap):
        places = jnp.where(vector % cap == k, ret[:, k : k + 1], places)
    first = src_ref[0].astype(jnp.float32)
    last = src_ref[clusters - 1].astype(jnp.float32)
    for p in range(peers):
        at = slice(p * nvec, (p + 1) * nvec)
        parts = []
        for k in range(cap):
            parts += halves(picked[k][at])
        edge = halves(jnp.where(p > me, last, first))[0]
        parts.append(jnp.where(jnp.abs(p - me) == 1, edge, places[at]))
        out_ref[p] = jnp.concatenate(parts, axis=0).astype(out_ref.dtype)


def joined(rows, nvec):
    return jnp.concatenate([rows[:nvec], rows[nvec:]], axis=1)


def load_slots(slots_any, dests_any, slot_ref, dest_ref, sems):
    copies = [
        pltpu.make_async_copy(slots_any, slot_ref, sems.at[0]),
        pltpu.make_async_copy(dests_any, dest_ref, sems.at[1]),
    ]
    for copy in copies:
        copy.start()
    return copies


def near_product(src_ref, near_ref, x_ref, near_out):
    clusters, nvec, leaf = src_ref.shape
    peers, rows, _ = x_ref.shape
    me = lax.axis_index("clus")
    before = x_ref[jnp.maximum(me - 1, 0)][rows - nvec :].astype(jnp.float32)
    after = x_ref[jnp.minimum(me + 1, peers - 1)][rows - nvec :].astype(jnp.float32)
    before = jnp.where(me > 0, before, 0.0)
    after = jnp.where(me < peers - 1, after, 0.0)
    before, after = [
        jnp.concatenate([x, jnp.zeros_like(x)], axis=1).astype(jnp.bfloat16)
        for x in (before, after)
    ]
    sources = [before] + [src_ref[s] for s in range(clusters)] + [after]

    def product(s):
        near_out[s * nvec : (s + 1) * nvec] = jnp.dot(
            jnp.concatenate(sources[s : s + 3], axis=1),
            near_ref[s].reshape(3 * leaf, leaf),
            preferred_element_type=jnp.float32,
        )

    return product


def placement(x_ref, pattern_ref, place, place_out):
    nvec, width = pattern_ref.shape
    peers, rows, _ = x_ref.shape
    cap = place.shape[0] // (peers * nvec)
    cluster = pattern_ref[...]
    me = lax.axis_index("clus")

    def step(p, carry):
        tile = x_ref[p, rows - nvec :, :].astype(jnp.float32)
        tile = jnp.where(jnp.abs(p - me) == 1, -1.0, tile)
        for k in range(cap):
            at = jnp.broadcast_to(tile[k : k + 1], (nvec, width))
            place[pl.ds((p * cap + k) * nvec, nvec)] = jnp.where(at == cluster, 1.0, 0.0)
        return carry

    lax.fori_loop(0, peers, step, 0, unroll=min(peers, 16))
    place_out[...] = place[...].T[: place_out.shape[0]].astype(jnp.bfloat16)


def widen_sources(x_ref, xf):
    peers = x_ref.shape[0]
    slots, nvec, _ = xf.shape
    cap = slots // peers

    def widen(p, carry):
        rows = x_ref[p].astype(jnp.float32)
        for k in range(cap):
            xf[p * cap + k] = joined(rows[2 * k * nvec : 2 * (k + 1) * nvec], nvec)
        return carry

    lax.fori_loop(0, peers, widen, 0, unroll=min(peers, 16))


def project(picked, u, owner, nvec, group):
    full = lax.dot_general(picked, u, (((1,), (1,)), ((), ())), preferred_element_type=jnp.float32)
    kept = full[:nvec]
    for i in range(1, group):
        kept = jnp.where(owner == i, full[i * nvec : (i + 1) * nvec], kept)
    return kept


def put_returns(total, x_ref, src_ref, out_ref):
    peers, rows, width = x_ref.shape
    clusters, nvec, _ = src_ref.shape
    each = total.shape[0] // peers
    cap = each // nvec
    me = lax.axis_index("clus")
    first = halves(src_ref[0].astype(jnp.float32))[1]
    last = halves(src_ref[clusters - 1].astype(jnp.float32))[1]
    sub = lax.broadcasted_iota(jnp.int32, (nvec, width), 0)
    for p in range(peers):
        before = x_ref[max(p - 1, 0), rows - nvec :, :].astype(jnp.float32)
        after = x_ref[min(p + 1, peers - 1), rows - nvec :, :].astype(jnp.float32)
        handed = jnp.where(sub // cap == 2, before, after)
        edge = jnp.where(p > me, last, first)
        parts = halves(total[p * each : (p + 1) * each])
        parts.append(jnp.where(jnp.abs(p - me) == 1, edge, handed))
        out_ref[p] = jnp.concatenate(parts, axis=0).astype(out_ref.dtype)


def far_kernel(
    slots_any,
    dests_any,
    x_ref,
    u_ref,
    v_ref,
    src_ref,
    near_ref,
    pattern_ref,
    out_ref,
    near_out,
    place_out,
    slot_ref,
    dest_ref,
    sems,
    place,
    xf,
    picked,
    *accs,
):
    peers = x_ref.shape[0]
    slots, nvec, leaf = xf.shape
    blocks, rank, _ = u_ref.shape
    group = leaf // rank
    groups = blocks // group
    copies = load_slots(slots_any, dests_any, slot_ref, dest_ref, sems)
    widen_sources(x_ref, xf)
    placement(x_ref, pattern_ref, place, place_out)
    for copy in copies:
        copy.wait()
    near = near_product(src_ref, near_ref, x_ref, near_out)
    clusters = src_ref.shape[0]
    for g in range(groups):
        rows = [xf[slot_ref[g * group + i]] for i in range(group)]
        picked[g] = jnp.concatenate(rows, axis=0).astype(jnp.bfloat16)
    owner = lax.broadcasted_iota(jnp.int32, (nvec, leaf), 1) // rank

    def coefficients(g):
        u = u_ref[g * group : (g + 1) * group].reshape(leaf, leaf)
        return project(picked[g], u, owner, nvec, group)

    def contributions(g, kept, ats):
        dest = jnp.full((nvec, leaf), ats[0], jnp.int32)
        for i in range(1, group):
            dest = jnp.where(owner == i, ats[i], dest)
        same = [jnp.where(dest == at, kept, 0.0) for at in ats]
        return jnp.dot(
            jnp.concatenate(same, axis=0).astype(jnp.bfloat16),
            v_ref[g * group : (g + 1) * group].reshape(leaf, leaf),
            preferred_element_type=jnp.float32,
        )

    def accumulate(acc, terms, ats):
        sums = [acc[at] + terms[i * nvec : (i + 1) * nvec] for i, at in enumerate(ats)]
        for at, value in zip(ats, sums):
            acc[at] = value

    for acc in accs:
        acc[...] = jnp.zeros_like(acc)
    chunks = [range(first, min(first + CHUNK, groups)) for first in range(0, groups, CHUNK)]
    ahead = [coefficients(g) for g in chunks[0]]
    for c, chunk in enumerate(chunks):
        kept = ahead
        if c + 1 < len(chunks):
            ahead = [coefficients(g) for g in chunks[c + 1]]
        ats = [[dest_ref[g * group + i] for i in range(group)] for g in chunk]
        terms = [contributions(g, k, at) for g, k, at in zip(chunk, kept, ats)]
        for s in range(c * clusters // len(chunks), (c + 1) * clusters // len(chunks)):
            near(s)
        for g, term, at in zip(chunk, terms, ats):
            accumulate(accs[g % len(accs)], term, at)
    total = accs[0][...] + accs[1][...]
    put_returns(total.reshape(slots * nvec, leaf), x_ref, src_ref, out_ref)


def sum_kernel(back_ref, near_out_ref, place_ref, near_ref, out_ref):
    peers, rows, width = back_ref.shape
    clusters, nvec, leaf = out_ref.shape
    each = (rows - nvec) // 2
    cap = each // nvec
    me = lax.axis_index("clus")
    terms = jnp.concatenate(
        [back_ref[:, i * each : (i + 1) * each, :].reshape(peers * each, width) for i in range(2)],
        axis=1,
    )
    total = near_out_ref[...] + jnp.dot(
        place_ref[...], terms, preferred_element_type=jnp.float32
    )

    relay = jnp.where(me + 3 < peers, me + 3, me - 3)
    tile = back_ref[relay][rows - nvec :].astype(jnp.float32)
    before = back_ref[jnp.maximum(me - 1, 0)].astype(jnp.float32)
    after = back_ref[jnp.minimum(me + 1, peers - 1)].astype(jnp.float32)
    row = lax.broadcasted_iota(jnp.int32, (clusters * nvec, width), 0)
    lane = lax.broadcasted_iota(jnp.int32, (clusters * nvec, width), 1)
    named = jnp.full((1, width), -1.0, jnp.float32)
    for i in range(2 * cap):
        k, alive = (i + 2 * cap, me > 0) if i < cap else (i, me < peers - 1)
        entry = jnp.where(alive, tile[k : k + 1], -1.0)
        named = jnp.where(lane[:1] // nvec == i, entry, named)
    match = (named == (row // nvec).astype(jnp.float32)) & (lane % nvec == row % nvec)
    match = jnp.where(match, 1.0, 0.0)[:, : 2 * each].astype(jnp.bfloat16)
    sides = jnp.concatenate(
        [
            jnp.concatenate([side[:each], side[each : 2 * each]], axis=1)
            for side in (before, after)
        ],
        axis=0,
    ).astype(jnp.bfloat16)
    total += jnp.dot(match, sides, preferred_element_type=jnp.float32)

    edges = []
    for side, alive, at in ((before, me > 0, (0, 0)), (after, me < peers - 1, (clusters - 1, 2))):
        edge = jnp.where(alive, side[2 * each :], 0.0).astype(jnp.bfloat16)
        edges.append(
            jnp.dot(edge, near_ref[at[0], at[1], width:, :], preferred_element_type=jnp.float32)
        )
    for s in range(clusters):
        part = total[s * nvec : (s + 1) * nvec]
        if s == 0:
            part += edges[0]
        if s == clusters - 1:
            part += edges[1]
        out_ref[s] = part


def cost(flops, moved):
    return pl.CostEstimate(flops=flops, bytes_accessed=moved, transcendentals=0)


def body(sources, near_blocks, far_u, far_v, send_list, far_slot, ret_list, ret_slot):
    clusters, nvec, leaf = sources.shape
    _, peers, cap = send_list.shape
    blocks, rank, _ = far_u.shape
    slots = peers * cap
    rows = 2 * cap * nvec + nvec
    params = pltpu.CompilerParams(vmem_limit_bytes=8 * 2**20)
    pattern = pl.pallas_call(
        pattern_kernel,
        out_shape=jax.ShapeDtypeStruct((nvec, leaf // 2), jnp.float32),
        out_specs=VMEM,
        compiler_params=params,
        cost_estimate=cost(10**10, nvec * leaf * 2),
        name="pattern",
    )()
    message = pl.pallas_call(
        pack_kernel,
        out_shape=jax.ShapeDtypeStruct((peers, rows, leaf // 2), jnp.bfloat16),
        in_specs=[VMEM] * 4,
        out_specs=VMEM,
        compiler_params=params,
        cost_estimate=cost(10**10, peers * rows * leaf),
        name="pack",
    )(send_list[0].T, ret_list[0].T, sources, pattern)
    incoming = lax.all_to_all(message, "clus", split_axis=0, concat_axis=0, tiled=True)
    returns, near_part, place = pl.pallas_call(
        far_kernel,
        out_shape=(
            jax.ShapeDtypeStruct((peers, rows, leaf // 2), jnp.bfloat16),
            jax.ShapeDtypeStruct((clusters * nvec, leaf), jnp.float32),
            jax.ShapeDtypeStruct((clusters * nvec, slots * nvec), jnp.bfloat16),
        ),
        in_specs=[ANY, ANY] + [VMEM] * 6,
        out_specs=(VMEM, VMEM, VMEM),
        scratch_shapes=[
            pltpu.SMEM((blocks,), jnp.int32),
            pltpu.SMEM((blocks,), jnp.int32),
            pltpu.SemaphoreType.DMA((2,)),
            pltpu.VMEM((slots * nvec, leaf // 2), jnp.float32),
            pltpu.VMEM((slots, nvec, leaf), jnp.float32),
            pltpu.VMEM((blocks * rank // leaf, leaf // rank * nvec, leaf), jnp.bfloat16),
            pltpu.VMEM((slots, nvec, leaf), jnp.float32),
            pltpu.VMEM((slots, nvec, leaf), jnp.float32),
        ],
        compiler_params=pltpu.CompilerParams(vmem_limit_bytes=16 * 2**20),
        cost_estimate=cost(4 * blocks * 8 * nvec * leaf * rank, 4 * blocks * rank * leaf),
        name="far",
    )(far_slot, ret_slot, incoming, far_u, far_v, sources, near_blocks, pattern)
    back = lax.all_to_all(returns, "clus", split_axis=0, concat_axis=0, tiled=True)
    return pl.pallas_call(
        sum_kernel,
        out_shape=jax.ShapeDtypeStruct((clusters, nvec, leaf), jnp.float32),
        in_specs=[VMEM] * 4,
        out_specs=VMEM,
        compiler_params=params,
        cost_estimate=cost(2 * clusters * nvec * slots * nvec * leaf, slots * nvec * leaf * 2),
        name="sum",
    )(back, near_part, place, near_blocks)


def solution(mesh):
    placed = (
        P(("groups", "clus"), None, None),
        P(("groups", "clus"), None, None, None),
        P(("groups", "clus"), None, None),
        P(("groups", "clus"), None, None),
        P(("groups", "clus"), None, None),
        P(("groups", "clus")),
        P(("groups", "clus"), None, None),
        P(("groups", "clus")),
    )
    return jax.shard_map(
        body,
        mesh=mesh,
        in_specs=placed,
        out_specs=P(("groups", "clus"), None, None),
        check_vma=False,
    )
```

```python
import jax
import jax.numpy as jnp
from jax import lax
from jax.experimental import pallas as pl
from jax.experimental.pallas import tpu as pltpu
from jax.sharding import PartitionSpec as P

VMEM = pl.BlockSpec(memory_space=pltpu.VMEM)
CHUNK = 4
ANY = pl.BlockSpec(memory_space=pl.ANY)


def halves(x):
    w = x.shape[1] // 2
    return [x[:, :w], x[:, w:]]


def pattern_kernel(out_ref):
    nvec, width = out_ref.shape
    lane = lax.broadcasted_iota(jnp.int32, (nvec, width), 1)
    sub = lax.broadcasted_iota(jnp.int32, (nvec, width), 0)
    out_ref[...] = jnp.where(lane % nvec == sub, lane // nvec, -2).astype(jnp.float32)


def pack_kernel(send_ref, ret_ref, src_ref, pattern_ref, out_ref):
    clusters, nvec, leaf = src_ref.shape
    cap, peers = send_ref.shape
    me = lax.axis_index("clus")
    rows = peers * nvec
    peer = lax.broadcasted_iota(jnp.int32, (rows, peers), 0) // nvec
    kind = lax.broadcasted_iota(jnp.int32, (rows, peers), 0) % nvec // cap
    column = lax.broadcasted_iota(jnp.int32, (rows, peers), 1)

    def entries_at(list_ref, which):
        entries = list_ref[...].astype(jnp.float32).astype(jnp.bfloat16)
        return lax.dot_general(
            jnp.where(which == column, 1.0, 0.0).astype(jnp.bfloat16),
            entries,
            (((1,), (1,)), ((), ())),
            preferred_element_type=jnp.float32,
        )

    send = jnp.maximum(entries_at(send_ref, peer), 0.0)
    ret = entries_at(ret_ref, jnp.where(kind == 1, me - 1, jnp.where(kind == 2, me + 1, peer)))
    row = lax.broadcasted_iota(jnp.int32, (rows, clusters * nvec), 0)
    lane = lax.broadcasted_iota(jnp.int32, (rows, clusters * nvec), 1)
    cluster = jnp.where(row % nvec == lane % nvec, lane // nvec, -2).astype(jnp.float32)
    source = src_ref[...].reshape(clusters * nvec, leaf)
    picked = []
    for k in range(cap):
        pick = jnp.where(send[:, k : k + 1] == cluster, 1.0, 0.0).astype(jnp.bfloat16)
        picked.append(jnp.dot(pick, source, preferred_element_type=jnp.float32))
    vector = lax.broadcasted_iota(jnp.int32, (rows, leaf // 2), 0) % nvec
    places = jnp.broadcast_to(ret[:, :1], (rows, leaf // 2))
    for k in range(1, cap):
        places = jnp.where(vector % cap == k, ret[:, k : k + 1], places)
    first = src_ref[0].astype(jnp.float32)
    last = src_ref[clusters - 1].astype(jnp.float32)
    for p in range(peers):
        at = slice(p * nvec, (p + 1) * nvec)
        parts = []
        for k in range(cap):
            parts += halves(picked[k][at])
        edge = halves(jnp.where(p > me, last, first))[0]
        parts.append(jnp.where(jnp.abs(p - me) == 1, edge, places[at]))
        out_ref[p] = jnp.concatenate(parts, axis=0).astype(out_ref.dtype)


def joined(rows, nvec):
    return jnp.concatenate([rows[:nvec], rows[nvec:]], axis=1)


def load_slots(slots_any, dests_any, slot_ref, dest_ref, sems):
    copies = [
        pltpu.make_async_copy(slots_any, slot_ref, sems.at[0]),
        pltpu.make_async_copy(dests_any, dest_ref, sems.at[1]),
    ]
    for copy in copies:
        copy.start()
    return copies


def near_product(src_ref, near_ref, x_ref, near_out):
    clusters, nvec, leaf = src_ref.shape
    peers, rows, _ = x_ref.shape
    me = lax.axis_index("clus")
    before = x_ref[jnp.maximum(me - 1, 0)][rows - nvec :].astype(jnp.float32)
    after = x_ref[jnp.minimum(me + 1, peers - 1)][rows - nvec :].astype(jnp.float32)
    before = jnp.where(me > 0, before, 0.0)
    after = jnp.where(me < peers - 1, after, 0.0)
    before, after = [
        jnp.concatenate([x, jnp.zeros_like(x)], axis=1).astype(jnp.bfloat16)
        for x in (before, after)
    ]
    sources = [before] + [src_ref[s] for s in range(clusters)] + [after]

    def product(s):
        near_out[s * nvec : (s + 1) * nvec] = jnp.dot(
            jnp.concatenate(sources[s : s + 3], axis=1),
            near_ref[s].reshape(3 * leaf, leaf),
            preferred_element_type=jnp.float32,
        )

    return product


def placement(x_ref, pattern_ref, place, place_out):
    nvec, width = pattern_ref.shape
    peers, rows, _ = x_ref.shape
    cap = place.shape[0] // (peers * nvec)
    cluster = pattern_ref[...]
    me = lax.axis_index("clus")

    def step(p, carry):
        tile = x_ref[p, rows - nvec :, :].astype(jnp.float32)
        tile = jnp.where(jnp.abs(p - me) == 1, -1.0, tile)
        for k in range(cap):
            at = jnp.broadcast_to(tile[k : k + 1], (nvec, width))
            place[pl.ds((p * cap + k) * nvec, nvec)] = jnp.where(at == cluster, 1.0, 0.0)
        return carry

    lax.fori_loop(0, peers, step, 0, unroll=min(peers, 16))
    place_out[...] = place[...].T[: place_out.shape[0]].astype(jnp.bfloat16)


def widen_sources(x_ref, xf):
    peers = x_ref.shape[0]
    slots, nvec, _ = xf.shape
    cap = slots // peers

    def widen(p, carry):
        rows = x_ref[p].astype(jnp.float32)
        for k in range(cap):
            xf[p * cap + k] = joined(rows[2 * k * nvec : 2 * (k + 1) * nvec], nvec)
        return carry

    lax.fori_loop(0, peers, widen, 0, unroll=min(peers, 16))


def project(picked, u, owner, nvec, group):
    full = lax.dot_general(picked, u, (((1,), (1,)), ((), ())), preferred_element_type=jnp.float32)
    kept = full[:nvec]
    for i in range(1, group):
        kept = jnp.where(owner == i, full[i * nvec : (i + 1) * nvec], kept)
    return kept


def put_returns(total, x_ref, src_ref, out_ref):
    peers, rows, width = x_ref.shape
    clusters, nvec, _ = src_ref.shape
    each = total.shape[0] // peers
    cap = each // nvec
    me = lax.axis_index("clus")
    first = halves(src_ref[0].astype(jnp.float32))[1]
    last = halves(src_ref[clusters - 1].astype(jnp.float32))[1]
    sub = lax.broadcasted_iota(jnp.int32, (nvec, width), 0)
    for p in range(peers):
        before = x_ref[max(p - 1, 0), rows - nvec :, :].astype(jnp.float32)
        after = x_ref[min(p + 1, peers - 1), rows - nvec :, :].astype(jnp.float32)
        handed = jnp.where(sub // cap == 2, before, after)
        edge = jnp.where(p > me, last, first)
        parts = halves(total[p * each : (p + 1) * each])
        parts.append(jnp.where(jnp.abs(p - me) == 1, edge, handed))
        out_ref[p] = jnp.concatenate(parts, axis=0).astype(out_ref.dtype)


def far_kernel(
    slots_any,
    dests_any,
    x_ref,
    u_ref,
    v_ref,
    src_ref,
    near_ref,
    pattern_ref,
    out_ref,
    near_out,
    place_out,
    slot_ref,
    dest_ref,
    sems,
    place,
    xf,
    picked,
    acc,
):
    peers = x_ref.shape[0]
    slots, nvec, leaf = xf.shape
    blocks, rank, _ = u_ref.shape
    group = leaf // rank
    groups = blocks // group
    copies = load_slots(slots_any, dests_any, slot_ref, dest_ref, sems)
    widen_sources(x_ref, xf)
    for copy in copies:
        copy.wait()
    near = near_product(src_ref, near_ref, x_ref, near_out)
    clusters = src_ref.shape[0]
    for g in range(groups):
        rows = [xf[slot_ref[g * group + i]] for i in range(group)]
        picked[g] = jnp.concatenate(rows, axis=0).astype(jnp.bfloat16)
    owner = lax.broadcasted_iota(jnp.int32, (nvec, leaf), 1) // rank

    def coefficients(g):
        u = u_ref[g * group : (g + 1) * group].reshape(leaf, leaf)
        return project(picked[g], u, owner, nvec, group)

    def contributions(g, kept, ats):
        dest = jnp.full((nvec, leaf), ats[0], jnp.int32)
        for i in range(1, group):
            dest = jnp.where(owner == i, ats[i], dest)
        same = [jnp.where(dest == at, kept, 0.0) for at in ats]
        return jnp.dot(
            jnp.concatenate(same, axis=0).astype(jnp.bfloat16),
            v_ref[g * group : (g + 1) * group].reshape(leaf, leaf),
            preferred_element_type=jnp.float32,
        )

    def accumulate(terms, ats):
        sums = [acc[at] + terms[i * nvec : (i + 1) * nvec] for i, at in enumerate(ats)]
        for at, value in zip(ats, sums):
            acc[at] = value

    acc[...] = jnp.zeros_like(acc)
    chunks = [range(first, min(first + CHUNK, groups)) for first in range(0, groups, CHUNK)]
    ahead = [coefficients(g) for g in chunks[0]]
    for c, chunk in enumerate(chunks):
        kept = ahead
        if c + 1 < len(chunks):
            ahead = [coefficients(g) for g in chunks[c + 1]]
        ats = [[dest_ref[g * group + i] for i in range(group)] for g in chunk]
        terms = [contributions(g, k, at) for g, k, at in zip(chunk, kept, ats)]
        for s in range(c * clusters // len(chunks), (c + 1) * clusters // len(chunks)):
            near(s)
        if c == 0:
            placement(x_ref, pattern_ref, place, place_out)
        for term, at in zip(terms, ats):
            accumulate(term, at)
    put_returns(acc[...].reshape(slots * nvec, leaf), x_ref, src_ref, out_ref)


def sum_kernel(back_ref, near_out_ref, place_ref, near_ref, out_ref):
    peers, rows, width = back_ref.shape
    clusters, nvec, leaf = out_ref.shape
    each = (rows - nvec) // 2
    cap = each // nvec
    me = lax.axis_index("clus")
    terms = jnp.concatenate(
        [back_ref[:, i * each : (i + 1) * each, :].reshape(peers * each, width) for i in range(2)],
        axis=1,
    )
    total = near_out_ref[...] + jnp.dot(
        place_ref[...], terms, preferred_element_type=jnp.float32
    )

    relay = jnp.where(me + 3 < peers, me + 3, me - 3)
    tile = back_ref[relay][rows - nvec :].astype(jnp.float32)
    before = back_ref[jnp.maximum(me - 1, 0)].astype(jnp.float32)
    after = back_ref[jnp.minimum(me + 1, peers - 1)].astype(jnp.float32)
    row = lax.broadcasted_iota(jnp.int32, (clusters * nvec, width), 0)
    lane = lax.broadcasted_iota(jnp.int32, (clusters * nvec, width), 1)
    named = jnp.full((1, width), -1.0, jnp.float32)
    for i in range(2 * cap):
        k, alive = (i + 2 * cap, me > 0) if i < cap else (i, me < peers - 1)
        entry = jnp.where(alive, tile[k : k + 1], -1.0)
        named = jnp.where(lane[:1] // nvec == i, entry, named)
    match = (named == (row // nvec).astype(jnp.float32)) & (lane % nvec == row % nvec)
    match = jnp.where(match, 1.0, 0.0)[:, : 2 * each].astype(jnp.bfloat16)
    sides = jnp.concatenate(
        [
            jnp.concatenate([side[:each], side[each : 2 * each]], axis=1)
            for side in (before, after)
        ],
        axis=0,
    ).astype(jnp.bfloat16)
    total += jnp.dot(match, sides, preferred_element_type=jnp.float32)

    edges = []
    for side, alive, at in ((before, me > 0, (0, 0)), (after, me < peers - 1, (clusters - 1, 2))):
        edge = jnp.where(alive, side[2 * each :], 0.0).astype(jnp.bfloat16)
        edges.append(
            jnp.dot(edge, near_ref[at[0], at[1], width:, :], preferred_element_type=jnp.float32)
        )
    for s in range(clusters):
        part = total[s * nvec : (s + 1) * nvec]
        if s == 0:
            part += edges[0]
        if s == clusters - 1:
            part += edges[1]
        out_ref[s] = part


def cost(flops, moved):
    return pl.CostEstimate(flops=flops, bytes_accessed=moved, transcendentals=0)


def body(sources, near_blocks, far_u, far_v, send_list, far_slot, ret_list, ret_slot):
    clusters, nvec, leaf = sources.shape
    _, peers, cap = send_list.shape
    blocks, rank, _ = far_u.shape
    slots = peers * cap
    rows = 2 * cap * nvec + nvec
    params = pltpu.CompilerParams(vmem_limit_bytes=8 * 2**20)
    pattern = pl.pallas_call(
        pattern_kernel,
        out_shape=jax.ShapeDtypeStruct((nvec, leaf // 2), jnp.float32),
        out_specs=VMEM,
        compiler_params=params,
        cost_estimate=cost(10**10, nvec * leaf * 2),
        name="pattern",
    )()
    message = pl.pallas_call(
        pack_kernel,
        out_shape=jax.ShapeDtypeStruct((peers, rows, leaf // 2), jnp.bfloat16),
        in_specs=[VMEM] * 4,
        out_specs=VMEM,
        compiler_params=params,
        cost_estimate=cost(10**10, peers * rows * leaf),
        name="pack",
    )(send_list[0].T, ret_list[0].T, sources, pattern)
    incoming = lax.all_to_all(message, "clus", split_axis=0, concat_axis=0, tiled=True)
    returns, near_part, place = pl.pallas_call(
        far_kernel,
        out_shape=(
            jax.ShapeDtypeStruct((peers, rows, leaf // 2), jnp.bfloat16),
            jax.ShapeDtypeStruct((clusters * nvec, leaf), jnp.float32),
            jax.ShapeDtypeStruct((clusters * nvec, slots * nvec), jnp.bfloat16),
        ),
        in_specs=[ANY, ANY] + [VMEM] * 6,
        out_specs=(VMEM, VMEM, VMEM),
        scratch_shapes=[
            pltpu.SMEM((blocks,), jnp.int32),
            pltpu.SMEM((blocks,), jnp.int32),
            pltpu.SemaphoreType.DMA((2,)),
            pltpu.VMEM((slots * nvec, leaf // 2), jnp.float32),
            pltpu.VMEM((slots, nvec, leaf), jnp.float32),
            pltpu.VMEM((blocks * rank // leaf, leaf // rank * nvec, leaf), jnp.bfloat16),
            pltpu.VMEM((slots, nvec, leaf), jnp.float32),
        ],
        compiler_params=pltpu.CompilerParams(vmem_limit_bytes=16 * 2**20),
        cost_estimate=cost(4 * blocks * 8 * nvec * leaf * rank, 4 * blocks * rank * leaf),
        name="far",
    )(far_slot, ret_slot, incoming, far_u, far_v, sources, near_blocks, pattern)
    back = lax.all_to_all(returns, "clus", split_axis=0, concat_axis=0, tiled=True)
    return pl.pallas_call(
        sum_kernel,
        out_shape=jax.ShapeDtypeStruct((clusters, nvec, leaf), jnp.float32),
        in_specs=[VMEM] * 4,
        out_specs=VMEM,
        compiler_params=params,
        cost_estimate=cost(2 * clusters * nvec * slots * nvec * leaf, slots * nvec * leaf * 2),
        name="sum",
    )(back, near_part, place, near_blocks)


def solution(mesh):
    placed = (
        P(("groups", "clus"), None, None),
        P(("groups", "clus"), None, None, None),
        P(("groups", "clus"), None, None),
        P(("groups", "clus"), None, None),
        P(("groups", "clus"), None, None),
        P(("groups", "clus")),
        P(("groups", "clus"), None, None),
        P(("groups", "clus")),
    )
    return jax.shard_map(
        body,
        mesh=mesh,
        in_specs=placed,
        out_specs=P(("groups", "clus"), None, None),
        check_vma=False,
    )
```

```python
import jax
import jax.numpy as jnp
from jax import lax
from jax.experimental import pallas as pl
from jax.experimental.pallas import tpu as pltpu
from jax.sharding import PartitionSpec as P

VMEM = pl.BlockSpec(memory_space=pltpu.VMEM)
CHUNK = 4
ANY = pl.BlockSpec(memory_space=pl.ANY)


def halves(x):
    w = x.shape[1] // 2
    return [x[:, :w], x[:, w:]]


def pattern_kernel(out_ref):
    nvec, width = out_ref.shape
    lane = lax.broadcasted_iota(jnp.int32, (nvec, width), 1)
    sub = lax.broadcasted_iota(jnp.int32, (nvec, width), 0)
    out_ref[...] = jnp.where(lane % nvec == sub, lane // nvec, -2).astype(jnp.float32)


def pack_kernel(send_ref, ret_ref, src_ref, pattern_ref, out_ref):
    clusters, nvec, leaf = src_ref.shape
    cap, peers = send_ref.shape
    me = lax.axis_index("clus")
    rows = peers * nvec
    peer = lax.broadcasted_iota(jnp.int32, (rows, peers), 0) // nvec
    kind = lax.broadcasted_iota(jnp.int32, (rows, peers), 0) % nvec // cap
    column = lax.broadcasted_iota(jnp.int32, (rows, peers), 1)

    def entries_at(list_ref, which):
        entries = list_ref[...].astype(jnp.float32).astype(jnp.bfloat16)
        return lax.dot_general(
            jnp.where(which == column, 1.0, 0.0).astype(jnp.bfloat16),
            entries,
            (((1,), (1,)), ((), ())),
            preferred_element_type=jnp.float32,
        )

    send = jnp.maximum(entries_at(send_ref, peer), 0.0)
    ret = entries_at(ret_ref, jnp.where(kind == 1, me - 1, jnp.where(kind == 2, me + 1, peer)))
    row = lax.broadcasted_iota(jnp.int32, (rows, clusters * nvec), 0)
    lane = lax.broadcasted_iota(jnp.int32, (rows, clusters * nvec), 1)
    cluster = jnp.where(row % nvec == lane % nvec, lane // nvec, -2).astype(jnp.float32)
    source = src_ref[...].reshape(clusters * nvec, leaf)
    picked = []
    for k in range(cap):
        pick = jnp.where(send[:, k : k + 1] == cluster, 1.0, 0.0).astype(jnp.bfloat16)
        picked.append(jnp.dot(pick, source, preferred_element_type=jnp.float32))
    vector = lax.broadcasted_iota(jnp.int32, (rows, leaf // 2), 0) % nvec
    places = jnp.broadcast_to(ret[:, :1], (rows, leaf // 2))
    for k in range(1, cap):
        places = jnp.where(vector % cap == k, ret[:, k : k + 1], places)
    first = src_ref[0].astype(jnp.float32)
    last = src_ref[clusters - 1].astype(jnp.float32)
    for p in range(peers):
        at = slice(p * nvec, (p + 1) * nvec)
        parts = []
        for k in range(cap):
            parts += halves(picked[k][at])
        edge = halves(jnp.where(p > me, last, first))[0]
        parts.append(jnp.where(jnp.abs(p - me) == 1, edge, places[at]))
        out_ref[p] = jnp.concatenate(parts, axis=0).astype(out_ref.dtype)


def joined(rows, nvec):
    return jnp.concatenate([rows[:nvec], rows[nvec:]], axis=1)


def load_slots(slots_any, dests_any, slot_ref, dest_ref, sems):
    copies = [
        pltpu.make_async_copy(slots_any, slot_ref, sems.at[0]),
        pltpu.make_async_copy(dests_any, dest_ref, sems.at[1]),
    ]
    for copy in copies:
        copy.start()
    return copies


def near_product(src_ref, near_ref, x_ref, near_out):
    clusters, nvec, leaf = src_ref.shape
    peers, rows, _ = x_ref.shape
    me = lax.axis_index("clus")
    before = x_ref[jnp.maximum(me - 1, 0)][rows - nvec :].astype(jnp.float32)
    after = x_ref[jnp.minimum(me + 1, peers - 1)][rows - nvec :].astype(jnp.float32)
    before = jnp.where(me > 0, before, 0.0)
    after = jnp.where(me < peers - 1, after, 0.0)
    before, after = [
        jnp.concatenate([x, jnp.zeros_like(x)], axis=1).astype(jnp.bfloat16)
        for x in (before, after)
    ]
    sources = [before] + [src_ref[s] for s in range(clusters)] + [after]

    def product(s):
        near_out[s * nvec : (s + 1) * nvec] = jnp.dot(
            jnp.concatenate(sources[s : s + 3], axis=1),
            near_ref[s].reshape(3 * leaf, leaf),
            preferred_element_type=jnp.float32,
        )

    return product


def placement(x_ref, pattern_ref, place, place_out):
    nvec, width = pattern_ref.shape
    peers, rows, _ = x_ref.shape
    cap = place.shape[0] // (peers * nvec)
    cluster = pattern_ref[...]
    me = lax.axis_index("clus")

    def step(p, carry):
        tile = x_ref[p, rows - nvec :, :].astype(jnp.float32)
        tile = jnp.where(jnp.abs(p - me) == 1, -1.0, tile)
        for k in range(cap):
            at = jnp.broadcast_to(tile[k : k + 1], (nvec, width))
            place[pl.ds((p * cap + k) * nvec, nvec)] = jnp.where(at == cluster, 1.0, 0.0)
        return carry

    lax.fori_loop(0, peers, step, 0, unroll=min(peers, 16))
    place_out[...] = place[...].T[: place_out.shape[0]].astype(jnp.bfloat16)


def widen_sources(x_ref, xf):
    peers = x_ref.shape[0]
    slots, nvec, _ = xf.shape
    cap = slots // peers

    def widen(p, carry):
        rows = x_ref[p].astype(jnp.float32)
        for k in range(cap):
            xf[p * cap + k] = joined(rows[2 * k * nvec : 2 * (k + 1) * nvec], nvec)
        return carry

    lax.fori_loop(0, peers, widen, 0, unroll=min(peers, 16))


def project(picked, u, owner, nvec, group):
    full = lax.dot_general(picked, u, (((1,), (1,)), ((), ())), preferred_element_type=jnp.float32)
    kept = full[:nvec]
    for i in range(1, group):
        kept = jnp.where(owner == i, full[i * nvec : (i + 1) * nvec], kept)
    return kept


def put_returns(total, x_ref, src_ref, out_ref):
    peers, rows, width = x_ref.shape
    clusters, nvec, _ = src_ref.shape
    each = total.shape[0] // peers
    cap = each // nvec
    me = lax.axis_index("clus")
    first = halves(src_ref[0].astype(jnp.float32))[1]
    last = halves(src_ref[clusters - 1].astype(jnp.float32))[1]
    sub = lax.broadcasted_iota(jnp.int32, (nvec, width), 0)
    for p in range(peers):
        before = x_ref[max(p - 1, 0), rows - nvec :, :].astype(jnp.float32)
        after = x_ref[min(p + 1, peers - 1), rows - nvec :, :].astype(jnp.float32)
        handed = jnp.where(sub // cap == 2, before, after)
        edge = jnp.where(p > me, last, first)
        parts = halves(total[p * each : (p + 1) * each])
        parts.append(jnp.where(jnp.abs(p - me) == 1, edge, handed))
        out_ref[p] = jnp.concatenate(parts, axis=0).astype(out_ref.dtype)


def far_kernel(
    slots_any,
    dests_any,
    x_ref,
    u_ref,
    v_ref,
    src_ref,
    near_ref,
    pattern_ref,
    out_ref,
    near_out,
    place_out,
    slot_ref,
    dest_ref,
    sems,
    place,
    xf,
    picked,
    acc,
):
    peers = x_ref.shape[0]
    slots, nvec, leaf = xf.shape
    blocks, rank, _ = u_ref.shape
    group = leaf // rank
    groups = blocks // group
    copies = load_slots(slots_any, dests_any, slot_ref, dest_ref, sems)
    widen_sources(x_ref, xf)
    placement(x_ref, pattern_ref, place, place_out)
    for copy in copies:
        copy.wait()
    near = near_product(src_ref, near_ref, x_ref, near_out)
    clusters = src_ref.shape[0]
    for g in range(groups):
        rows = [xf[slot_ref[g * group + i]] for i in range(group)]
        picked[g] = jnp.concatenate(rows, axis=0).astype(jnp.bfloat16)
    owner = lax.broadcasted_iota(jnp.int32, (nvec, leaf), 1) // rank

    def coefficients(g):
        u = u_ref[g * group : (g + 1) * group].reshape(leaf, leaf)
        return project(picked[g], u, owner, nvec, group)

    def contributions(g, kept, ats):
        dest = jnp.full((nvec, leaf), ats[0], jnp.int32)
        for i in range(1, group):
            dest = jnp.where(owner == i, ats[i], dest)
        same = [jnp.where(dest == at, kept, 0.0) for at in ats]
        return jnp.dot(
            jnp.concatenate(same, axis=0).astype(jnp.bfloat16),
            v_ref[g * group : (g + 1) * group].reshape(leaf, leaf),
            preferred_element_type=jnp.float32,
        )

    def accumulate(terms, ats):
        sums = [acc[at] + terms[i * nvec : (i + 1) * nvec] for i, at in enumerate(ats)]
        for at, value in zip(ats, sums):
            acc[at] = value

    acc[...] = jnp.zeros_like(acc)
    chunks = [range(first, min(first + CHUNK, groups)) for first in range(0, groups, CHUNK)]
    ahead = [coefficients(g) for g in chunks[0]]
    late = []
    for c, chunk in enumerate(chunks):
        kept = ahead
        if c + 1 < len(chunks):
            ahead = [coefficients(g) for g in chunks[c + 1]]
        ats = [[dest_ref[g * group + i] for i in range(group)] for g in chunk]
        terms = [contributions(g, k, at) for g, k, at in zip(chunk, kept, ats)]
        for s in range(c * clusters // len(chunks), (c + 1) * clusters // len(chunks)):
            near(s)
        for term, at in late:
            accumulate(term, at)
        late = list(zip(terms, ats))
    for term, at in late:
        accumulate(term, at)
    put_returns(acc[...].reshape(slots * nvec, leaf), x_ref, src_ref, out_ref)


def sum_kernel(back_ref, near_out_ref, place_ref, near_ref, out_ref):
    peers, rows, width = back_ref.shape
    clusters, nvec, leaf = out_ref.shape
    each = (rows - nvec) // 2
    cap = each // nvec
    me = lax.axis_index("clus")
    terms = jnp.concatenate(
        [back_ref[:, i * each : (i + 1) * each, :].reshape(peers * each, width) for i in range(2)],
        axis=1,
    )
    total = near_out_ref[...] + jnp.dot(
        place_ref[...], terms, preferred_element_type=jnp.float32
    )

    relay = jnp.where(me + 3 < peers, me + 3, me - 3)
    tile = back_ref[relay][rows - nvec :].astype(jnp.float32)
    before = back_ref[jnp.maximum(me - 1, 0)].astype(jnp.float32)
    after = back_ref[jnp.minimum(me + 1, peers - 1)].astype(jnp.float32)
    row = lax.broadcasted_iota(jnp.int32, (clusters * nvec, width), 0)
    lane = lax.broadcasted_iota(jnp.int32, (clusters * nvec, width), 1)
    named = jnp.full((1, width), -1.0, jnp.float32)
    for i in range(2 * cap):
        k, alive = (i + 2 * cap, me > 0) if i < cap else (i, me < peers - 1)
        entry = jnp.where(alive, tile[k : k + 1], -1.0)
        named = jnp.where(lane[:1] // nvec == i, entry, named)
    match = (named == (row // nvec).astype(jnp.float32)) & (lane % nvec == row % nvec)
    match = jnp.where(match, 1.0, 0.0)[:, : 2 * each].astype(jnp.bfloat16)
    sides = jnp.concatenate(
        [
            jnp.concatenate([side[:each], side[each : 2 * each]], axis=1)
            for side in (before, after)
        ],
        axis=0,
    ).astype(jnp.bfloat16)
    total += jnp.dot(match, sides, preferred_element_type=jnp.float32)

    edges = []
    for side, alive, at in ((before, me > 0, (0, 0)), (after, me < peers - 1, (clusters - 1, 2))):
        edge = jnp.where(alive, side[2 * each :], 0.0).astype(jnp.bfloat16)
        edges.append(
            jnp.dot(edge, near_ref[at[0], at[1], width:, :], preferred_element_type=jnp.float32)
        )
    for s in range(clusters):
        part = total[s * nvec : (s + 1) * nvec]
        if s == 0:
            part += edges[0]
        if s == clusters - 1:
            part += edges[1]
        out_ref[s] = part


def cost(flops, moved):
    return pl.CostEstimate(flops=flops, bytes_accessed=moved, transcendentals=0)


def body(sources, near_blocks, far_u, far_v, send_list, far_slot, ret_list, ret_slot):
    clusters, nvec, leaf = sources.shape
    _, peers, cap = send_list.shape
    blocks, rank, _ = far_u.shape
    slots = peers * cap
    rows = 2 * cap * nvec + nvec
    params = pltpu.CompilerParams(vmem_limit_bytes=8 * 2**20)
    pattern = pl.pallas_call(
        pattern_kernel,
        out_shape=jax.ShapeDtypeStruct((nvec, leaf // 2), jnp.float32),
        out_specs=VMEM,
        compiler_params=params,
        cost_estimate=cost(10**10, nvec * leaf * 2),
        name="pattern",
    )()
    message = pl.pallas_call(
        pack_kernel,
        out_shape=jax.ShapeDtypeStruct((peers, rows, leaf // 2), jnp.bfloat16),
        in_specs=[VMEM] * 4,
        out_specs=VMEM,
        compiler_params=params,
        cost_estimate=cost(10**10, peers * rows * leaf),
        name="pack",
    )(send_list[0].T, ret_list[0].T, sources, pattern)
    incoming = lax.all_to_all(message, "clus", split_axis=0, concat_axis=0, tiled=True)
    returns, near_part, place = pl.pallas_call(
        far_kernel,
        out_shape=(
            jax.ShapeDtypeStruct((peers, rows, leaf // 2), jnp.bfloat16),
            jax.ShapeDtypeStruct((clusters * nvec, leaf), jnp.float32),
            jax.ShapeDtypeStruct((clusters * nvec, slots * nvec), jnp.bfloat16),
        ),
        in_specs=[ANY, ANY] + [VMEM] * 6,
        out_specs=(VMEM, VMEM, VMEM),
        scratch_shapes=[
            pltpu.SMEM((blocks,), jnp.int32),
            pltpu.SMEM((blocks,), jnp.int32),
            pltpu.SemaphoreType.DMA((2,)),
            pltpu.VMEM((slots * nvec, leaf // 2), jnp.float32),
            pltpu.VMEM((slots, nvec, leaf), jnp.float32),
            pltpu.VMEM((blocks * rank // leaf, leaf // rank * nvec, leaf), jnp.bfloat16),
            pltpu.VMEM((slots, nvec, leaf), jnp.float32),
        ],
        compiler_params=pltpu.CompilerParams(vmem_limit_bytes=16 * 2**20),
        cost_estimate=cost(4 * blocks * 8 * nvec * leaf * rank, 4 * blocks * rank * leaf),
        name="far",
    )(far_slot, ret_slot, incoming, far_u, far_v, sources, near_blocks, pattern)
    back = lax.all_to_all(returns, "clus", split_axis=0, concat_axis=0, tiled=True)
    return pl.pallas_call(
        sum_kernel,
        out_shape=jax.ShapeDtypeStruct((clusters, nvec, leaf), jnp.float32),
        in_specs=[VMEM] * 4,
        out_specs=VMEM,
        compiler_params=params,
        cost_estimate=cost(2 * clusters * nvec * slots * nvec * leaf, slots * nvec * leaf * 2),
        name="sum",
    )(back, near_part, place, near_blocks)


def solution(mesh):
    placed = (
        P(("groups", "clus"), None, None),
        P(("groups", "clus"), None, None, None),
        P(("groups", "clus"), None, None),
        P(("groups", "clus"), None, None),
        P(("groups", "clus"), None, None),
        P(("groups", "clus")),
        P(("groups", "clus"), None, None),
        P(("groups", "clus")),
    )
    return jax.shard_map(
        body,
        mesh=mesh,
        in_specs=placed,
        out_specs=P(("groups", "clus"), None, None),
        check_vma=False,
    )
```

```python
import jax
import jax.numpy as jnp
from jax import lax
from jax.experimental import pallas as pl
from jax.experimental.pallas import tpu as pltpu
from jax.sharding import PartitionSpec as P

VMEM = pl.BlockSpec(memory_space=pltpu.VMEM)
CHUNK = 4
ANY = pl.BlockSpec(memory_space=pl.ANY)


def halves(x):
    w = x.shape[1] // 2
    return [x[:, :w], x[:, w:]]


def pattern_kernel(out_ref):
    nvec, width = out_ref.shape
    lane = lax.broadcasted_iota(jnp.int32, (nvec, width), 1)
    sub = lax.broadcasted_iota(jnp.int32, (nvec, width), 0)
    out_ref[...] = jnp.where(lane % nvec == sub, lane // nvec, -2).astype(jnp.float32)


def pack_kernel(send_ref, ret_ref, src_ref, pattern_ref, out_ref):
    clusters, nvec, leaf = src_ref.shape
    cap, peers = send_ref.shape
    me = lax.axis_index("clus")
    rows = peers * nvec
    peer = lax.broadcasted_iota(jnp.int32, (rows, peers), 0) // nvec
    kind = lax.broadcasted_iota(jnp.int32, (rows, peers), 0) % nvec // cap
    column = lax.broadcasted_iota(jnp.int32, (rows, peers), 1)

    def entries_at(list_ref, which):
        entries = list_ref[...].astype(jnp.float32).astype(jnp.bfloat16)
        return lax.dot_general(
            jnp.where(which == column, 1.0, 0.0).astype(jnp.bfloat16),
            entries,
            (((1,), (1,)), ((), ())),
            preferred_element_type=jnp.float32,
        )

    send = jnp.maximum(entries_at(send_ref, peer), 0.0)
    ret = entries_at(ret_ref, jnp.where(kind == 1, me - 1, jnp.where(kind == 2, me + 1, peer)))
    row = lax.broadcasted_iota(jnp.int32, (rows, clusters * nvec), 0)
    lane = lax.broadcasted_iota(jnp.int32, (rows, clusters * nvec), 1)
    cluster = jnp.where(row % nvec == lane % nvec, lane // nvec, -2).astype(jnp.float32)
    source = src_ref[...].reshape(clusters * nvec, leaf)
    picked = []
    for k in range(cap):
        pick = jnp.where(send[:, k : k + 1] == cluster, 1.0, 0.0).astype(jnp.bfloat16)
        picked.append(jnp.dot(pick, source, preferred_element_type=jnp.float32))
    vector = lax.broadcasted_iota(jnp.int32, (rows, leaf // 2), 0) % nvec
    places = jnp.broadcast_to(ret[:, :1], (rows, leaf // 2))
    for k in range(1, cap):
        places = jnp.where(vector % cap == k, ret[:, k : k + 1], places)
    first = src_ref[0].astype(jnp.float32)
    last = src_ref[clusters - 1].astype(jnp.float32)
    for p in range(peers):
        at = slice(p * nvec, (p + 1) * nvec)
        parts = []
        for k in range(cap):
            parts += halves(picked[k][at])
        edge = halves(jnp.where(p > me, last, first))[0]
        parts.append(jnp.where(jnp.abs(p - me) == 1, edge, places[at]))
        out_ref[p] = jnp.concatenate(parts, axis=0).astype(out_ref.dtype)


def joined(rows, nvec):
    return jnp.concatenate([rows[:nvec], rows[nvec:]], axis=1)


def load_slots(slots_any, dests_any, slot_ref, dest_ref, sems):
    copies = [
        pltpu.make_async_copy(slots_any, slot_ref, sems.at[0]),
        pltpu.make_async_copy(dests_any, dest_ref, sems.at[1]),
    ]
    for copy in copies:
        copy.start()
    return copies


def near_product(src_ref, near_ref, x_ref, near_out):
    clusters, nvec, leaf = src_ref.shape
    peers, rows, _ = x_ref.shape
    me = lax.axis_index("clus")
    before = x_ref[jnp.maximum(me - 1, 0)][rows - nvec :].astype(jnp.float32)
    after = x_ref[jnp.minimum(me + 1, peers - 1)][rows - nvec :].astype(jnp.float32)
    before = jnp.where(me > 0, before, 0.0)
    after = jnp.where(me < peers - 1, after, 0.0)
    before, after = [
        jnp.concatenate([x, jnp.zeros_like(x)], axis=1).astype(jnp.bfloat16)
        for x in (before, after)
    ]
    sources = [before] + [src_ref[s] for s in range(clusters)] + [after]

    def product(s):
        near_out[s * nvec : (s + 1) * nvec] = jnp.dot(
            jnp.concatenate(sources[s : s + 3], axis=1),
            near_ref[s].reshape(3 * leaf, leaf),
            preferred_element_type=jnp.float32,
        )

    return product


def placement(x_ref, pattern_ref, place, place_out):
    nvec, width = pattern_ref.shape
    peers, rows, _ = x_ref.shape
    cap = place.shape[0] // (peers * nvec)
    cluster = pattern_ref[...]
    me = lax.axis_index("clus")

    def step(p, carry):
        tile = x_ref[p, rows - nvec :, :].astype(jnp.float32)
        tile = jnp.where(jnp.abs(p - me) == 1, -1.0, tile)
        for k in range(cap):
            at = jnp.broadcast_to(tile[k : k + 1], (nvec, width))
            place[pl.ds((p * cap + k) * nvec, nvec)] = jnp.where(at == cluster, 1.0, 0.0)
        return carry

    lax.fori_loop(0, peers, step, 0, unroll=min(peers, 16))
    place_out[...] = place[...].T[: place_out.shape[0]].astype(jnp.bfloat16)


def widen_sources(x_ref, xf):
    peers = x_ref.shape[0]
    slots, nvec, _ = xf.shape
    cap = slots // peers

    def widen(p, carry):
        rows = x_ref[p].astype(jnp.float32)
        for k in range(cap):
            xf[p * cap + k] = joined(rows[2 * k * nvec : 2 * (k + 1) * nvec], nvec)
        return carry

    lax.fori_loop(0, peers, widen, 0, unroll=min(peers, 16))


def project(picked, u, owner, nvec, group):
    full = lax.dot_general(picked, u, (((1,), (1,)), ((), ())), preferred_element_type=jnp.float32)
    kept = full[:nvec]
    for i in range(1, group):
        kept = jnp.where(owner == i, full[i * nvec : (i + 1) * nvec], kept)
    return kept


def put_returns(total, x_ref, src_ref, out_ref):
    peers, rows, width = x_ref.shape
    clusters, nvec, _ = src_ref.shape
    each = total.shape[0] // peers
    cap = each // nvec
    me = lax.axis_index("clus")
    first = halves(src_ref[0].astype(jnp.float32))[1]
    last = halves(src_ref[clusters - 1].astype(jnp.float32))[1]
    sub = lax.broadcasted_iota(jnp.int32, (nvec, width), 0)
    for p in range(peers):
        before = x_ref[max(p - 1, 0), rows - nvec :, :].astype(jnp.float32)
        after = x_ref[min(p + 1, peers - 1), rows - nvec :, :].astype(jnp.float32)
        handed = jnp.where(sub // cap == 2, before, after)
        edge = jnp.where(p > me, last, first)
        parts = halves(total[p * each : (p + 1) * each])
        parts.append(jnp.where(jnp.abs(p - me) == 1, edge, handed))
        out_ref[p] = jnp.concatenate(parts, axis=0).astype(out_ref.dtype)


def far_kernel(
    slots_any,
    dests_any,
    x_ref,
    u_ref,
    v_ref,
    src_ref,
    near_ref,
    pattern_ref,
    out_ref,
    near_out,
    place_out,
    slot_ref,
    dest_ref,
    sems,
    place,
    xf,
    picked,
    acc,
):
    peers = x_ref.shape[0]
    slots, nvec, leaf = xf.shape
    blocks, rank, _ = u_ref.shape
    group = leaf // rank
    groups = blocks // group
    copies = load_slots(slots_any, dests_any, slot_ref, dest_ref, sems)
    widen_sources(x_ref, xf)
    placement(x_ref, pattern_ref, place, place_out)
    near = near_product(src_ref, near_ref, x_ref, near_out)
    clusters = src_ref.shape[0]
    early = clusters * 3 // 8
    for s in range(early):
        near(s)
    for copy in copies:
        copy.wait()
    for g in range(groups):
        rows = [xf[slot_ref[g * group + i]] for i in range(group)]
        picked[g] = jnp.concatenate(rows, axis=0).astype(jnp.bfloat16)
    owner = lax.broadcasted_iota(jnp.int32, (nvec, leaf), 1) // rank

    def coefficients(g):
        u = u_ref[g * group : (g + 1) * group].reshape(leaf, leaf)
        return project(picked[g], u, owner, nvec, group)

    def contributions(g, kept, ats):
        dest = jnp.full((nvec, leaf), ats[0], jnp.int32)
        for i in range(1, group):
            dest = jnp.where(owner == i, ats[i], dest)
        same = [jnp.where(dest == at, kept, 0.0) for at in ats]
        return jnp.dot(
            jnp.concatenate(same, axis=0).astype(jnp.bfloat16),
            v_ref[g * group : (g + 1) * group].reshape(leaf, leaf),
            preferred_element_type=jnp.float32,
        )

    def accumulate(terms, ats):
        sums = [acc[at] + terms[i * nvec : (i + 1) * nvec] for i, at in enumerate(ats)]
        for at, value in zip(ats, sums):
            acc[at] = value

    acc[...] = jnp.zeros_like(acc)
    chunks = [range(first, min(first + CHUNK, groups)) for first in range(0, groups, CHUNK)]
    ahead = [coefficients(g) for g in chunks[0]]
    for c, chunk in enumerate(chunks):
        kept = ahead
        if c + 1 < len(chunks):
            ahead = [coefficients(g) for g in chunks[c + 1]]
        ats = [[dest_ref[g * group + i] for i in range(group)] for g in chunk]
        terms = [contributions(g, k, at) for g, k, at in zip(chunk, kept, ats)]
        share = [early + (clusters - early) * i // len(chunks) for i in (c, c + 1)]
        for s in range(*share):
            near(s)
        for term, at in zip(terms, ats):
            accumulate(term, at)
    put_returns(acc[...].reshape(slots * nvec, leaf), x_ref, src_ref, out_ref)


def sum_kernel(back_ref, near_out_ref, place_ref, near_ref, out_ref):
    peers, rows, width = back_ref.shape
    clusters, nvec, leaf = out_ref.shape
    each = (rows - nvec) // 2
    cap = each // nvec
    me = lax.axis_index("clus")
    terms = jnp.concatenate(
        [back_ref[:, i * each : (i + 1) * each, :].reshape(peers * each, width) for i in range(2)],
        axis=1,
    )
    total = near_out_ref[...] + jnp.dot(
        place_ref[...], terms, preferred_element_type=jnp.float32
    )

    relay = jnp.where(me + 3 < peers, me + 3, me - 3)
    tile = back_ref[relay][rows - nvec :].astype(jnp.float32)
    before = back_ref[jnp.maximum(me - 1, 0)].astype(jnp.float32)
    after = back_ref[jnp.minimum(me + 1, peers - 1)].astype(jnp.float32)
    row = lax.broadcasted_iota(jnp.int32, (clusters * nvec, width), 0)
    lane = lax.broadcasted_iota(jnp.int32, (clusters * nvec, width), 1)
    named = jnp.full((1, width), -1.0, jnp.float32)
    for i in range(2 * cap):
        k, alive = (i + 2 * cap, me > 0) if i < cap else (i, me < peers - 1)
        entry = jnp.where(alive, tile[k : k + 1], -1.0)
        named = jnp.where(lane[:1] // nvec == i, entry, named)
    match = (named == (row // nvec).astype(jnp.float32)) & (lane % nvec == row % nvec)
    match = jnp.where(match, 1.0, 0.0)[:, : 2 * each].astype(jnp.bfloat16)
    sides = jnp.concatenate(
        [
            jnp.concatenate([side[:each], side[each : 2 * each]], axis=1)
            for side in (before, after)
        ],
        axis=0,
    ).astype(jnp.bfloat16)
    total += jnp.dot(match, sides, preferred_element_type=jnp.float32)

    edges = []
    for side, alive, at in ((before, me > 0, (0, 0)), (after, me < peers - 1, (clusters - 1, 2))):
        edge = jnp.where(alive, side[2 * each :], 0.0).astype(jnp.bfloat16)
        edges.append(
            jnp.dot(edge, near_ref[at[0], at[1], width:, :], preferred_element_type=jnp.float32)
        )
    for s in range(clusters):
        part = total[s * nvec : (s + 1) * nvec]
        if s == 0:
            part += edges[0]
        if s == clusters - 1:
            part += edges[1]
        out_ref[s] = part


def cost(flops, moved):
    return pl.CostEstimate(flops=flops, bytes_accessed=moved, transcendentals=0)


def body(sources, near_blocks, far_u, far_v, send_list, far_slot, ret_list, ret_slot):
    clusters, nvec, leaf = sources.shape
    _, peers, cap = send_list.shape
    blocks, rank, _ = far_u.shape
    slots = peers * cap
    rows = 2 * cap * nvec + nvec
    params = pltpu.CompilerParams(vmem_limit_bytes=8 * 2**20)
    pattern = pl.pallas_call(
        pattern_kernel,
        out_shape=jax.ShapeDtypeStruct((nvec, leaf // 2), jnp.float32),
        out_specs=VMEM,
        compiler_params=params,
        cost_estimate=cost(10**10, nvec * leaf * 2),
        name="pattern",
    )()
    message = pl.pallas_call(
        pack_kernel,
        out_shape=jax.ShapeDtypeStruct((peers, rows, leaf // 2), jnp.bfloat16),
        in_specs=[VMEM] * 4,
        out_specs=VMEM,
        compiler_params=params,
        cost_estimate=cost(10**10, peers * rows * leaf),
        name="pack",
    )(send_list[0].T, ret_list[0].T, sources, pattern)
    incoming = lax.all_to_all(message, "clus", split_axis=0, concat_axis=0, tiled=True)
    returns, near_part, place = pl.pallas_call(
        far_kernel,
        out_shape=(
            jax.ShapeDtypeStruct((peers, rows, leaf // 2), jnp.bfloat16),
            jax.ShapeDtypeStruct((clusters * nvec, leaf), jnp.float32),
            jax.ShapeDtypeStruct((clusters * nvec, slots * nvec), jnp.bfloat16),
        ),
        in_specs=[ANY, ANY] + [VMEM] * 6,
        out_specs=(VMEM, VMEM, VMEM),
        scratch_shapes=[
            pltpu.SMEM((blocks,), jnp.int32),
            pltpu.SMEM((blocks,), jnp.int32),
            pltpu.SemaphoreType.DMA((2,)),
            pltpu.VMEM((slots * nvec, leaf // 2), jnp.float32),
            pltpu.VMEM((slots, nvec, leaf), jnp.float32),
            pltpu.VMEM((blocks * rank // leaf, leaf // rank * nvec, leaf), jnp.bfloat16),
            pltpu.VMEM((slots, nvec, leaf), jnp.float32),
        ],
        compiler_params=pltpu.CompilerParams(vmem_limit_bytes=16 * 2**20),
        cost_estimate=cost(4 * blocks * 8 * nvec * leaf * rank, 4 * blocks * rank * leaf),
        name="far",
    )(far_slot, ret_slot, incoming, far_u, far_v, sources, near_blocks, pattern)
    back = lax.all_to_all(returns, "clus", split_axis=0, concat_axis=0, tiled=True)
    return pl.pallas_call(
        sum_kernel,
        out_shape=jax.ShapeDtypeStruct((clusters, nvec, leaf), jnp.float32),
        in_specs=[VMEM] * 4,
        out_specs=VMEM,
        compiler_params=params,
        cost_estimate=cost(2 * clusters * nvec * slots * nvec * leaf, slots * nvec * leaf * 2),
        name="sum",
    )(back, near_part, place, near_blocks)


def solution(mesh):
    placed = (
        P(("groups", "clus"), None, None),
        P(("groups", "clus"), None, None, None),
        P(("groups", "clus"), None, None),
        P(("groups", "clus"), None, None),
        P(("groups", "clus"), None, None),
        P(("groups", "clus")),
        P(("groups", "clus"), None, None),
        P(("groups", "clus")),
    )
    return jax.shard_map(
        body,
        mesh=mesh,
        in_specs=placed,
        out_specs=P(("groups", "clus"), None, None),
        check_vma=False,
    )
```
